32 devices in a mesh: dp: 4 (over y, x), fsdp: 8 (over z, core).
Axes of the slice: x: 2, y: 2, z: 4, core: 2. Of those that a mesh axis runs over, the one named last changes fastest.
Arguments:
- tokens: bfloat16 [32768, 512], P(('dp', 'fsdp')), may hold values from -6 to 6
- memory: bfloat16 [32768, 512], P(('dp', 'fsdp')), may hold values from -6 to 6
- out_cotangent: bfloat16 [32768, 512], P(('dp', 'fsdp')), may hold values from -6 to 6
- seq_lengths: int32 [32, 32], P(('dp', 'fsdp')), may hold values from 0 to 1024, as said below
- memory_lengths: int32 [32, 32], P(('dp', 'fsdp')), may hold values from 0 to 1024, as said below
- residual_gate: float32 [1], replicated, may hold values from 0.5 to 1
- self_in: float32 [512, 1536], P(('dp', 'fsdp')), may hold values from -0.25 to 0.25
- self_out: float32 [512, 512], P(None, ('dp', 'fsdp')), may hold values from -1 to 1
- self_bias: float32 [3, 512], P(None, ('dp', 'fsdp')), may hold values from -1.5 to 1.5
- cross_query: float32 [512, 512], P(('dp', 'fsdp')), may hold values from -0.25 to 0.25
- cross_key_value: float32 [512, 1024], P(('dp', 'fsdp')), may hold values from -0.25 to 0.25
- cross_out: float32 [512, 512], P(None, ('dp', 'fsdp')), may hold values from -1 to 1
- cross_bias: float32 [3, 512], P(None, ('dp', 'fsdp')), may hold values from -1.5 to 1.5
- feed_in: float32 [512, 2048], P(('dp', 'fsdp')), may hold values from -0.25 to 0.25
- feed_out: float32 [2048, 512], P(None, ('dp', 'fsdp')), may hold values from -0.25 to 0.25
- feed_bias_in: float32 [2048], P(('dp', 'fsdp')), may hold values from -2.5 to 2.5
- feed_bias_out: float32 [512], P(('dp', 'fsdp')), may hold values from -6 to 6
Outputs:
- output: bfloat16 [32768, 512], P(('dp', 'fsdp'))
- tokens_grad: float32 [32768, 512], P(('dp', 'fsdp'))
- memory_grad: float32 [32768, 512], P(('dp', 'fsdp'))
- self_in_grad: float32 [512, 1536], P(('dp', 'fsdp'))
- self_out_grad: float32 [512, 512], P(None, ('dp', 'fsdp'))
- self_bias_grad: float32 [3, 512], P(None, ('dp', 'fsdp'))
- cross_query_grad: float32 [512, 512], P(('dp', 'fsdp'))
- cross_key_value_grad: float32 [512, 1024], P(('dp', 'fsdp'))
- cross_out_grad: float32 [512, 512], P(None, ('dp', 'fsdp'))
- cross_bias_grad: float32 [3, 512], P(None, ('dp', 'fsdp'))
- feed_in_grad: float32 [512, 2048], P(('dp', 'fsdp'))
- feed_out_grad: float32 [2048, 512], P(None, ('dp', 'fsdp'))
- feed_bias_in_grad: float32 [2048], P(('dp', 'fsdp'))
- feed_bias_out_grad: float32 [512], P(('dp', 'fsdp'))
The draws below stay inside these ranges and needn't reach their ends.
Inputs may be any that keep to these rules, and one draw needn't show every extreme that they name: `seq_lengths`: in each row the first k entries (k from 1 to 32, varying by row) are sentence lengths of 1 or more and the rest are 0; a row sums to at most 1024, and the first row holds one sentence of 1024 tokens. `memory_lengths`: nonzero exactly where seq_lengths is; a row sums to at most 1024, and the first row holds one memory of 1024 tokens.
All inputs are finite; a program needn't handle non-finite values.
Results may differ from the reference program's by a relative error of at most 0.023.
The reference program's roundings to bfloat16 on the way count: a program that leaves them out, or rounds other values in their place, can miss the bound.
Values may be sent and summed in bfloat16 or wider, within the bound.
No kernel may reach another device: no remote copies, remote signals or barrier semaphores. Data moves between devices by JAX's collectives and lax.ppermute only.
A program may use at most 192 MiB of HBM per device.

```python
from functools import partial
import jax
import jax.numpy as jnp
from jax import lax

D = 512
HEAD = 64
FF = 2048
TOK_DEV = 1024
MEM_DEV = 1024
SLOTS = 32
PACKS = 32
TOKENS = 32768
MEMORY_TOKENS = 32768


def slot_counts(key):
    used_slots = jax.random.randint(jax.random.fold_in(key, 101), (PACKS,), 1, SLOTS + 1)
    return used_slots.at[0].set(1)


def spread_lengths(key, used_slots, capacity):
    slack_rows = jax.random.randint(jax.random.fold_in(key, 1), (PACKS,), 0, capacity // 8 + 1)
    slack_rows = slack_rows.at[0].set(0)
    filled = capacity - slack_rows
    slot_index = jnp.arange(SLOTS, dtype=jnp.int32)[None, :]
    active = (slot_index < used_slots[:, None]).astype(jnp.int32)
    shares = jax.random.randint(jax.random.fold_in(key, 2), (PACKS, SLOTS), 1, 5) * active
    running = jnp.cumsum(shares, axis=1, dtype=jnp.int32)
    whole_sum = running[:, -1:]
    boundary = jnp.minimum(slot_index + 1, used_slots[:, None]) + (filled[:, None] - used_slots[:, None]) * running // whole_sum
    earlier = jnp.concatenate([jnp.zeros((PACKS, 1), jnp.int32), boundary[:, :-1]], axis=1)
    return (boundary - earlier).astype(jnp.int32)


def draw_seq_lengths(key, part):
    used_slots = slot_counts(key)
    key = jax.random.fold_in(key, 3)
    return spread_lengths(key, used_slots, TOK_DEV)


def draw_memory_lengths(key, part):
    used_slots = slot_counts(key)
    key = jax.random.fold_in(key, 4)
    return spread_lengths(key, used_slots, MEM_DEV)


def strengthened(entries, stream_key, source, target, parts, factor):
    owner, partner = [(jnp.arange(entries.shape[dim]) // (entries.shape[dim] // parts)).reshape([-1 if axis == dim else 1 for axis in range(entries.ndim)]) for dim in (source, target)]
    chosen = jax.random.permutation(stream_key, parts)[partner]
    strong = (owner == chosen) | (owner == (partner + parts // 2) % parts)
    return jnp.where(strong, factor * entries, entries)


def block_scale(own_key, dims, cuts, least, largest):
    def one(dim, blocks):
        steps = jax.random.uniform(jax.random.fold_in(jax.random.fold_in(own_key, 6), dim), (blocks,), jnp.float32, least / len(cuts), largest / len(cuts))
        return jnp.repeat(jnp.exp(steps), dims[dim] // blocks).reshape((-1,) + (1,) * (len(dims) - dim - 1))

    gain = one(*cuts[0])
    for cut in cuts[1:]:
        gain = gain * one(*cut)
    return gain


def normal_values(stream_key, dims, scale, reach, cuts=(), kind=jnp.bfloat16):
    level = block_scale(stream_key, dims, cuts, -0.22, 0.18) if cuts else 1.0
    values = jax.random.normal(stream_key, dims, jnp.float32) * scale * level
    return jnp.minimum(jnp.maximum(values, -reach), reach).astype(kind)


def heavy_noise(key, dims, scale, bound, cuts, heavy, kind=jnp.bfloat16):
    drawn = scale * jax.random.normal(key, dims, jnp.float32)
    if cuts:
        drawn = drawn * block_scale(key, dims, cuts, -0.22, 0.18)
    return jnp.clip(strengthened(drawn, jax.random.fold_in(key, 3), *heavy), -bound, bound).astype(kind)


def setup_inputs(seed: int = 0) -> dict:
    splits = jax.random.split(jax.random.key(seed), 18)
    return {
        "tokens": heavy_noise(splits[0], (TOKENS, D), 1.0, 6.0, ((0, 32),), (0, 1, 32, 2.75)),
        "memory": heavy_noise(splits[1], (MEMORY_TOKENS, D), 1.0, 6.0, ((0, 32),), (0, 1, 32, 2.75)),
        "out_cotangent": heavy_noise(splits[2], (TOKENS, D), 1.0, 6.0, ((0, 32),), (0, 1, 32, 2.75)),
        "seq_lengths": draw_seq_lengths(jax.random.fold_in(splits[17], 71), 0),
        "memory_lengths": draw_memory_lengths(jax.random.fold_in(splits[17], 71), 0),
        "residual_gate": jnp.clip(jax.random.uniform(splits[5], (1,), jnp.float32, 0.5, 1.0), 0.5, 1.0),
        "self_in": normal_values(splits[6], (D, 3 * D), D ** -0.5, 0.25, ((0, 32),), jnp.float32),
        "self_out": normal_values(splits[7], (D, D), (D // 16) ** -0.5, 1.0, ((1, 32),), jnp.float32),
        "self_bias": normal_values(splits[8], (3, D), 0.3, 1.5, ((1, 32),), jnp.float32),
        "cross_query": normal_values(splits[9], (D, D), D ** -0.5, 0.25, ((0, 32),), jnp.float32),
        "cross_key_value": normal_values(splits[10], (D, 2 * D), D ** -0.5, 0.25, ((0, 32),), jnp.float32),
        "cross_out": normal_values(splits[11], (D, D), (D // 16) ** -0.5, 1.0, ((1, 32),), jnp.float32),
        "cross_bias": normal_values(splits[12], (3, D), 0.3, 1.5, ((1, 32),), jnp.float32),
        "feed_in": normal_values(splits[13], (D, FF), D ** -0.5, 0.25, ((0, 32),), jnp.float32),
        "feed_out": normal_values(splits[14], (FF, D), (FF // 4) ** -0.5, 0.25, ((1, 32),), jnp.float32),
        "feed_bias_in": normal_values(splits[15], (FF,), 0.5, 2.5, ((0, 32),), jnp.float32),
        "feed_bias_out": normal_values(splits[16], (D,), 1.5, 6.0, ((0, 32),), jnp.float32),
    }


@jax.custom_vjp
def low(v):
    return lax.optimization_barrier(v.astype(jnp.bfloat16)).astype(jnp.float32)

@jax.custom_vjp
def low_back(v):
    return v

def low_keep(v):
    return (low(v), None)

def low_pass(kept, grad):
    return (grad,)

def back_keep(v):
    return (v, None)

def back_low(kept, grad):
    return (low(grad),)
low.defvjp(low_keep, low_pass)
low_back.defvjp(back_keep, back_low)

def matmul(left, right):
    return jnp.dot(left, right, precision=lax.Precision.HIGHEST, preferred_element_type=jnp.float32)

def segment_numbers(lengths, positions, padding_id):
    boundary = jnp.cumsum(lengths, dtype=jnp.int32)
    position = jnp.arange(positions, dtype=jnp.int32)
    number = lax.optimization_barrier(jnp.sum((position[:, None] >= boundary[None, :]).astype(jnp.int32), axis=1, dtype=jnp.int32))
    present = position < boundary[-1]
    return (jnp.where(present, number, padding_id), present)

def attend(queries, key_rows, value_rows, allowed):
    head_count = queries.shape[1] // HEAD
    query_heads = queries.reshape(queries.shape[0], head_count, HEAD)
    key_heads = key_rows.reshape(key_rows.shape[0], head_count, HEAD)
    value_heads = value_rows.reshape(value_rows.shape[0], head_count, HEAD)
    raw_scores = low_back(jnp.einsum('qhd,khd->hqk', query_heads, key_heads, precision=lax.Precision.HIGHEST))
    scores = jnp.where(allowed[None], raw_scores * HEAD ** (-0.5), -1e+30)
    chances = jax.nn.softmax(scores, axis=-1)
    mixed_heads = jnp.einsum('hqk,khd->qhd', low(chances), value_heads, precision=lax.Precision.HIGHEST)
    return mixed_heads.reshape(queries.shape[0], queries.shape[1])

def pack_forward(rounded, scale_gate, token_rows, memory_rows, target_lengths, source_lengths):
    self_in, self_out, self_bias, cross_query, cross_key_value, cross_out, cross_bias, feed_in, feed_out, feed_bias_in, feed_bias_out = rounded
    model_width = token_rows.shape[1]
    query_ids, present = segment_numbers(target_lengths, TOK_DEV, SLOTS)
    memory_ids = segment_numbers(source_lengths, MEM_DEV, SLOTS + 1)[0]
    position = jnp.arange(TOK_DEV, dtype=jnp.int32)
    self_allowed = (query_ids[:, None] == query_ids[None, :]) & (position[None, :] <= position[:, None])
    cross_allowed = query_ids[:, None] == memory_ids[None, :]
    branch_scale = scale_gate * present.astype(jnp.float32)[:, None]
    zero_row = jnp.zeros((1, model_width), jnp.float32)
    projected = low(low_back(matmul(token_rows, self_in) + jnp.concatenate([self_bias[0:1], zero_row, self_bias[1:2]], axis=1)))
    self_mixed = low(low_back(attend(projected[:, :model_width], projected[:, model_width:2 * model_width], projected[:, 2 * model_width:], self_allowed)))
    first_sum = token_rows + branch_scale * low_back(matmul(self_mixed, self_out) + self_bias[2])
    cross_queries = low(low_back(matmul(low(first_sum), cross_query) + cross_bias[0]))
    memory_kv = low(low_back(matmul(memory_rows, cross_key_value) + jnp.concatenate([zero_row, cross_bias[1:2]], axis=1)))
    cross_mixed = low(low_back(attend(cross_queries, memory_kv[:, :model_width], memory_kv[:, model_width:], cross_allowed)))
    second_sum = first_sum + branch_scale * low_back(matmul(cross_mixed, cross_out) + cross_bias[2])
    before = low_back(matmul(low(second_sum), feed_in) + feed_bias_in)
    hidden = low(jax.nn.gelu(before, approximate=True))
    return second_sum + branch_scale * low_back(matmul(hidden, feed_out) + feed_bias_out)

def reference(tokens, memory, out_cotangent, seq_lengths, memory_lengths, residual_gate, self_in, self_out, self_bias, cross_query, cross_key_value, cross_out, cross_bias, feed_in, feed_out, feed_bias_in, feed_bias_out):
    masters = (self_in, self_out, self_bias, cross_query, cross_key_value, cross_out, cross_bias, feed_in, feed_out, feed_bias_in, feed_bias_out)
    scale_gate = residual_gate[0]

    def layer_forward(token_rows, memory_rows, weight_list):
        rounded = tuple((low(weight_entry) for weight_entry in weight_list))
        packed_step = jax.checkpoint(partial(pack_forward, rounded, scale_gate))

        def scan_step(running, pieces):
            return (running, packed_step(*pieces))
        pieces = (token_rows.reshape(PACKS, TOK_DEV, D), memory_rows.reshape(PACKS, MEM_DEV, D), seq_lengths, memory_lengths)
        result = lax.scan(scan_step, jnp.zeros((), jnp.float32), pieces)[1]
        return result.reshape(TOKENS, D)
    result, pull_back = jax.vjp(layer_forward, tokens.astype(jnp.float32), memory.astype(jnp.float32), masters)
    tokens_grad, memory_grad, gradients = pull_back(out_cotangent.astype(jnp.float32))
    return (result.astype(jnp.bfloat16), tokens_grad, memory_grad, gradients[0], gradients[1], gradients[2], gradients[3], gradients[4], gradients[5], gradients[6], gradients[7], gradients[8], gradients[9], gradients[10])
```

```python
import jax
import jax.numpy as jnp
from jax import lax
from jax.sharding import PartitionSpec as P

HEAD = 64
AXES = ("dp", "fsdp")


def rows_all(shard):
    return lax.all_gather(shard, AXES, axis=0, tiled=True)


def sum_to_owners(grads, device_count, orders):
    me = lax.axis_index(AXES)
    running = []
    for grad in grads:
        rows, columns = grad.shape
        bits = device_count.bit_length() - 1
        running.append(grad.reshape((2,) * bits + (rows // device_count, columns)))
    left = [list(range(device_count.bit_length() - 1)) for _ in grads]
    for step in range(device_count.bit_length() - 1):
        sent = []
        for part, order in enumerate(orders):
            bit = order[step]
            axis = len(left[part]) - 1 - left[part].index(bit)
            mine = (me >> bit) & 1
            away = lax.dynamic_index_in_dim(running[part], 1 - mine, axis, keepdims=False)
            pairs = [(i, i ^ (1 << bit)) for i in range(device_count)]
            sent.append((axis, mine, lax.ppermute(away.astype(jnp.bfloat16), AXES, pairs)))
            left[part].remove(bit)
        for part, (axis, mine, got) in enumerate(sent):
            kept = lax.dynamic_index_in_dim(running[part], mine, axis, keepdims=False)
            running[part] = kept.astype(jnp.float32) + got.astype(jnp.float32)
    return running


def column_orders(device_count):
    bits = device_count.bit_length() - 1
    high = list(range(1, bits))[::-1]
    first = [0] + high
    second = [0] + [high[1], high[0]] + high[2:]
    return first, second


def scatter_rows(grad, device_count):
    half = grad.shape[1] // 256 * 128
    first, second = column_orders(device_count)
    left, right = sum_to_owners(
        [grad[:, :half], grad[:, half:]], device_count, (first, second)
    )
    return jnp.concatenate([left, right], axis=1)


def segment_numbers(lengths, positions, padding_id):
    boundary = jnp.cumsum(lengths, dtype=jnp.int32)
    position = lax.broadcasted_iota(jnp.int32, (positions, 1), 0)
    number = jnp.sum((position >= boundary[None, :]).astype(jnp.int32), axis=1, dtype=jnp.int32)
    present = position[:, 0] < boundary[-1]
    return (jnp.where(present, number, padding_id), present)


def allowed_block(query_ids, key_ids, row_start, causal):
    allowed = query_ids[:, None] == key_ids[None, :]
    if causal:
        query_place = row_start + lax.broadcasted_iota(jnp.int32, (query_ids.shape[0], 1), 0)
        key_place = lax.broadcasted_iota(jnp.int32, (1, key_ids.shape[0]), 1)
        allowed = allowed & (key_place <= query_place)
    return allowed


def block_layout(queries, query_ids):
    query_count = queries.shape[0]
    block_rows = min(512, query_count)
    block_count = query_count // block_rows
    head_count = queries.shape[1] // HEAD
    shaped = queries.reshape(block_count, block_rows, head_count, HEAD)
    id_blocks = query_ids.reshape(block_count, block_rows)
    starts = jnp.arange(block_count, dtype=jnp.int32) * block_rows
    return (shaped, id_blocks, starts)


def block_scores(query_block, key_heads, id_block, key_ids, row_start, causal):
    raw_scores = jnp.einsum(
        "qhd,khd->hqk", query_block, key_heads, preferred_element_type=jnp.float32
    )
    allowed = allowed_block(id_block, key_ids, row_start, causal)
    return jnp.where(allowed[None], raw_scores * HEAD ** (-0.5), -1e30)


def attend_forward(queries, key_rows, value_rows, query_ids, key_ids, causal):
    shaped, id_blocks, starts = block_layout(queries, query_ids)
    head_count = shaped.shape[2]
    key_heads = key_rows.reshape(key_rows.shape[0], head_count, HEAD)
    value_heads = value_rows.reshape(value_rows.shape[0], head_count, HEAD)

    def per_block(pieces):
        query_block, id_block, row_start = pieces
        scores = block_scores(query_block, key_heads, id_block, key_ids, row_start, causal)
        row_max = jnp.max(scores, axis=-1, keepdims=True)
        exponentials = jnp.exp(scores - row_max)
        row_total = jnp.sum(exponentials, axis=-1, keepdims=True)
        weights_low = (exponentials / row_total).astype(jnp.bfloat16)
        mixed_heads = jnp.einsum(
            "hqk,khd->qhd", weights_low, value_heads, preferred_element_type=jnp.float32
        )
        return (mixed_heads.astype(jnp.bfloat16), (row_max + jnp.log(row_total))[..., 0])

    mixed_heads, log_totals = lax.map(per_block, (shaped, id_blocks, starts))
    return (mixed_heads.reshape(queries.shape[0], queries.shape[1]), log_totals)


def attend_backward(
    queries, key_rows, value_rows, query_ids, key_ids, causal, log_totals, incoming
):
    shaped, id_blocks, starts = block_layout(queries, query_ids)
    head_count = shaped.shape[2]
    key_heads = key_rows.reshape(key_rows.shape[0], head_count, HEAD)
    value_heads = value_rows.reshape(value_rows.shape[0], head_count, HEAD)
    incoming_blocks = incoming.reshape(shaped.shape)

    def per_block(running, pieces):
        key_sum, value_sum = running
        query_block, incoming_block, log_block, id_block, row_start = pieces
        scores = block_scores(query_block, key_heads, id_block, key_ids, row_start, causal)
        chances = jnp.exp(scores - log_block[..., None])
        pushed = jnp.einsum(
            "qhd,khd->hqk", incoming_block, value_heads, preferred_element_type=jnp.float32
        )
        row_delta = jnp.sum(chances * pushed, axis=-1, keepdims=True)
        score_grad = (chances * (pushed - row_delta) * HEAD ** (-0.5)).astype(jnp.bfloat16)
        query_grad = jnp.einsum(
            "hqk,khd->qhd", score_grad, key_heads, preferred_element_type=jnp.float32
        )
        key_sum = key_sum + jnp.einsum(
            "hqk,qhd->khd", score_grad, query_block, preferred_element_type=jnp.float32
        )
        value_sum = value_sum + jnp.einsum(
            "hqk,qhd->khd",
            chances.astype(jnp.bfloat16),
            incoming_block,
            preferred_element_type=jnp.float32,
        )
        return ((key_sum, value_sum), query_grad)

    start_sums = (
        jnp.zeros(key_heads.shape, jnp.float32),
        jnp.zeros(value_heads.shape, jnp.float32),
    )
    sums_after, query_grads = lax.scan(
        per_block, start_sums, (shaped, incoming_blocks, log_totals, id_blocks, starts)
    )
    return (
        query_grads.reshape(queries.shape[0], queries.shape[1]),
        sums_after[0].reshape(key_rows.shape[0], key_rows.shape[1]),
        sums_after[1].reshape(value_rows.shape[0], value_rows.shape[1]),
    )


def gelu_tanh(values):
    return jax.nn.gelu(values, approximate=True)


def on_device(
    tokens,
    memory,
    out_cotangent,
    seq_lengths,
    memory_lengths,
    residual_gate,
    self_in,
    self_out,
    self_bias,
    cross_query,
    cross_key_value,
    cross_out,
    cross_bias,
    feed_in,
    feed_out,
    feed_bias_in,
    feed_bias_out,
):
    low_type = jnp.bfloat16
    full_type = jnp.float32
    model_width = tokens.shape[1]
    slot_count = seq_lengths.shape[1]
    query_ids, present = segment_numbers(seq_lengths[0], tokens.shape[0], slot_count)
    memory_ids = segment_numbers(memory_lengths[0], memory.shape[0], slot_count + 1)[0]
    branch_scale = residual_gate[0] * present.astype(full_type)[:, None]
    zero_row = jnp.zeros((1, model_width), full_type)
    device_count = lax.axis_size(AXES)
    own_rows = self_in.shape[0]
    packed = jnp.concatenate(
        [
            self_in,
            self_out.T,
            cross_query,
            cross_key_value,
            cross_out.T,
            feed_in,
            feed_out.T,
            self_bias.T,
            cross_bias.T,
            feed_bias_out[:, None],
            feed_bias_in.reshape(own_rows, -1),
        ],
        axis=1,
    ).astype(low_type)
    spare = -packed.shape[1] % 128
    whole = rows_all(jnp.pad(packed, ((0, 0), (0, spare))))
    ff = feed_in.shape[1]
    d = model_width
    self_full = (whole[:, : 3 * d], whole[:, 3 * d : 4 * d].T)
    cross_full = (
        whole[:, 4 * d : 5 * d],
        whole[:, 5 * d : 7 * d],
        whole[:, 7 * d : 8 * d].T,
    )
    feed_full = (
        whole[:, 8 * d : 8 * d + ff],
        whole[:, 8 * d + ff : 8 * d + 2 * ff].T,
    )
    at = 8 * d + 2 * ff
    self_bias_full = whole[:, at : at + 3].T.astype(full_type)
    cross_bias_full = whole[:, at + 3 : at + 6].T.astype(full_type)
    feed_bias_out_full = whole[:, at + 6].astype(full_type)
    feed_bias_in_full = whole[:, at + 7 : at + 7 + ff // d].reshape(ff).astype(full_type)
    projected = (
        jnp.dot(tokens, self_full[0], preferred_element_type=full_type)
        + jnp.concatenate([self_bias_full[0:1], zero_row, self_bias_full[1:2]], axis=1)
    ).astype(low_type)
    self_mixed, self_logs = attend_forward(
        projected[:, :model_width],
        projected[:, model_width : 2 * model_width],
        projected[:, 2 * model_width :],
        query_ids,
        query_ids,
        True,
    )
    first_sum = tokens.astype(full_type) + branch_scale * (
        jnp.dot(self_mixed, self_full[1], preferred_element_type=full_type) + self_bias_full[2]
    )
    first_low = first_sum.astype(low_type)
    cross_queries = (
        jnp.dot(first_low, cross_full[0], preferred_element_type=full_type) + cross_bias_full[0]
    ).astype(low_type)
    memory_kv = (
        jnp.dot(memory, cross_full[1], preferred_element_type=full_type)
        + jnp.concatenate([zero_row, cross_bias_full[1:2]], axis=1)
    ).astype(low_type)
    cross_mixed, cross_logs = attend_forward(
        cross_queries,
        memory_kv[:, :model_width],
        memory_kv[:, model_width:],
        query_ids,
        memory_ids,
        False,
    )
    second_sum = first_sum + branch_scale * (
        jnp.dot(cross_mixed, cross_full[2], preferred_element_type=full_type) + cross_bias_full[2]
    )
    second_low = second_sum.astype(low_type)
    before = jnp.dot(second_low, feed_full[0], preferred_element_type=full_type) + feed_bias_in_full
    hidden = gelu_tanh(before).astype(low_type)
    output = (
        second_sum
        + branch_scale
        * (
            jnp.dot(hidden, feed_full[1], preferred_element_type=full_type)
            + feed_bias_out_full
        )
    ).astype(low_type)
    upstream = out_cotangent.astype(full_type)
    feed_signal = (branch_scale * upstream).astype(low_type)
    feed_out_local = jnp.einsum("tf,td->fd", hidden, feed_signal, preferred_element_type=full_type)
    feed_bias_out_local = jnp.sum(feed_signal.astype(full_type), axis=0)
    hidden_grad = jnp.einsum(
        "td,fd->tf", feed_signal, feed_full[1], preferred_element_type=full_type
    )
    gelu_pull = jax.vjp(gelu_tanh, before)[1]
    before_grad = gelu_pull(hidden_grad)[0].astype(low_type)
    feed_in_local = jnp.einsum(
        "td,tf->df", second_low, before_grad, preferred_element_type=full_type
    )
    feed_bias_in_local = jnp.sum(before_grad.astype(full_type), axis=0)
    second_grad = upstream + jnp.einsum(
        "tf,df->td", before_grad, feed_full[0], preferred_element_type=full_type
    )
    feed_owned = scatter_rows(jnp.concatenate([feed_in_local, feed_out_local.T], axis=1), device_count)
    cross_signal = (branch_scale * second_grad).astype(low_type)
    cross_out_local = jnp.einsum(
        "tc,td->cd", cross_mixed, cross_signal, preferred_element_type=full_type
    )
    cross_mixed_grad = jnp.einsum(
        "td,cd->tc", cross_signal, cross_full[2], preferred_element_type=full_type
    ).astype(low_type)
    query_part, key_part, value_part = attend_backward(
        cross_queries,
        memory_kv[:, :model_width],
        memory_kv[:, model_width:],
        query_ids,
        memory_ids,
        False,
        cross_logs,
        cross_mixed_grad,
    )
    cross_query_signal = query_part.astype(low_type)
    memory_signal = jnp.concatenate([key_part, value_part], axis=1).astype(low_type)
    cross_query_local = jnp.einsum(
        "tc,td->cd", first_low, cross_query_signal, preferred_element_type=full_type
    )
    cross_key_value_local = jnp.einsum(
        "mc,me->ce", memory, memory_signal, preferred_element_type=full_type
    )
    cross_bias_local = jnp.stack(
        [
            jnp.sum(cross_query_signal.astype(full_type), axis=0),
            jnp.sum(memory_signal[:, model_width:].astype(full_type), axis=0),
            jnp.sum(cross_signal.astype(full_type), axis=0),
        ]
    )
    memory_grad = jnp.einsum(
        "me,ce->mc", memory_signal, cross_full[1], preferred_element_type=full_type
    )
    first_grad = second_grad + jnp.einsum(
        "td,cd->tc", cross_query_signal, cross_full[0], preferred_element_type=full_type
    )
    cross_owned = scatter_rows(
        jnp.concatenate([cross_query_local, cross_key_value_local, cross_out_local.T], axis=1),
        device_count,
    )
    self_signal = (branch_scale * first_grad).astype(low_type)
    self_out_local = jnp.einsum(
        "tc,td->cd", self_mixed, self_signal, preferred_element_type=full_type
    )
    self_mixed_grad = jnp.einsum(
        "td,cd->tc", self_signal, self_full[1], preferred_element_type=full_type
    ).astype(low_type)
    query_self, key_self, value_self = attend_backward(
        projected[:, :model_width],
        projected[:, model_width : 2 * model_width],
        projected[:, 2 * model_width :],
        query_ids,
        query_ids,
        True,
        self_logs,
        self_mixed_grad,
    )
    projected_signal = jnp.concatenate([query_self, key_self, value_self], axis=1).astype(low_type)
    self_in_local = jnp.einsum(
        "tc,te->ce", tokens, projected_signal, preferred_element_type=full_type
    )
    self_bias_local = jnp.stack(
        [
            jnp.sum(projected_signal[:, :model_width].astype(full_type), axis=0),
            jnp.sum(projected_signal[:, 2 * model_width :].astype(full_type), axis=0),
            jnp.sum(self_signal.astype(full_type), axis=0),
        ]
    )
    tokens_grad = first_grad + jnp.einsum(
        "te,ce->tc", projected_signal, self_full[0], preferred_element_type=full_type
    )
    bias_columns = jnp.concatenate(
        [
            self_bias_local.T,
            cross_bias_local.T,
            feed_bias_out_local[:, None],
            feed_bias_in_local.reshape(d, -1),
        ],
        axis=1,
    )
    bias_columns = jnp.pad(bias_columns, ((0, 0), (0, -bias_columns.shape[1] % 128)))
    self_owned = scatter_rows(
        jnp.concatenate([self_in_local, self_out_local.T, bias_columns], axis=1), device_count
    )
    bias_owned = self_owned[:, 4 * d :]
    return (
        output,
        tokens_grad,
        memory_grad,
        self_owned[:, : 3 * d],
        self_owned[:, 3 * d : 4 * d].T,
        bias_owned[:, 0:3].T,
        cross_owned[:, :d],
        cross_owned[:, d : 3 * d],
        cross_owned[:, 3 * d :].T,
        bias_owned[:, 3:6].T,
        feed_owned[:, :ff],
        feed_owned[:, ff:].T,
        bias_owned[:, 7 : 7 + ff // d].reshape(feed_bias_in.shape),
        bias_owned[:, 6],
    )


def solution(mesh):
    return jax.shard_map(
        on_device,
        mesh=mesh,
        in_specs=(
            P(("dp", "fsdp"), None),
            P(("dp", "fsdp"), None),
            P(("dp", "fsdp"), None),
            P(("dp", "fsdp"), None),
            P(("dp", "fsdp"), None),
            P(),
            P(("dp", "fsdp"), None),
            P(None, ("dp", "fsdp")),
            P(None, ("dp", "fsdp")),
            P(("dp", "fsdp"), None),
            P(("dp", "fsdp"), None),
            P(None, ("dp", "fsdp")),
            P(None, ("dp", "fsdp")),
            P(("dp", "fsdp"), None),
            P(None, ("dp", "fsdp")),
            P(("dp", "fsdp")),
            P(("dp", "fsdp")),
        ),
        out_specs=(
            P(("dp", "fsdp"), None),
            P(("dp", "fsdp"), None),
            P(("dp", "fsdp"), None),
            P(("dp", "fsdp"), None),
            P(None, ("dp", "fsdp")),
            P(None, ("dp", "fsdp")),
            P(("dp", "fsdp"), None),
            P(("dp", "fsdp"), None),
            P(None, ("dp", "fsdp")),
            P(None, ("dp", "fsdp")),
            P(("dp", "fsdp"), None),
            P(None, ("dp", "fsdp")),
            P(("dp", "fsdp")),
            P(("dp", "fsdp")),
        ),
        check_vma=False,
    )
```

```python
import functools

import jax
import jax.numpy as jnp
from jax import lax
from jax.experimental import pallas as pl
from jax.experimental.pallas import tpu as pltpu
from jax.sharding import PartitionSpec as P

HEAD = 64
LANES = 128
FAR = -1e30
AXES = ("dp", "fsdp")
LOW = jnp.bfloat16
FULL = jnp.float32
ROOM = 56 << 20


def nn(left, right):
    return lax.dot_general(left, right, (((1,), (0,)), ((), ())), preferred_element_type=FULL)


def nt(left, right):
    return lax.dot_general(left, right, (((1,), (1,)), ((), ())), preferred_element_type=FULL)


def tn(left, right):
    return lax.dot_general(left, right, (((0,), (0,)), ((), ())), preferred_element_type=FULL)


def one_head(pair, odd):
    lane = lax.broadcasted_iota(jnp.int32, pair.shape, 1)
    return jnp.where((lane >= HEAD) == bool(odd), pair, jnp.zeros_like(pair))


def later_keys(rows, keys):
    query = lax.broadcasted_iota(jnp.int32, (rows, keys), 0)
    key = lax.broadcasted_iota(jnp.int32, (rows, keys), 1)
    return query, key


def call(body, name, grid, ins, outs, scratch=(), flops=0, moved=0, after=(), scalars=()):
    used = len(ins)

    def only_used(*refs):
        front = len(scalars)
        body(*refs[: front + used], *refs[front + used + len(after) :])

    def spec_of(spec):
        if not scalars or spec.index_map is None:
            return spec
        place = spec.index_map
        return pl.BlockSpec(
            spec.block_shape, lambda i, *_: place(i), pipeline_mode=spec.pipeline_mode
        )

    return pl.pallas_call(
        only_used if after else body,
        name=name,
        grid_spec=pltpu.PrefetchScalarGridSpec(
            num_scalar_prefetch=len(scalars),
            grid=(grid,),
            in_specs=[spec_of(spec) for _, spec in ins]
            + [pl.BlockSpec(memory_space=pl.ANY) for _ in after],
            out_specs=[spec_of(spec) for _, _, spec in outs],
            scratch_shapes=list(scratch),
        ),
        out_shape=[jax.ShapeDtypeStruct(shape, kind) for shape, kind, _ in outs],
        compiler_params=pltpu.CompilerParams(vmem_limit_bytes=ROOM),
        cost_estimate=pl.CostEstimate(flops=flops, bytes_accessed=moved, transcendentals=0),
    )(*scalars, *[array for array, _ in ins], *after)


def rows_of(block, columns):
    return pl.BlockSpec((block, columns), lambda i: (i, 0))


def fixed(shape, place=None):
    place = (0,) * len(shape) if place is None else place
    return pl.BlockSpec(shape, lambda i: place, pipeline_mode=pl.Buffered(1))


def all_of(array):
    return (array, fixed(array.shape))


def out_all(shape, kind):
    return (shape, kind, fixed(shape))


def attend(queries, hot, keys_ref, values_ref, count, causal):
    rows = queries.shape[0]
    pairs = queries.shape[1] // LANES
    lane = lax.broadcasted_iota(jnp.int32, (rows, LANES), 1)
    logs = jnp.zeros((rows, LANES), FULL)
    if causal:
        query, key = later_keys(rows, rows)
        ahead = jnp.where(key <= query, 0.0, FAR)
    mixed = []
    for pair in range(pairs):
        columns = slice(pair * LANES, (pair + 1) * LANES)
        total = None
        for odd in range(2):
            asked = jnp.concatenate([one_head(queries[:, columns], odd), hot], axis=1)
            spans = [(0, count)]
            if causal:
                spans = [(0, count - rows), (count - rows, count)]
                spans = [span for span in spans if span[0] < span[1]]
            scores = [nt(asked, keys_ref[pair, a:b, :]) for a, b in spans]
            if causal:
                scores[-1] = scores[-1] + ahead
            top = functools.reduce(
                jnp.maximum, [jnp.max(part, axis=1, keepdims=True) for part in scores]
            )
            weights = [jnp.exp(part - top) for part in scores]
            amount = sum(jnp.sum(part, axis=1, keepdims=True) for part in weights)
            share = 1.0 / amount
            heads = sum(
                nn((part * share).astype(LOW), values_ref[a:b, columns])
                for part, (a, b) in zip(weights, spans)
            )
            total = heads if total is None else jnp.where(lane < HEAD, total, heads)
            logs = jnp.where(lane == 2 * pair + odd, top + jnp.log(amount), logs)
        mixed.append(total)
    return jnp.concatenate(mixed, axis=1), logs.T[: 2 * pairs]


def keep_keys(keys_ref, place, keys, hot):
    pairs = keys.shape[1] // LANES
    for pair in range(pairs):
        keys_ref[pair, place, :LANES] = keys[:, pair * LANES : (pair + 1) * LANES]
        keys_ref[pair, place, LANES:] = hot


def self_forward(
    tokens, hot, far, gate, w_in, w_out, bias_columns, w_query,
    projected, mixed, logs, first, cross_queries, keys, values, bias,
):
    step = pl.program_id(0)
    rows, d = tokens.shape

    @pl.when(step == 0)
    def _():
        bias[...] = bias_columns[:, :LANES].astype(FULL).T[:8]

    joined_bias = jnp.concatenate([bias[0:1, :], jnp.zeros((1, d), FULL), bias[1:2, :]], axis=1)
    made = (nn(tokens[...], w_in[...]) + joined_bias).astype(LOW)
    projected[...] = made
    place = pl.ds(pl.multiple_of(step * rows, rows), rows)
    keep_keys(keys, place, made[:, d : 2 * d], far[...])
    values[place, :] = made[:, 2 * d :]
    for block in range(values.shape[0] // rows):

        @pl.when(step == block)
        def _(count=(block + 1) * rows):
            scaled = made[:, :d] * jnp.asarray(HEAD**-0.5, LOW)
            mixed[...], logs[...] = attend(scaled, hot[...], keys, values, count, True)

    branch = nt(mixed[...].astype(LOW), w_out[...]) + bias[2:3, :]
    total = tokens[...].astype(FULL) + gate[...] * branch
    first[...] = total
    cross_queries[...] = (nn(total.astype(LOW), w_query[...]) + bias[3:4, :]).astype(LOW)


def cross_forward(
    queries, memory, hot, far, gate, first, w_kv, w_out, bias_columns,
    memory_kv, mixed, logs, second, keys, bias,
):
    d = memory.shape[1]

    @pl.when(pl.program_id(0) == 0)
    def _():
        bias[...] = bias_columns[:, :LANES].astype(FULL).T[:8]
        made = nn(memory[...], w_kv[...])
        memory_kv[:, :d] = made[:, :d].astype(LOW)
        memory_kv[:, d:] = (made[:, d:] + bias[4:5, :]).astype(LOW)
        keep_keys(keys, slice(None), memory_kv[:, :d], far[...])

    scaled = queries[...] * jnp.asarray(HEAD**-0.5, LOW)
    mixed[...], logs[...] = attend(
        scaled, hot[...], keys, memory_kv.at[:, d:], memory.shape[0], False
    )
    branch = nt(mixed[...].astype(LOW), w_out[...]) + bias[5:6, :]
    second[...] = first[...] + gate[...] * branch


def head_sums(left, right):
    d = left.shape[1]
    head = lax.broadcasted_iota(jnp.int32, (d // HEAD, d), 0)
    column = lax.broadcasted_iota(jnp.int32, (d // HEAD, d), 1)
    chosen = (column // HEAD == head).astype(FULL)
    return lax.dot_general(
        chosen,
        left.astype(FULL) * right.astype(FULL),
        (((1,), (1,)), ((), ())),
        precision=lax.Precision.HIGHEST,
        preferred_element_type=FULL,
    )


def gelu_both(z):
    c = 0.7978845608028654
    square = z * z
    bent = jnp.tanh(c * z * (1.0 + 0.044715 * square))
    half = 0.5 * (1.0 + bent)
    slope = half + 0.5 * z * (1.0 - bent * bent) * (c * (1.0 + 3.0 * 0.044715 * square))
    return z * half, slope


def spread(d, ff):
    each = ff // d
    row = lax.broadcasted_iota(jnp.int32, (d, ff), 0)
    entry = lax.broadcasted_iota(jnp.int32, (d, ff), 1)
    column = lax.broadcasted_iota(jnp.int32, (LANES, ff), 0)
    there = lax.broadcasted_iota(jnp.int32, (LANES, ff), 1)
    return entry // each == row, (there % each == column).astype(LOW)


def columns_to_row(columns, ff):
    owner, place = spread(columns.shape[0], ff)
    return jnp.sum(jnp.where(owner, nn(columns, place), 0.0), axis=0, keepdims=True)


def row_to_columns(row, d):
    owner, place = spread(d, row.shape[1])
    return nt(jnp.where(owner, row, 0.0).astype(LOW), place).astype(LOW)


def rows_to_columns(*rows):
    d = rows[0].shape[1]
    stack = jnp.concatenate([*rows, jnp.zeros((LANES - len(rows), d), FULL)], axis=0)
    return stack.T.astype(LOW)


def feed_both(
    second, upstream, gate, mixed, w_in, w_out, w_cross_out, bias_columns,
    output, second_grad, cross_signal, mixed_grad, deltas, feed_grad, sums,
    second_low, signal_all, hidden_all, before_all, bias, bias_in, bias_in_grad,
):
    step = pl.program_id(0)
    rows, d = second.shape
    ff = w_in.shape[1]
    place = pl.ds(pl.multiple_of(step * rows, rows), rows)
    low = second[...].astype(LOW)
    second_low[place, :] = low
    given = upstream[...].astype(FULL)
    signal = (gate[...] * given).astype(LOW)
    signal_all[place, :] = signal

    @pl.when(step == 0)
    def _():
        bias[...] = bias_columns[:, :LANES].astype(FULL).T[:8]
        bias_in[...] = columns_to_row(bias_columns[:, LANES:], ff)
        bias_in_grad[...] = jnp.zeros_like(bias_in_grad)
        sums[...] = jnp.zeros_like(sums)

    made = bias[6:7, :]
    back = given


    width = 512
    for start in range(0, ff, width):
        part = slice(start, start + width)
        before = nn(low, w_in[:, part]) + bias_in[:, part]
        hidden, slope = gelu_both(before)
        hidden = hidden.astype(LOW)
        hidden_all[place, part] = hidden
        made = made + nt(hidden, w_out[:, part])
        before_grad = (nn(signal, w_out[:, part]) * slope).astype(LOW)
        before_all[place, part] = before_grad
        back = back + nt(before_grad, w_in[:, part])
        bias_in_grad[:, part] += jnp.sum(before_grad.astype(FULL), axis=0, keepdims=True)
    output[...] = (second[...] + gate[...] * made).astype(LOW)
    second_grad[...] = back
    crossed = (gate[...] * back).astype(LOW)
    cross_signal[...] = crossed
    mixed_back = nn(crossed, w_cross_out[...]).astype(LOW)
    mixed_grad[...] = mixed_back
    deltas[...] = head_sums(mixed_back, mixed[...])
    sums[0:1, :] += jnp.sum(signal.astype(FULL), axis=0, keepdims=True)
    sums[1:2, :] += jnp.sum(crossed.astype(FULL), axis=0, keepdims=True)

    @pl.when(step == pl.num_programs(0) - 1)
    def _():
        for start in range(0, ff, width):
            part = slice(start, start + width)
            feed_grad[:, part] = tn(second_low[...], before_all[:, part]).astype(LOW)
            feed_grad[:, ff + start : ff + start + width] = tn(
                signal_all[...], hidden_all[:, part]
            ).astype(LOW)
        feed_grad[:, 2 * ff : 2 * ff + LANES] = rows_to_columns(sums[0:1, :])
        feed_grad[:, 2 * ff + LANES :] = row_to_columns(bias_in_grad[...], d)


def attend_back(
    queries, keys, values, hot, far, mixed_grad, logs, deltas,
    query_grad, key_grad, value_grad, key_sum, value_sum, reached, *, causal, block, pair,
):
    count = keys.shape[0]
    reached[:, :LANES] = keys[...]
    reached[:, LANES:] = far[...]
    turned = keys[...].T
    if causal:
        key, query = later_keys(block, block)
        ahead = jnp.where(key <= query, 0.0, FAR)
    for start in range(queries.shape[0] - block, -1, -block):
        place = slice(start, start + block)
        spans = [(0, count)]
        if causal:
            spans = [(0, start), (start, start + block)]
            spans = [span for span in spans if span[0] < span[1]]
        first = start == queries.shape[0] - block
        grad = []
        for odd in range(2):
            head = 2 * pair + odd
            asked = one_head(queries[place, :], odd) * jnp.asarray(HEAD**-0.5, LOW)
            wanted = jnp.concatenate([asked, hot[place, :]], axis=1)
            incoming = one_head(mixed_grad[place, :], odd)
            turned_grad = None
            for a, b in spans:
                scores = nt(reached[a:b, :], wanted)
                if causal and b == start + block:
                    scores = scores + ahead
                chances = jnp.exp(scores - logs[head : head + 1, place])
                pushed = nt(values[a:b, :], incoming)
                score_grad = (chances * (pushed - deltas[head : head + 1, place])).astype(LOW)
                value_part = nn(chances.astype(LOW), incoming)
                key_part = nn(score_grad, asked)
                if first and odd == 0:
                    value_sum[a:b, :] = value_part
                    key_sum[a:b, :] = key_part
                else:
                    value_sum[a:b, :] += value_part
                    key_sum[a:b, :] += key_part
                part = nn(turned[odd * HEAD : (odd + 1) * HEAD, a:b], score_grad)
                turned_grad = part if turned_grad is None else turned_grad + part
            grad.append(turned_grad)
        both = jnp.concatenate(grad, axis=0) * HEAD**-0.5
        query_grad[place, :] = both.T.astype(LOW)
    key_grad[...] = key_sum[...].astype(LOW)
    value_grad[...] = value_sum[...].astype(LOW)


def back_of_pair(
    queries, keys, values, hot, far, mixed_grad, logs, deltas, pair, causal, at, after=()
):
    count = queries.shape[0]
    key_count = keys.shape[0]
    column = lambda rows, place: pl.BlockSpec((rows, LANES), lambda i: (0, place))
    whole = lambda array: fixed(array.shape)
    flops = 5 * 2 * count * key_count * LANES * 2 // (2 if causal else 1)
    return call(
        functools.partial(attend_back, causal=causal, block=256, pair=pair),
        "self_back" if causal else "cross_back",
        1,
        [
            (queries, column(count, at[0] + pair)),
            (keys, column(key_count, at[1] + pair)),
            (values, column(key_count, at[2] + pair)),
            (hot, whole(hot)),
            (far, whole(far)),
            (mixed_grad, column(count, pair)),
            (logs, whole(logs)),
            (deltas, whole(deltas)),
        ],
        [
            ((count, LANES), LOW, fixed((count, LANES))),
            ((key_count, LANES), LOW, fixed((key_count, LANES))),
            ((key_count, LANES), LOW, fixed((key_count, LANES))),
        ],
        [
            pltpu.VMEM((key_count, LANES), FULL),
            pltpu.VMEM((key_count, LANES), FULL),
            pltpu.VMEM((key_count, 2 * LANES), LOW),
        ],
        flops=flops,
        moved=8 << 18,
        after=after,
    )


def joined(refs):
    return jnp.concatenate([ref[...] for ref in refs], axis=1)


def column_sum(array):
    return jnp.sum(array.astype(FULL), axis=0, keepdims=True)


def part_by_core(bits, grads, keep, away):
    own = keep.shape[1]
    for core in range(2):

        @pl.when(bits[0] == core)
        def _(core=core):
            for slab in range(2 * keep.shape[0]):
                there = keep if slab % 2 == core else away
                there[slab // 2] = grads[slab * own : (slab + 1) * own, :]


def cross_joined(bits, *refs, pairs):
    parts, refs = refs[: 3 * pairs], refs[3 * pairs :]
    (
        first, second_grad, memory, cross_signal, cross_mixed, self_mixed, gate, w_query, w_out,
        sums, *outs,
    ) = refs
    *owned, first_grad, mixed_grad, deltas, grads = outs
    d = first.shape[1]
    query_signal = joined(parts[0::3])
    key_signal = joined(parts[1::3])
    value_signal = joined(parts[2::3])
    grads[:, :d] = tn(memory[...], key_signal).astype(LOW)
    grads[:, d : 2 * d] = tn(memory[...], value_signal).astype(LOW)
    grads[:, 2 * d : 3 * d] = tn(first[...].astype(LOW), query_signal).astype(LOW)
    grads[:, 3 * d : 4 * d] = tn(cross_signal[...], cross_mixed[...].astype(LOW)).astype(LOW)
    back = second_grad[...] + nt(query_signal, w_query[...])
    first_grad[...] = back
    signal = (gate[...] * back).astype(LOW)
    grads[:, 4 * d : 5 * d] = tn(signal, self_mixed[...].astype(LOW)).astype(LOW)
    grads[:, 5 * d :] = rows_to_columns(
        column_sum(query_signal), column_sum(value_signal), sums[1:2, :], column_sum(signal)
    )
    mixed_back = nn(signal, w_out[...]).astype(LOW)
    mixed_grad[...] = mixed_back
    deltas[...] = head_sums(mixed_back, self_mixed[...])
    if len(owned) == 2:
        part_by_core(bits, grads, *owned)
    else:
        owned[0][...] = grads[...]


def self_joined(bits, *refs, pairs):
    parts, (tokens, *owned, signal, grads) = refs[: 3 * pairs], refs[3 * pairs :]
    d = tokens.shape[1]
    added = []
    for which in range(3):
        part = joined(parts[which::3])
        signal[:, which * d : (which + 1) * d] = part
        grads[:, which * d : (which + 1) * d] = tn(tokens[...], part).astype(LOW)
        if which != 1:
            added.append(column_sum(part))
    grads[:, 3 * d :] = rows_to_columns(*added)
    if len(owned) == 2:
        part_by_core(bits, grads, *owned)
    else:
        owned[0][...] = grads[...]


def last_grads(*refs, pairs):
    parts = refs[: 2 * pairs]
    signal, first_grad, w_in, w_kv, tokens_grad, memory_grad = refs[2 * pairs :]
    d = w_in.shape[0]
    tokens_grad[...] = first_grad[...] + nt(signal[...], w_in[...])
    memory_grad[...] = nt(joined(parts[0::2]), w_kv[:, :d]) + nt(joined(parts[1::2]), w_kv[:, d:])


def sum_to_owners(grads, device_count, orders):
    me = lax.axis_index(AXES)
    bits = device_count.bit_length() - 1
    running = []
    for grad in grads:
        rows, columns = grad.shape
        running.append(grad.reshape((2,) * bits + (rows // device_count, columns)))
    left = [list(range(bits)) for _ in grads]
    for step in range(bits):
        sent = []
        for part, order in enumerate(orders):
            bit = order[step]
            axis = len(left[part]) - 1 - left[part].index(bit)
            mine = (me >> bit) & 1
            away = lax.dynamic_index_in_dim(running[part], 1 - mine, axis, keepdims=False)
            pairs = [(i, i ^ (1 << bit)) for i in range(device_count)]
            sent.append((axis, mine, lax.ppermute(away.astype(LOW), AXES, pairs)))
            left[part].remove(bit)
        for part, (axis, mine, got) in enumerate(sent):
            kept = lax.dynamic_index_in_dim(running[part], mine, axis, keepdims=False)
            running[part] = kept.astype(FULL) + got.astype(FULL)
    return running


def swap(array, bit, device_count):
    return lax.ppermute(array, AXES, [(i, i ^ (1 << bit)) for i in range(device_count)])


def scatter_rows(grad, device_count):
    bits = device_count.bit_length() - 1
    high = list(range(1, bits))[::-1]
    half = grad.shape[1] // 256 * 128
    orders = ([0] + high, [0, high[1], high[0]] + high[2:])
    return jnp.concatenate(
        sum_to_owners([grad[:, :half], grad[:, half:]], device_count, orders), axis=1
    )


def plus(kept, got):
    return kept.astype(FULL) + got.astype(FULL)


def fold_core(bits, keep, got, away_x, away_y, keep_x, keep_y):
    half = away_x.shape[-1]
    x, y = bits[3], bits[4]
    for y_place in range(2):
        left = lambda at: plus(keep[y_place, at, :, :, :, :half], got[y_place, at, :, :, :, :half])
        away_x[y_place] = left(1 - x).astype(LOW)
        keep_x[y_place] = left(x)
    for x_place in range(2):
        right = lambda at: plus(keep[at, x_place, :, :, :, half:], got[at, x_place, :, :, :, half:])
        away_y[x_place] = right(1 - y).astype(LOW)
        keep_y[x_place] = right(y)


def fold_plane(bits, keep_x, got_x, keep_y, got_y, away_y, away_x, next_y, next_x):
    x, y = bits[3], bits[4]
    away_y[...] = plus(keep_x[1 - y], got_x[1 - y]).astype(LOW)
    next_y[...] = plus(keep_x[y], got_x[y])
    away_x[...] = plus(keep_y[1 - x], got_y[1 - x]).astype(LOW)
    next_x[...] = plus(keep_y[x], got_y[x])


def fold_line(bits, keep_y, got_y, keep_x, got_x, away, keep):
    half = keep_y.shape[-1]
    z = bits[1]
    for place in range(2):
        away[place, :, :half] = plus(keep_y[place, 1 - z], got_y[place, 1 - z]).astype(LOW)
        away[place, :, half:] = plus(keep_x[place, 1 - z], got_x[place, 1 - z]).astype(LOW)
        keep[place, :, :half] = plus(keep_y[place, z], got_y[place, z])
        keep[place, :, half:] = plus(keep_x[place, z], got_x[place, z])


def fold_ends(bits, keep, got, away, last):
    z = bits[2]
    away[...] = plus(keep[1 - z], got[1 - z]).astype(LOW)
    last[...] = plus(keep[z], got[z])


class Halving:
    def __init__(self, name, bits, keep, away, half, device_count):
        self.name, self.bits, self.half, self.device_count = name, bits, half, device_count
        self.own, self.columns = keep.shape[-2:]
        shape = (2, 2, 2, 2, self.own, self.columns)
        self.kept = [keep.reshape(shape)]
        self.sent = [away.reshape(shape)]
        self.got = self.send(0)

    def send(self, *order):
        return [swap(array, bit, self.device_count) for array, bit in zip(self.sent, order)]

    def fold(self, body, step, outs, *order):
        ins = [all_of(part) for pair in zip(self.kept, self.got) for part in pair]
        made = call(
            body, self.name + step, 1, ins, [out_all(*out) for out in outs],
            scalars=(self.bits,), after=self.after,
        )
        count = len(made) // 2
        self.sent, self.kept = made[:count], made[count:]
        self.got = self.send(*order)

    def step(self, number, after=()):
        self.after = tuple(after)
        own, half, rest = self.own, self.half, self.columns - self.half
        if number == 1:
            left, right = (2, 2, 2, own, half), (2, 2, 2, own, rest)
            outs = [(left, LOW), (right, LOW), (left, FULL), (right, FULL)]
            self.fold(fold_core, "_core", outs, 3, 4)
        if number == 2:
            left, right = (2, 2, own, half), (2, 2, own, rest)
            outs = [(left, LOW), (right, LOW), (left, FULL), (right, FULL)]
            self.fold(fold_plane, "_plane", outs, 4, 3)
        if number == 3:
            both = (2, own, self.columns)
            self.fold(fold_line, "_line", [(both, LOW), (both, FULL)], 1)
        if number == 4:
            both = (own, self.columns)
            self.fold(fold_ends, "_ends", [(both, LOW), (both, FULL)], 2)


def cross_last(keep, got, kv, query, cross_out, self_out, cross_bias, self_bias):
    total = plus(keep[...], got[...])
    d = query.shape[1]
    kv[...] = total[:, : 2 * d]
    query[...] = total[:, 2 * d : 3 * d]
    cross_out[...] = total[:, 3 * d : 4 * d]
    self_out[...] = total[:, 4 * d : 5 * d]
    turned = turned_bias(total[:, 5 * d :])
    cross_bias[...] = turned[0:3]
    self_bias[...] = turned[3:4]


def turned_bias(columns):
    own = columns.shape[0]
    square = jnp.concatenate([columns, jnp.zeros((LANES - own, LANES), FULL)], axis=0)
    return square.T[:8, :own]


def self_last(keep, got, third, self_in, bias):
    total = plus(keep[...], got[...])
    columns = self_in.shape[1]
    self_in[...] = total[:, :columns]
    bias[0:2, :] = turned_bias(total[:, columns:])[0:2]
    bias[2:3, :] = third[...]


def feed_last(total, feed_in, feed_out, bias_out, bias_in):
    ff = feed_in.shape[1]
    feed_in[...] = total[:, :ff].astype(FULL)
    feed_out[...] = total[:, ff : 2 * ff].astype(FULL)
    bias_out[...] = turned_bias(total[:, 2 * ff : 2 * ff + LANES].astype(FULL))[0:1]
    bias_in[...] = total[:, 2 * ff + LANES :].astype(FULL)


def pack(
    self_in, self_out, cross_query, cross_kv, cross_out, feed_in, feed_out, self_bias, cross_bias,
    bias_out, bias_in, own_self, own_cross, own_feed,
):
    d = self_out.shape[1]
    ff = feed_in.shape[1]
    own = self_in.shape[0]
    own_self[:, : 3 * d] = self_in[...].astype(LOW)
    own_self[:, 3 * d : 4 * d] = self_out[...].astype(LOW)
    rows = jnp.concatenate(
        [self_bias[...], cross_bias[...], bias_out[...], jnp.zeros((LANES - 7, own), FULL)], axis=0
    )
    wide = jnp.concatenate([rows, jnp.zeros((LANES, LANES - own), FULL)], axis=1)
    own_self[:, 4 * d : 4 * d + LANES] = wide.T[:own].astype(LOW)
    own_self[:, 4 * d + LANES :] = jnp.zeros((own, LANES), LOW)
    own_self[:, 4 * d + LANES : 4 * d + LANES + ff // d] = bias_in[...].astype(LOW)
    own_cross[:, : 2 * d] = cross_kv[...].astype(LOW)
    own_cross[:, 2 * d : 3 * d] = cross_query[...].astype(LOW)
    own_cross[:, 3 * d :] = cross_out[...].astype(LOW)
    own_feed[:, :ff] = feed_in[...].astype(LOW)
    own_feed[:, ff:] = feed_out[...].astype(LOW)


def gather_halves(left, right, device_count):
    me = lax.axis_index(AXES)
    held = [left, right]
    known = [[], []]
    for bits in ((2, 2), (1, 1), (3, 4), (4, 3), (0, 0)):
        got = [swap(array, bit, device_count) for array, bit in zip(held, bits)]
        for part, bit in enumerate(bits):
            axis = sum(other > bit for other in known[part])
            low = jnp.stack([held[part], got[part]], axis)
            high = jnp.stack([got[part], held[part]], axis)
            held[part] = jnp.where((me >> bit) & 1, high, low)
            known[part].append(bit)
    return [array.reshape(-1, array.shape[-1]) for array in held]


def numbered(lengths, positions, padding):
    boundary = jnp.cumsum(lengths, dtype=jnp.int32)
    position = lax.broadcasted_iota(jnp.int32, (positions, 1), 0)
    number = jnp.sum((position >= boundary[None, :]).astype(jnp.int32), axis=1, keepdims=True)
    present = position < boundary[-1]
    return jnp.where(present, number, padding), present


def on_device(
    tokens, memory, out_cotangent, seq_lengths, memory_lengths, residual_gate,
    self_in, self_out, self_bias, cross_query, cross_key_value, cross_out, cross_bias,
    feed_in, feed_out, feed_bias_in, feed_bias_out,
):
    device_count = lax.axis_size(AXES)
    count, d = tokens.shape
    key_count = memory.shape[0]
    ff = feed_in.shape[1]
    own = self_in.shape[0]
    pairs = d // LANES
    heads = d // HEAD
    block = 256
    steps = count // block
    halving = lax.axis_size("dp") == 4 and lax.axis_size("fsdp") == 8
    me = lax.axis_index(AXES)
    bits = jnp.stack([(me >> bit) & 1 for bit in range(5)]).astype(jnp.int32)
    own_self, own_cross, own_feed = call(
        pack,
        "pack",
        1,
        [
            all_of(array)
            for array in (
                self_in, self_out.T, cross_query, cross_key_value, cross_out.T, feed_in,
                feed_out.T, self_bias, cross_bias, feed_bias_out[None], feed_bias_in.reshape(own, -1),
            )
        ],
        [
            out_all((own, 4 * d + 2 * LANES), LOW),
            out_all((own, 4 * d), LOW),
            out_all((own, 2 * ff), LOW),
        ],
    )
    feed_whole = lax.all_gather(own_feed, AXES, axis=0, tiled=True)
    if halving:
        self_whole, cross_whole = gather_halves(own_self, own_cross, device_count)
    else:
        self_whole = lax.all_gather(own_self, AXES, axis=0, tiled=True)
        cross_whole = lax.all_gather(own_cross, AXES, axis=0, tiled=True)
    w_self_in = (self_whole, fixed((d, 3 * d), (0, 0)))
    w_self_out = (self_whole, fixed((d, d), (0, 3)))
    bias_columns = (self_whole, fixed((d, 2 * LANES), (0, 4 * d // (2 * LANES))))
    w_kv = (cross_whole, fixed((d, 2 * d), (0, 0)))
    w_query = (cross_whole, fixed((d, d), (0, 2)))
    w_cross_out = (cross_whole, fixed((d, d), (0, 3)))
    w_feed_in = (feed_whole, fixed((d, ff), (0, 0)))
    w_feed_out = (feed_whole, fixed((d, ff), (0, 1)))

    slots = seq_lengths.shape[1]
    query_ids, present = numbered(seq_lengths[0], count, slots)
    memory_ids, _ = numbered(memory_lengths[0], key_count, slots + 1)
    lanes = lax.broadcasted_iota(jnp.int32, (1, LANES), 1)
    hot = (query_ids == lanes).astype(LOW)
    self_far = jnp.where(query_ids == lanes, 0.0, FAR).astype(LOW)
    memory_far = jnp.where(memory_ids == lanes, 0.0, FAR).astype(LOW)
    gate = residual_gate[0] * present.astype(FULL)

    each = lambda array: (array, rows_of(block, array.shape[1]))
    out_rows = lambda columns, kind: ((count, columns), kind, rows_of(block, columns))
    out_heads = ((heads, count), FULL, pl.BlockSpec((heads, block), lambda i: (0, i)))

    projected, self_mixed, self_logs, first, cross_queries = call(
        self_forward,
        "self_forward",
        steps,
        [each(tokens), each(hot), each(self_far), each(gate), w_self_in, w_self_out, bias_columns,
         w_query],
        [out_rows(3 * d, LOW), out_rows(d, FULL), out_heads, out_rows(d, FULL), out_rows(d, LOW)],
        [pltpu.VMEM((pairs, count, 2 * LANES), LOW), pltpu.VMEM((count, d), LOW),
         pltpu.VMEM((8, d), FULL)],
        flops=15 << 30, moved=8 << 20,
    )
    memory_kv, cross_mixed, cross_logs, second = call(
        cross_forward,
        "cross_forward",
        steps,
        [each(cross_queries), all_of(memory), each(hot), all_of(memory_far), each(gate),
         each(first), w_kv, w_cross_out, bias_columns],
        [out_all((key_count, 2 * d), LOW), out_rows(d, FULL), out_heads, out_rows(d, FULL)],
        [pltpu.VMEM((pairs, key_count, 2 * LANES), LOW), pltpu.VMEM((8, d), FULL)],
        flops=20 << 30, moved=8 << 20,
    )
    output, second_grad, cross_signal, cross_mixed_grad, cross_deltas, feed_grad, feed_sums = call(
        feed_both,
        "feed_both",
        steps,
        [each(second), each(out_cotangent), each(gate), each(cross_mixed), w_feed_in, w_feed_out,
         w_cross_out, bias_columns],
        [out_rows(d, LOW), out_rows(d, FULL), out_rows(d, LOW), out_rows(d, LOW), out_heads,
         out_all((d, 2 * ff + 2 * LANES), LOW), out_all((8, d), FULL)],
        [pltpu.VMEM((count, d), LOW), pltpu.VMEM((count, d), LOW), pltpu.VMEM((count, ff), LOW),
         pltpu.VMEM((count, ff), LOW), pltpu.VMEM((8, d), FULL), pltpu.VMEM((1, ff), FULL),
         pltpu.VMEM((1, ff), FULL)],
        flops=25 << 30, moved=16 << 20,
    )
    feed_total = lax.psum_scatter(feed_grad, "dp", scatter_dimension=0, tiled=True)
    feed_total = lax.psum_scatter(feed_total, "fsdp", scatter_dimension=0, tiled=True)

    cross_parts = []
    for pair in range(pairs):
        cross_parts += back_of_pair(
            cross_queries, memory_kv, memory_kv, hot, memory_far, cross_mixed_grad, cross_logs,
            cross_deltas, pair, False, (0, 0, pairs),
        )

    def owned(columns):
        if halving:
            return [out_all((device_count // 2, own, columns), LOW)] * 2
        return [out_all((d, columns), LOW)]

    cross_columns = 5 * d + LANES
    *cross_owned, first_grad, self_mixed_grad, self_deltas = call(
        functools.partial(cross_joined, pairs=pairs),
        "cross_joined",
        1,
        [all_of(part) for part in cross_parts]
        + [all_of(first), all_of(second_grad), all_of(memory), all_of(cross_signal),
           all_of(cross_mixed), all_of(self_mixed), all_of(gate), w_query, w_self_out,
           all_of(feed_sums)],
        owned(cross_columns)
        + [out_all((count, d), FULL), out_all((count, d), LOW), out_all((heads, count), FULL)],
        [pltpu.VMEM((d, cross_columns), LOW)],
        flops=8 << 30, moved=16 << 20, scalars=(bits,),
    )
    if halving:
        cross_sum = Halving("cross_sum", bits, *cross_owned, 11 * LANES, device_count)

    self_parts = []
    for pair in range(pairs):
        after = ()
        if halving and pair:
            after = tuple(cross_sum.got)
            cross_sum.step(pair, self_parts[-1:])
        self_parts += back_of_pair(
            projected, projected, projected, hot, self_far, self_mixed_grad, self_logs,
            self_deltas, pair, True, (0, pairs, 2 * pairs), after,
        )
    after = ()
    if halving:
        after = tuple(cross_sum.got)
        cross_sum.step(4, self_parts[-1:])
    self_columns = 3 * d + LANES
    *self_owned, self_signal = call(
        functools.partial(self_joined, pairs=pairs),
        "self_joined",
        1,
        [all_of(part) for part in self_parts] + [all_of(tokens)],
        owned(self_columns) + [out_all((count, 3 * d), LOW)],
        [pltpu.VMEM((d, self_columns), LOW)],
        flops=2 << 30, moved=8 << 20, scalars=(bits,), after=after,
    )
    if halving:
        self_sum = Halving("self_sum", bits, *self_owned, 6 * LANES, device_count)
        ends = [(cross_sum.kept[0], cross_sum.got[0])]
        for number in range(1, 5):
            self_sum.step(number)
        ends.append((self_sum.kept[0], self_sum.got[0]))
    else:
        ends = []
        for grads in (cross_owned[0], self_owned[0]):
            total = scatter_rows(grads, device_count)
            ends.append((total, jnp.zeros_like(total)))
    tokens_grad, memory_grad = call(
        functools.partial(last_grads, pairs=pairs),
        "last_grads",
        1,
        [all_of(part) for index, part in enumerate(cross_parts) if index % 3]
        + [all_of(self_signal), all_of(first_grad), w_self_in, w_kv],
        [out_all((count, d), FULL), out_all((key_count, d), FULL)],
        flops=3 << 30, moved=12 << 20,
    )
    kv_grad, query_grad, cross_out_grad, self_out_grad, cross_bias_grad, third = call(
        cross_last, "cross_last", 1, [all_of(array) for array in ends[0]],
        [out_all((own, 2 * d), FULL), out_all((own, d), FULL), out_all((own, d), FULL),
         out_all((own, d), FULL), out_all((3, own), FULL), out_all((1, own), FULL)],
    )
    feed_in_grad, feed_out_grad, bias_out_grad, bias_in_grad = call(
        feed_last, "feed_last", 1, [all_of(feed_total)],
        [out_all((own, ff), FULL), out_all((own, ff), FULL), out_all((1, own), FULL),
         out_all((own, LANES), FULL)],
    )
    self_in_grad, self_bias_grad = call(
        self_last, "self_last", 1, [all_of(array) for array in (*ends[1], third)],
        [out_all((own, 3 * d), FULL), out_all((3, own), FULL)],
    )
    return (
        output,
        tokens_grad,
        memory_grad,
        self_in_grad,
        self_out_grad.T,
        self_bias_grad,
        query_grad,
        kv_grad,
        cross_out_grad.T,
        cross_bias_grad,
        feed_in_grad,
        feed_out_grad.T,
        bias_in_grad[:, : ff // d].reshape(feed_bias_in.shape),
        bias_out_grad[0],
    )


def solution(mesh):
    return jax.shard_map(
        on_device,
        mesh=mesh,
        in_specs=(
            P(("dp", "fsdp"), None),
            P(("dp", "fsdp"), None),
            P(("dp", "fsdp"), None),
            P(("dp", "fsdp"), None),
            P(("dp", "fsdp"), None),
            P(),
            P(("dp", "fsdp"), None),
            P(None, ("dp", "fsdp")),
            P(None, ("dp", "fsdp")),
            P(("dp", "fsdp"), None),
            P(("dp", "fsdp"), None),
            P(None, ("dp", "fsdp")),
            P(None, ("dp", "fsdp")),
            P(("dp", "fsdp"), None),
            P(None, ("dp", "fsdp")),
            P(("dp", "fsdp")),
            P(("dp", "fsdp")),
        ),
        out_specs=(
            P(("dp", "fsdp"), None),
            P(("dp", "fsdp"), None),
            P(("dp", "fsdp"), None),
            P(("dp", "fsdp"), None),
            P(None, ("dp", "fsdp")),
            P(None, ("dp", "fsdp")),
            P(("dp", "fsdp"), None),
            P(("dp", "fsdp"), None),
            P(None, ("dp", "fsdp")),
            P(None, ("dp", "fsdp")),
            P(("dp", "fsdp"), None),
            P(None, ("dp", "fsdp")),
            P(("dp", "fsdp")),
            P(("dp", "fsdp")),
        ),
        check_vma=False,
    )
```

```python
import functools

import jax
import jax.numpy as jnp
from jax import lax
from jax.experimental import pallas as pl
from jax.experimental.pallas import tpu as pltpu
from jax.sharding import PartitionSpec as P

HEAD = 64
LANES = 128
FAR = -1e30
AXES = ("dp", "fsdp")
LOW = jnp.bfloat16
FULL = jnp.float32
ROOM = 56 << 20


def nn(left, right):
    return lax.dot_general(left, right, (((1,), (0,)), ((), ())), preferred_element_type=FULL)


def nt(left, right):
    return lax.dot_general(left, right, (((1,), (1,)), ((), ())), preferred_element_type=FULL)


def tn(left, right):
    return lax.dot_general(left, right, (((0,), (0,)), ((), ())), preferred_element_type=FULL)


def one_head(pair, odd):
    lane = lax.broadcasted_iota(jnp.int32, pair.shape, 1)
    return jnp.where((lane >= HEAD) == bool(odd), pair, jnp.zeros_like(pair))


def later_keys(rows, keys):
    query = lax.broadcasted_iota(jnp.int32, (rows, keys), 0)
    key = lax.broadcasted_iota(jnp.int32, (rows, keys), 1)
    return query, key


def call(body, name, grid, ins, outs, scratch=(), flops=0, moved=0, after=(), scalars=()):
    used = len(ins)

    def only_used(*refs):
        front = len(scalars)
        body(*refs[: front + used], *refs[front + used + len(after) :])

    def spec_of(spec):
        if not scalars or spec.index_map is None:
            return spec
        place = spec.index_map
        return pl.BlockSpec(
            spec.block_shape, lambda i, *_: place(i), pipeline_mode=spec.pipeline_mode
        )

    return pl.pallas_call(
        only_used if after else body,
        name=name,
        grid_spec=pltpu.PrefetchScalarGridSpec(
            num_scalar_prefetch=len(scalars),
            grid=(grid,),
            in_specs=[spec_of(spec) for _, spec in ins]
            + [pl.BlockSpec(memory_space=pl.ANY) for _ in after],
            out_specs=[spec_of(spec) for _, _, spec in outs],
            scratch_shapes=list(scratch),
        ),
        out_shape=[jax.ShapeDtypeStruct(shape, kind) for shape, kind, _ in outs],
        compiler_params=pltpu.CompilerParams(vmem_limit_bytes=ROOM),
        cost_estimate=pl.CostEstimate(flops=flops, bytes_accessed=moved, transcendentals=0),
    )(*scalars, *[array for array, _ in ins], *after)


def rows_of(block, columns):
    return pl.BlockSpec((block, columns), lambda i: (i, 0))


def fixed(shape, place=None):
    place = (0,) * len(shape) if place is None else place
    return pl.BlockSpec(shape, lambda i: place, pipeline_mode=pl.Buffered(1))


def all_of(array):
    return (array, fixed(array.shape))


def out_all(shape, kind):
    return (shape, kind, fixed(shape))


def attend(queries, hot, keys_ref, values_ref, count, causal):
    rows = queries.shape[0]
    heads = queries.shape[1] // HEAD
    lane = lax.broadcasted_iota(jnp.int32, (rows, LANES), 1)
    logs = jnp.zeros((rows, LANES), FULL)
    if causal:
        query, key = later_keys(rows, rows)
        ahead = jnp.where(key <= query, 0.0, FAR)

    def scores_of(head):
        columns = slice(head // 2 * LANES, (head // 2 + 1) * LANES)
        asked = jnp.concatenate([one_head(queries[:, columns], head % 2), hot], axis=1)
        scores = nt(asked, keys_ref[head // 2, :count, :])
        if not causal:
            return scores
        if count == rows:
            return scores + ahead
        return jnp.concatenate(
            [scores[:, : count - rows], scores[:, count - rows :] + ahead], axis=1
        )

    mixed = []
    following = scores_of(0)
    for head in range(heads):
        scores = following
        if head + 1 < heads:
            following = scores_of(head + 1)
        columns = slice(head // 2 * LANES, (head // 2 + 1) * LANES)
        top = jnp.max(scores, axis=1, keepdims=True)
        weights = jnp.exp(scores - top)
        amount = jnp.sum(weights, axis=1, keepdims=True)
        low = (weights * (1.0 / amount)).astype(LOW)
        here = nn(low, values_ref[:count, columns])
        if head % 2:
            mixed.append(jnp.where(lane < HEAD, other, here))
        other = here
        logs = jnp.where(lane == head, top + jnp.log(amount), logs)
    return jnp.concatenate(mixed, axis=1), logs.T[:heads]


def keep_keys(keys_ref, place, keys, hot):
    pairs = keys.shape[1] // LANES
    for pair in range(pairs):
        keys_ref[pair, place, :LANES] = keys[:, pair * LANES : (pair + 1) * LANES]
        keys_ref[pair, place, LANES:] = hot


def self_forward(
    tokens, hot, far, gate, w_in, w_out, bias_columns, w_query,
    projected, mixed, logs, first, first_low, cross_queries, keys, values, bias,
):
    step = pl.program_id(0)
    rows, d = tokens.shape

    @pl.when(step == 0)
    def _():
        bias[...] = bias_columns[:, :LANES].astype(FULL).T[:8]

    joined_bias = jnp.concatenate([bias[0:1, :], jnp.zeros((1, d), FULL), bias[1:2, :]], axis=1)
    made = (nn(tokens[...], w_in[...]) + joined_bias).astype(LOW)
    projected[...] = made
    place = pl.ds(pl.multiple_of(step * rows, rows), rows)
    keep_keys(keys, place, made[:, d : 2 * d], far[...])
    values[place, :] = made[:, 2 * d :]
    for block in range(values.shape[0] // rows):

        @pl.when(step == block)
        def _(count=(block + 1) * rows):
            scaled = made[:, :d] * jnp.asarray(HEAD**-0.5, LOW)
            mixed[...], logs[...] = attend(scaled, hot[...], keys, values, count, True)

    branch = nt(mixed[...].astype(LOW), w_out[...]) + bias[2:3, :]
    total = tokens[...].astype(FULL) + gate[...] * branch
    first[...] = total
    first_low[...] = total.astype(LOW)
    cross_queries[...] = (nn(total.astype(LOW), w_query[...]) + bias[3:4, :]).astype(LOW)


def cross_forward(
    queries, memory, hot, far, gate, first, w_kv, w_out, bias_columns,
    memory_kv, mixed, logs, second, keys, bias,
):
    d = memory.shape[1]

    @pl.when(pl.program_id(0) == 0)
    def _():
        bias[...] = bias_columns[:, :LANES].astype(FULL).T[:8]
        made = nn(memory[...], w_kv[...])
        memory_kv[:, :d] = made[:, :d].astype(LOW)
        memory_kv[:, d:] = (made[:, d:] + bias[4:5, :]).astype(LOW)
        keep_keys(keys, slice(None), memory_kv[:, :d], far[...])

    scaled = queries[...] * jnp.asarray(HEAD**-0.5, LOW)
    mixed[...], logs[...] = attend(
        scaled, hot[...], keys, memory_kv.at[:, d:], memory.shape[0], False
    )
    branch = nt(mixed[...].astype(LOW), w_out[...]) + bias[5:6, :]
    second[...] = first[...] + gate[...] * branch


def head_sums(left, right):
    d = left.shape[1]
    head = lax.broadcasted_iota(jnp.int32, (d // HEAD, d), 0)
    column = lax.broadcasted_iota(jnp.int32, (d // HEAD, d), 1)
    chosen = (column // HEAD == head).astype(FULL)
    return lax.dot_general(
        chosen,
        left.astype(FULL) * right.astype(FULL),
        (((1,), (1,)), ((), ())),
        precision=lax.Precision.HIGHEST,
        preferred_element_type=FULL,
    )


def gelu_both(z):
    c = 0.7978845608028654
    square = z * z
    bent = jnp.tanh(c * z * (1.0 + 0.044715 * square))
    half = 0.5 * (1.0 + bent)
    slope = half + 0.5 * z * (1.0 - bent * bent) * (c * (1.0 + 3.0 * 0.044715 * square))
    return z * half, slope


def spread(d, ff):
    each = ff // d
    row = lax.broadcasted_iota(jnp.int32, (d, ff), 0)
    entry = lax.broadcasted_iota(jnp.int32, (d, ff), 1)
    column = lax.broadcasted_iota(jnp.int32, (LANES, ff), 0)
    there = lax.broadcasted_iota(jnp.int32, (LANES, ff), 1)
    return entry // each == row, (there % each == column).astype(LOW)


def columns_to_row(columns, ff):
    owner, place = spread(columns.shape[0], ff)
    return jnp.sum(jnp.where(owner, nn(columns, place), 0.0), axis=0, keepdims=True)


def row_to_columns(row, d):
    owner, place = spread(d, row.shape[1])
    return nt(jnp.where(owner, row, 0.0).astype(LOW), place).astype(LOW)


def rows_to_columns(*rows):
    d = rows[0].shape[1]
    stack = jnp.concatenate([*rows, jnp.zeros((LANES - len(rows), d), FULL)], axis=0)
    return stack.T.astype(LOW)


def feed_both(
    second, upstream, gate, mixed, w_in, w_out, w_cross_out, bias_columns,
    output, second_grad, mixed_grad, deltas, feed_grad, sums,
    second_low, signal_all, hidden_all, before_all, cross_all, mixed_all, bias, bias_in, bias_in_grad,
    *, inner, own,
):
    step = pl.program_id(0)
    rows, d = second.shape
    ff = w_in.shape[1]
    place = pl.ds(pl.multiple_of(step * rows, rows), rows)
    low = second[...].astype(LOW)
    second_low[place, :] = low
    mixed_all[place, :] = mixed[...].astype(LOW)
    given = upstream[...].astype(FULL)
    signal = (gate[...] * given).astype(LOW)
    signal_all[place, :] = signal

    @pl.when(step == 0)
    def _():
        bias[...] = bias_columns[:, :LANES].astype(FULL).T[:8]
        bias_in[...] = columns_to_row(bias_columns[:, LANES:], ff)
        bias_in_grad[...] = jnp.zeros_like(bias_in_grad)
        sums[...] = jnp.zeros_like(sums)

    made = bias[6:7, :]
    back = given
    width = 1024
    parts = [slice(start, start + width) for start in range(0, ff, width)]
    products = lambda part: (nn(low, w_in[:, part]) + bias_in[:, part], nn(signal, w_out[:, part]))
    following = products(parts[0])
    for index, part in enumerate(parts):
        before, hidden_back = following
        if index + 1 < len(parts):
            following = products(parts[index + 1])
        hidden, slope = gelu_both(before)
        hidden = hidden.astype(LOW)
        hidden_all[place, part] = hidden
        before_grad = (hidden_back * slope).astype(LOW)
        before_all[place, part] = before_grad
        bias_in_grad[:, part] += column_sum(before_grad)
        made = made + nt(hidden, w_out[:, part])
        back = back + nt(before_grad, w_in[:, part])
    output[...] = (second[...] + gate[...] * made).astype(LOW)
    second_grad[...] = back
    crossed = (gate[...] * back).astype(LOW)
    cross_all[place, :] = crossed
    mixed_back = nn(crossed, w_cross_out[...]).astype(LOW)
    mixed_grad[...] = mixed_back
    deltas[...] = head_sums(mixed_back, mixed[...])
    sums[0:1, :] += column_sum(signal)
    sums[1:2, :] += column_sum(crossed)

    @pl.when(step == pl.num_programs(0) - 1)
    def _():
        def keep(start, grad):
            end = start + grad.shape[1]
            outer = d // own // inner
            for owner in range(inner * outer if inner > 1 else 0):
                to = (owner % inner * outer + owner // inner) * own
                feed_grad[to : to + own, start:end] = grad[owner * own : (owner + 1) * own]
            if inner == 1:
                feed_grad[:, start:end] = grad

        for part in parts:
            keep(part.start, tn(second_low[...], before_all[:, part]).astype(LOW))
            keep(ff + part.start, tn(signal_all[...], hidden_all[:, part]).astype(LOW))
        keep(2 * ff, tn(cross_all[...], mixed_all[...]).astype(LOW))
        at = 2 * ff + d
        keep(at, rows_to_columns(sums[0:1, :]))
        keep(at + LANES, row_to_columns(bias_in_grad[...], d))


def column_sum(array):
    return jnp.sum(array.astype(FULL), axis=0, keepdims=True)


def attend_back(
    queries, keys, values, hot, far, mixed_grad, logs, deltas, pair,
    query_grad, key_grad, value_grad, key_sum, value_sum, reached, causal, block=256,
):
    count = keys.shape[0]
    reached[:, :LANES] = keys[...]
    reached[:, LANES:] = far[...]
    turned = keys[...].T
    if causal:
        key, query = later_keys(block, block)
        ahead = jnp.where(key <= query, 0.0, FAR)
    items = [
        (start, odd) for start in range(queries.shape[0] - block, -1, -block) for odd in range(2)
    ]

    def products(item):
        start, odd = item
        place = slice(start, start + block)
        reach = start + block if causal else count
        asked = one_head(queries[place, :], odd) * jnp.asarray(HEAD**-0.5, LOW)
        incoming = one_head(mixed_grad[place, :], odd)
        scores = nt(reached[:reach, :], jnp.concatenate([asked, hot[place, :]], axis=1))
        if causal and start:
            scores = jnp.concatenate([scores[:start], scores[start:] + ahead], axis=0)
        elif causal:
            scores = scores + ahead
        return scores, nt(values[:reach, :], incoming), asked, incoming, place, reach

    following = products(items[0])
    for index, (start, odd) in enumerate(items):
        scores, pushed, asked, incoming, place, reach = following
        if index + 1 < len(items):
            following = products(items[index + 1])
        head = pl.ds(2 * pair + odd, 1)
        chances = jnp.exp(scores - logs[head, place])
        score_grad = (chances * (pushed - deltas[head, place])).astype(LOW)
        turned_grad = nn(turned[odd * HEAD : (odd + 1) * HEAD, :reach], score_grad)
        value_part = nn(chances.astype(LOW), incoming)
        key_part = nn(score_grad, asked)
        if index == 0:
            value_sum[...] = value_part
            key_sum[...] = key_part
        else:
            value_sum[:reach, :] += value_part
            key_sum[:reach, :] += key_part
        if odd:
            both = jnp.concatenate([other, turned_grad], axis=0) * HEAD**-0.5
            query_grad[place, :] = both.T.astype(LOW)
        other = turned_grad
    key_grad[...] = key_sum[...].astype(LOW)
    value_grad[...] = value_sum[...].astype(LOW)


def cross_back(
    bits, queries, keys, values, hot, far, in_grad, logs, cross_deltas, sums,
    first, second_grad, memory, self_mixed, gate, weights, self_weights,
    *outs,
):
    (
        *owned, key_grad, value_grad, first_grad, mixed_grad, deltas,
        key_sum, value_sum, reached, signals, first_here, second_here, memory_here, mixed_here,
        w_query, w_out, grads, arrived,
    ) = outs
    pair = pl.program_id(0)
    d = memory.shape[1]
    copies = [
        pltpu.make_async_copy(source, target, arrived.at[index])
        for index, (source, target) in enumerate(
            [
                (first, first_here), (second_grad, second_here), (memory, memory_here),
                (self_mixed, mixed_here), (weights.at[:, 2 * d : 3 * d], w_query),
                (self_weights.at[:, 3 * d : 4 * d], w_out),
            ]
        )
    ]

    @pl.when(pair == 0)
    def _():
        for copy in copies:
            copy.start()

    attend_back(
        queries, keys, values, hot, far, in_grad, logs, cross_deltas, pair,
        signals.at[0, pair], signals.at[1, pair], signals.at[2, pair],
        key_sum, value_sum, reached, False,
    )
    key_grad[...] = signals[1, pair]
    value_grad[...] = signals[2, pair]

    @pl.when(pair == pl.num_programs(0) - 1)
    def _():
        for copy in copies:
            copy.wait()
        pairs = signals.shape[1]
        query_signal, key_signal, value_signal = (
            jnp.concatenate([signals[which, place] for place in range(pairs)], axis=1)
            for which in range(3)
        )
        back = second_here[...] + nt(query_signal, w_query[...])
        first_grad[...] = back
        signal = (gate[...] * back).astype(LOW)
        mixed_back = nn(signal, w_out[...]).astype(LOW)
        mixed_grad[...] = mixed_back
        deltas[...] = head_sums(mixed_back, mixed_here[...])
        grads[:, :d] = tn(memory_here[...], key_signal).astype(LOW)
        grads[:, d : 2 * d] = tn(memory_here[...], value_signal).astype(LOW)
        grads[:, 2 * d : 3 * d] = tn(first_here[...], query_signal).astype(LOW)
        grads[:, 3 * d : 4 * d] = tn(signal, mixed_here[...].astype(LOW)).astype(LOW)
        grads[:, 4 * d :] = rows_to_columns(
            column_sum(query_signal), column_sum(value_signal), sums[1:2, :], column_sum(signal)
        )
        if len(owned) == 2:
            part_by_core(bits, grads, *owned)
        else:
            owned[0][...] = grads[...]


def self_back(
    bits, queries, keys, values, hot, far, in_grad, logs, deltas, tokens, *rest, before, ending
):
    if ending:
        earlier, earlier_sums, *rest = rest
    *owned, query_grad, key_grad, value_grad, key_sum, value_sum, reached, signals, grads = rest
    step = pl.program_id(0)
    pairs = signals.shape[1]
    wide = pairs * LANES
    attend_back(
        queries, keys, values, hot, far, in_grad, logs, deltas, before + step,
        signals.at[0, step], signals.at[1, step], signals.at[2, step],
        key_sum, value_sum, reached, True,
    )
    query_grad[...] = signals[0, step]
    key_grad[...] = signals[1, step]
    value_grad[...] = signals[2, step]

    @pl.when(step == pl.num_programs(0) - 1)
    def _():
        at = 3 * wide if ending else 0
        if ending:
            grads[:, :at] = earlier[...]
        added = []
        for which in range(3):
            part = jnp.concatenate([signals[which, place] for place in range(pairs)], axis=1)
            grads[:, at + which * wide : at + (which + 1) * wide] = tn(
                tokens[...], part
            ).astype(LOW)
            if which != 1:
                added.append(column_sum(part))
        if not ending:
            owned[0][...] = grads[...]
            owned[1][0:1, :] = added[0]
            owned[1][1:2, :] = added[1]
            return
        grads[:, 2 * at :] = rows_to_columns(
            *[
                jnp.concatenate([earlier_sums[row : row + 1, :], added[row]], axis=1)
                for row in range(2)
            ]
        )
        if len(owned) == 2:
            part_by_core(bits, grads, *owned)
        else:
            owned[0][...] = grads[...]


def part_by_core(bits, grads, keep, away):
    own = keep.shape[1]
    for core in range(2):

        @pl.when(bits[0] == core)
        def _(core=core):
            for slab in range(2 * keep.shape[0]):
                there = keep if slab % 2 == core else away
                there[slab // 2] = grads[slab * own : (slab + 1) * own, :]


def memory_back(key_signal, value_signal, w_kv, memory_grad):
    d = key_signal.shape[1]
    memory_grad[...] = nt(key_signal[...], w_kv[:, :d]) + nt(value_signal[...], w_kv[:, d:])


def tokens_back(first_grad, w_in, *refs):
    *signals, tokens_grad = refs
    d = first_grad.shape[1]
    total = first_grad[...]
    wide = signals[0].shape[1]
    for index, signal in enumerate(signals):
        start = index % 3 * d + index // 3 * wide
        total = total + nt(signal[...], w_in[:, start : start + wide])
    tokens_grad[...] = total


def sum_to_owners(grads, device_count, orders):
    me = lax.axis_index(AXES)
    bits = device_count.bit_length() - 1
    running = []
    for grad in grads:
        rows, columns = grad.shape
        running.append(grad.reshape((2,) * bits + (rows // device_count, columns)))
    left = [list(range(bits)) for _ in grads]
    for step in range(bits):
        sent = []
        for part, order in enumerate(orders):
            bit = order[step]
            axis = len(left[part]) - 1 - left[part].index(bit)
            mine = (me >> bit) & 1
            away = lax.dynamic_index_in_dim(running[part], 1 - mine, axis, keepdims=False)
            pairs = [(i, i ^ (1 << bit)) for i in range(device_count)]
            sent.append((axis, mine, lax.ppermute(away.astype(LOW), AXES, pairs)))
            left[part].remove(bit)
        for part, (axis, mine, got) in enumerate(sent):
            kept = lax.dynamic_index_in_dim(running[part], mine, axis, keepdims=False)
            running[part] = kept.astype(FULL) + got.astype(FULL)
    return running


def swap(array, bit, device_count):
    return lax.ppermute(array, AXES, [(i, i ^ (1 << bit)) for i in range(device_count)])


def scatter_rows(grad, device_count):
    bits = device_count.bit_length() - 1
    high = list(range(1, bits))[::-1]
    half = grad.shape[1] // 256 * 128
    orders = ([0] + high, [0, high[1], high[0]] + high[2:])
    return jnp.concatenate(
        sum_to_owners([grad[:, :half], grad[:, half:]], device_count, orders), axis=1
    )


def swap(array, change, device_count):
    return lax.ppermute(array, AXES, [(i, i ^ change) for i in range(device_count)])


def picked(terms, first, second):
    total = None
    for term in terms:
        for place in (first, second):
            term = lax.dynamic_index_in_dim(term, place, 0, keepdims=False)
        total = term.astype(FULL) if total is None else total + term.astype(FULL)
    return total


class Halving:
    def __init__(self, me, keep, away, device_count):
        self.count = device_count
        self.x, self.y = (me >> 3) & 1, (me >> 4) & 1
        self.low, self.high = (me >> 1) & 1, (me >> 2) & 1
        shape = (2, 2, 4, *keep.shape[1:])
        self.terms = [keep.reshape(shape)]
        self.got = [swap(away.reshape(shape), 1, device_count)]

    def plane(self):
        terms = self.terms + self.got
        changes = ((0, 1), (1, 0), (1, 1))
        self.sent = [picked(terms, self.y ^ y, self.x ^ x).astype(LOW) for y, x in changes]
        self.got = [
            swap(array, 8 * x + 16 * y, self.count) for array, (y, x) in zip(self.sent, changes)
        ]
        self.terms = [
            lax.dynamic_index_in_dim(
                lax.dynamic_index_in_dim(term, self.y, 0, keepdims=False), self.x, 0, keepdims=False
            )
            for term in terms
        ]

    def line(self):
        terms = [term.reshape(2, 2, *term.shape[1:]) for term in self.terms + self.got]
        changes = ((0, 1), (1, 0), (1, 1))
        self.sent = [
            picked(terms, self.high ^ high, self.low ^ low).astype(LOW) for high, low in changes
        ]
        self.got = [
            swap(array, 2 * low + 4 * high, self.count)
            for array, (high, low) in zip(self.sent, changes)
        ]
        self.kept = picked(terms, self.high, self.low)

    def wait_for(self, *arrays):
        self.got = list(lax.optimization_barrier((*self.got, *arrays))[: len(self.got)])


def total_of(keep, *got):
    total = keep[...]
    for part in got:
        total = total + part[...].astype(FULL)
    return total


def cross_last(*refs):
    *parts, kv, query, self_out, cross_bias, self_bias = refs
    total = total_of(*parts)
    d = query.shape[1]
    kv[...] = total[:, : 2 * d]
    query[...] = total[:, 2 * d : 3 * d]
    self_out[...] = total[:, 3 * d : 4 * d]
    turned = turned_bias(total[:, 4 * d :])
    cross_bias[...] = turned[0:3]
    self_bias[...] = turned[3:4]


def turned_bias(columns):
    own = columns.shape[0]
    square = jnp.concatenate([columns, jnp.zeros((LANES - own, LANES), FULL)], axis=0)
    return square.T[:8, :own]


def self_last(third, *refs):
    *parts, self_in, bias = refs
    total = total_of(*parts)
    columns = self_in.shape[1]
    half = columns // 2
    wide = half // 3
    for call_index in range(2):
        for which in range(3):
            at = call_index * half + which * wide
            to = which * 2 * wide + call_index * wide
            self_in[:, to : to + wide] = total[:, at : at + wide]
    bias[0:2, :] = turned_bias(total[:, columns:])[0:2]
    bias[2:3, :] = third[...]


def feed_last(total, feed_in, feed_out, cross_out, bias_out, bias_in):
    ff = feed_in.shape[1]
    at = 2 * ff + cross_out.shape[1]
    feed_in[...] = total[:, :ff].astype(FULL)
    feed_out[...] = total[:, ff : 2 * ff].astype(FULL)
    cross_out[...] = total[:, 2 * ff : at].astype(FULL)
    bias_out[...] = turned_bias(total[:, at : at + LANES].astype(FULL))[0:1]
    bias_in[...] = columns_to_row(total[:, at + LANES :], bias_in.shape[1])


def pack(
    self_in, self_out, cross_query, cross_kv, cross_out, feed_in, feed_out, self_bias, cross_bias,
    bias_out, bias_in, near, own_feed,
):
    d = self_out.shape[1]
    ff = feed_in.shape[1]
    own = self_in.shape[0]
    near[:, : 3 * d] = self_in[...].astype(LOW)
    near[:, 3 * d : 4 * d] = self_out[...].astype(LOW)
    rows = jnp.concatenate(
        [self_bias[...], cross_bias[...], bias_out[...], jnp.zeros((LANES - 7, own), FULL)], axis=0
    )
    wide = jnp.concatenate([rows, jnp.zeros((LANES, LANES - own), FULL)], axis=1)
    at = 4 * d + LANES
    near[:, 4 * d : at] = wide.T[:own].astype(LOW)
    near[:, at : at + LANES] = row_to_columns(bias_in[...], own)
    at += LANES
    near[:, at : at + 2 * d] = cross_kv[...].astype(LOW)
    near[:, at + 2 * d : at + 3 * d] = cross_query[...].astype(LOW)
    near[:, at + 3 * d :] = cross_out[...].astype(LOW)
    own_feed[:, :ff] = feed_in[...].astype(LOW)
    own_feed[:, ff:] = feed_out[...].astype(LOW)


def marks(seq_lengths, memory_lengths, residual_gate, hot, self_far, memory_far, gate):
    slots = seq_lengths.shape[0]
    lane = lax.broadcasted_iota(jnp.int32, hot.shape, 1)

    def numbered(lengths, padding):
        position = lax.broadcasted_iota(jnp.int32, hot.shape, 0)
        end = lengths[0]
        number = jnp.where(position >= end, 1, 0)
        for slot in range(1, slots):
            end = end + lengths[slot]
            number = number + jnp.where(position >= end, 1, 0)
        present = position < end
        return jnp.where(present, number, padding), present

    ids, present = numbered(seq_lengths, slots)
    hot[...] = jnp.where(ids == lane, 1.0, 0.0).astype(LOW)
    self_far[...] = jnp.where(ids == lane, 0.0, FAR).astype(LOW)
    gate[...] = jnp.where(present[:, :1], residual_gate[0], 0.0)
    ids, _ = numbered(memory_lengths, slots + 1)
    memory_far[...] = jnp.where(ids == lane, 0.0, FAR).astype(LOW)


def gather_near(near, cut, device_count):
    me = lax.axis_index(AXES)
    others = [swap(near, 2 * change, device_count) for change in (1, 2, 3)]
    first, second, third, fourth = near, *others
    odd = jnp.where(
        (me >> 1) & 1,
        jnp.stack([second, first, fourth, third]),
        jnp.stack([first, second, third, fourth]),
    )
    line = jnp.where((me >> 2) & 1, jnp.concatenate([odd[2:], odd[:2]]), odd)
    held = [line[..., :cut], line[..., cut:]]
    known = [[1, 1], [1, 1]]
    for bits in ((3, 4), (4, 3), (0, 0)):
        got = [swap(array, 1 << bit, device_count) for array, bit in zip(held, bits)]
        for part, bit in enumerate(bits):
            mine, theirs = held[part], got[part]
            if bit == 0:
                axis = mine.ndim - 2
            else:
                axis = sum(other > bit for other in known[part])
            low = jnp.stack([mine, theirs], axis)
            high = jnp.stack([theirs, mine], axis)
            held[part] = jnp.where((me >> bit) & 1, high, low)
            known[part].append(bit)
    return [array.reshape(-1, array.shape[-1]) for array in held]


def on_device(
    tokens, memory, out_cotangent, seq_lengths, memory_lengths, residual_gate,
    self_in, self_out, self_bias, cross_query, cross_key_value, cross_out, cross_bias,
    feed_in, feed_out, feed_bias_in, feed_bias_out,
):
    device_count = lax.axis_size(AXES)
    count, d = tokens.shape
    key_count = memory.shape[0]
    ff = feed_in.shape[1]
    own = self_in.shape[0]
    pairs = d // LANES
    heads = d // HEAD
    block = 256
    steps = count // block
    halving = lax.axis_size("dp") == 4 and lax.axis_size("fsdp") == 8
    me = lax.axis_index(AXES)
    bits = (me & 1).astype(jnp.int32)[None]
    cut = 4 * d + 2 * LANES
    near, own_feed = call(
        pack,
        "pack",
        1,
        [
            all_of(array)
            for array in (
                self_in, self_out.T, cross_query, cross_key_value, cross_out.T, feed_in,
                feed_out.T, self_bias, cross_bias, feed_bias_out[None], feed_bias_in[None],
            )
        ],
        [out_all((own, cut + 4 * d), LOW), out_all((own, 2 * ff), LOW)],
    )
    feed_whole = lax.all_gather(own_feed, AXES, axis=0, tiled=True)
    if halving:
        self_whole, cross_whole = gather_near(near, cut, device_count)
    else:
        self_whole = lax.all_gather(near[:, :cut], AXES, axis=0, tiled=True)
        cross_whole = lax.all_gather(near[:, cut:], AXES, axis=0, tiled=True)
    hot, self_far, memory_far, gate = call(
        marks,
        "marks",
        1,
        [],
        [out_all((count, LANES), LOW), out_all((count, LANES), LOW),
         out_all((key_count, LANES), LOW), out_all((count, 1), FULL)],
        scalars=(seq_lengths[0], memory_lengths[0], residual_gate),
    )
    w_self_in = (self_whole, fixed((d, 3 * d), (0, 0)))
    w_self_out = (self_whole, fixed((d, d), (0, 3)))
    bias_columns = (self_whole, fixed((d, 2 * LANES), (0, 4 * d // (2 * LANES))))
    w_kv = (cross_whole, fixed((d, 2 * d), (0, 0)))
    w_query = (cross_whole, fixed((d, d), (0, 2)))
    w_cross_out = (cross_whole, fixed((d, d), (0, 3)))
    w_feed_in = (feed_whole, fixed((d, ff), (0, 0)))
    w_feed_out = (feed_whole, fixed((d, ff), (0, 1)))

    each = lambda array: (array, rows_of(block, array.shape[1]))
    out_rows = lambda columns, kind: ((count, columns), kind, rows_of(block, columns))
    out_heads = ((heads, count), FULL, pl.BlockSpec((heads, block), lambda i: (0, i)))

    projected, self_mixed, self_logs, first, first_low, cross_queries = call(
        self_forward,
        "self_forward",
        steps,
        [each(tokens), each(hot), each(self_far), each(gate), w_self_in, w_self_out, bias_columns,
         w_query],
        [out_rows(3 * d, LOW), out_rows(d, FULL), out_heads, out_rows(d, FULL), out_rows(d, LOW), out_rows(d, LOW)],
        [pltpu.VMEM((pairs, count, 2 * LANES), LOW), pltpu.VMEM((count, d), LOW),
         pltpu.VMEM((8, d), FULL)],
        flops=15 << 30, moved=8 << 20,
    )
    block = 512
    steps = count // block
    out_heads = ((heads, count), FULL, pl.BlockSpec((heads, block), lambda i: (0, i)))
    memory_kv, cross_mixed, cross_logs, second = call(
        cross_forward,
        "cross_forward",
        steps,
        [each(cross_queries), all_of(memory), each(hot), all_of(memory_far), each(gate),
         each(first), w_kv, w_cross_out, bias_columns],
        [out_all((key_count, 2 * d), LOW), out_rows(d, FULL), out_heads, out_rows(d, FULL)],
        [pltpu.VMEM((pairs, key_count, 2 * LANES), LOW), pltpu.VMEM((8, d), FULL)],
        flops=20 << 30, moved=8 << 20,
    )
    inner = lax.axis_size("fsdp") if halving else 1
    output, second_grad, cross_mixed_grad, cross_deltas, feed_grad, feed_sums = call(
        functools.partial(feed_both, inner=inner, own=own),
        "feed_both",
        steps,
        [each(second), each(out_cotangent), each(gate), each(cross_mixed), w_feed_in, w_feed_out,
         w_cross_out, bias_columns],
        [out_rows(d, LOW), out_rows(d, FULL), out_rows(d, LOW), out_heads,
         out_all((d, 2 * ff + d + 2 * LANES), LOW), out_all((8, d), FULL)],
        [pltpu.VMEM((count, d), LOW), pltpu.VMEM((count, d), LOW), pltpu.VMEM((count, ff), LOW),
         pltpu.VMEM((count, ff), LOW), pltpu.VMEM((count, d), LOW), pltpu.VMEM((count, d), LOW),
         pltpu.VMEM((8, d), FULL), pltpu.VMEM((1, ff), FULL), pltpu.VMEM((1, ff), FULL)],
        flops=25 << 30, moved=16 << 20,
    )
    ways = ("fsdp", "dp") if halving else ("dp", "fsdp")
    feed_total = lax.psum_scatter(feed_grad, ways[0], scatter_dimension=0, tiled=True)

    def pair_columns(array, start, width=LANES):
        return (array, pl.BlockSpec((array.shape[0], width), lambda i: (0, start + i)))

    def out_pairs(rows, columns):
        return ((rows, columns), LOW, pl.BlockSpec((rows, LANES), lambda i: (0, i)))

    def owned(columns):
        if halving:
            return [out_all((device_count // 2, own, columns), LOW)] * 2
        return [out_all((d, columns), LOW)]

    def pair_room(rows, steps):
        return [
            pltpu.VMEM((rows, LANES), FULL), pltpu.VMEM((rows, LANES), FULL),
            pltpu.VMEM((rows, 2 * LANES), LOW), pltpu.VMEM((3, steps, rows, LANES), LOW),
        ]

    left_there = lambda array: (array, pl.BlockSpec(memory_space=pl.ANY))
    cross_columns = 4 * d + LANES
    *cross_owned, key_signal, value_signal, first_grad, self_mixed_grad, self_deltas = call(
        cross_back,
        "cross_back",
        pairs,
        [pair_columns(cross_queries, 0), pair_columns(memory_kv, 0),
         pair_columns(memory_kv, pairs), all_of(hot), all_of(memory_far),
         pair_columns(cross_mixed_grad, 0), all_of(cross_logs), all_of(cross_deltas),
         all_of(feed_sums), left_there(first_low), left_there(second_grad), left_there(memory),
         left_there(self_mixed), all_of(gate), left_there(cross_whole), left_there(self_whole)],
        owned(cross_columns)
        + [out_pairs(key_count, d), out_pairs(key_count, d), out_all((count, d), FULL),
           out_all((count, d), LOW), out_all((heads, count), FULL)],
        pair_room(key_count, pairs)
        + [pltpu.VMEM((count, d), LOW), pltpu.VMEM((count, d), FULL),
           pltpu.VMEM((key_count, d), LOW), pltpu.VMEM((count, d), FULL),
           pltpu.VMEM((d, d), LOW), pltpu.VMEM((d, d), LOW),
           pltpu.VMEM((d, cross_columns), LOW), pltpu.SemaphoreType.DMA((6,))],
        flops=30 << 30, moved=24 << 20, scalars=(bits,),
    )
    if halving:
        cross_sum = Halving(me, *cross_owned, device_count)

    half = pairs // 2
    self_columns = 3 * d + LANES

    def self_part(before, ending, outs, earlier=(), after=()):
        wide = half * LANES
        columns = self_columns if ending else 3 * wide
        return call(
            functools.partial(self_back, before=before, ending=ending),
            "self_back",
            half,
            [pair_columns(projected, before), pair_columns(projected, pairs + before),
             pair_columns(projected, 2 * pairs + before), all_of(hot), all_of(self_far),
             pair_columns(self_mixed_grad, before), all_of(self_logs), all_of(self_deltas),
             all_of(tokens)]
            + [all_of(array) for array in earlier],
            outs + [out_pairs(count, wide)] * 3,
            pair_room(count, half) + [pltpu.VMEM((d, columns), LOW)],
            flops=12 << 30, moved=8 << 20, scalars=(bits,), after=after,
        )

    wide = half * LANES
    *earlier, query_one, key_one, value_one = self_part(
        0, False, [out_all((d, 3 * wide), LOW), out_all((8, wide), FULL)]
    )
    after = ()
    if halving:
        cross_sum.wait_for(query_one)
        cross_sum.plane()
        after = tuple(cross_sum.sent)
    *self_owned, query_two, key_two, value_two = self_part(
        half, True, owned(self_columns), earlier, after
    )
    after = ()
    if halving:
        cross_sum.wait_for(query_two)
        feed_total, _ = lax.optimization_barrier((feed_total, cross_sum.got[0]))
    feed_total = lax.psum_scatter(feed_total, ways[1], scatter_dimension=0, tiled=True)
    if halving:
        self_sum = Halving(me, *self_owned, device_count)
        cross_sum.line()
        self_sum.wait_for(*cross_sum.sent)
        self_sum.plane()
        cross_sum.wait_for(*self_sum.sent)
        after = tuple(self_sum.sent)
    tokens_grad, = call(
        tokens_back,
        "tokens_back",
        1,
        [all_of(array) for array in (first_grad,)]
        + [w_self_in]
        + [all_of(array) for array in (query_one, key_one, value_one, query_two, key_two, value_two)],
        [out_all((count, d), FULL)],
        flops=3 << 30, moved=8 << 20, after=after,
    )
    if halving:
        self_sum.wait_for(tokens_grad)
        cross_sum.wait_for(tokens_grad)
        self_sum.line()
        after = tuple(self_sum.sent)
    memory_grad, = call(
        memory_back,
        "memory_back",
        1,
        [all_of(key_signal), all_of(value_signal), w_kv],
        [out_all((key_count, d), FULL)],
        flops=2 << 30, moved=5 << 20, after=after,
    )
    if halving:
        self_sum.wait_for(memory_grad)
        ends = [(cross_sum.kept, *cross_sum.got), (self_sum.kept, *self_sum.got)]
    else:
        ends = [(scatter_rows(grads[0], device_count),) for grads in (cross_owned, self_owned)]
    kv_grad, query_grad, self_out_grad, cross_bias_grad, third = call(
        cross_last, "cross_last", 1, [all_of(array) for array in ends[0]],
        [out_all((own, 2 * d), FULL), out_all((own, d), FULL), out_all((own, d), FULL),
         out_all((3, own), FULL), out_all((1, own), FULL)],
    )
    feed_in_grad, feed_out_grad, cross_out_grad, bias_out_grad, bias_in_grad = call(
        feed_last, "feed_last", 1, [all_of(feed_total)],
        [out_all((own, ff), FULL), out_all((own, ff), FULL), out_all((own, d), FULL),
         out_all((1, own), FULL), out_all((1, own * ff // d), FULL)],
    )
    self_in_grad, self_bias_grad = call(
        self_last, "self_last", 1, [all_of(array) for array in (third, *ends[1])],
        [out_all((own, 3 * d), FULL), out_all((3, own), FULL)],
    )
    return (
        output,
        tokens_grad,
        memory_grad,
        self_in_grad,
        self_out_grad.T,
        self_bias_grad,
        query_grad,
        kv_grad,
        cross_out_grad.T,
        cross_bias_grad,
        feed_in_grad,
        feed_out_grad.T,
        bias_in_grad[0],
        bias_out_grad[0],
    )


def solution(mesh):
    return jax.shard_map(
        on_device,
        mesh=mesh,
        in_specs=(
            P(("dp", "fsdp"), None),
            P(("dp", "fsdp"), None),
            P(("dp", "fsdp"), None),
            P(("dp", "fsdp"), None),
            P(("dp", "fsdp"), None),
            P(),
            P(("dp", "fsdp"), None),
            P(None, ("dp", "fsdp")),
            P(None, ("dp", "fsdp")),
            P(("dp", "fsdp"), None),
            P(("dp", "fsdp"), None),
            P(None, ("dp", "fsdp")),
            P(None, ("dp", "fsdp")),
            P(("dp", "fsdp"), None),
            P(None, ("dp", "fsdp")),
            P(("dp", "fsdp")),
            P(("dp", "fsdp")),
        ),
        out_specs=(
            P(("dp", "fsdp"), None),
            P(("dp", "fsdp"), None),
            P(("dp", "fsdp"), None),
            P(("dp", "fsdp"), None),
            P(None, ("dp", "fsdp")),
            P(None, ("dp", "fsdp")),
            P(("dp", "fsdp"), None),
            P(("dp", "fsdp"), None),
            P(None, ("dp", "fsdp")),
            P(None, ("dp", "fsdp")),
            P(("dp", "fsdp"), None),
            P(None, ("dp", "fsdp")),
            P(("dp", "fsdp")),
            P(("dp", "fsdp")),
        ),
        check_vma=False,
    )
```

```python
import functools

import jax
import jax.numpy as jnp
from jax import lax
from jax.experimental import pallas as pl
from jax.experimental.pallas import tpu as pltpu
from jax.sharding import PartitionSpec as P

HEAD = 64
LANES = 128
FAR = -1e30
FIRST = 7
AXES = ("dp", "fsdp")
LOW = jnp.bfloat16
FULL = jnp.float32


def nn(left, right):
    return lax.dot_general(left, right, (((1,), (0,)), ((), ())), preferred_element_type=FULL)


def nt(left, right):
    return lax.dot_general(left, right, (((1,), (1,)), ((), ())), preferred_element_type=FULL)


def tn(left, right):
    return lax.dot_general(left, right, (((0,), (0,)), ((), ())), preferred_element_type=FULL)


def one_head(pair, odd):
    lane = lax.broadcasted_iota(jnp.int32, pair.shape, 1)
    return jnp.where((lane >= HEAD) == bool(odd), pair, jnp.zeros_like(pair))


def later_keys(rows, keys):
    query = lax.broadcasted_iota(jnp.int32, (rows, keys), 0)
    key = lax.broadcasted_iota(jnp.int32, (rows, keys), 1)
    return query, key


def call(
    body, name, grid, ins, outs, scratch=(), flops=0, moved=0, after=(), scalars=(), room=46
):
    used = len(ins)

    def only_used(*refs):
        front = len(scalars)
        body(*refs[: front + used], *refs[front + used + len(after) :])

    def spec_of(spec):
        if not scalars or spec.index_map is None:
            return spec
        place = spec.index_map
        return pl.BlockSpec(
            spec.block_shape, lambda i, *_: place(i), pipeline_mode=spec.pipeline_mode
        )

    made = pl.pallas_call(
        only_used if after else body,
        name=name,
        grid_spec=pltpu.PrefetchScalarGridSpec(
            num_scalar_prefetch=len(scalars),
            grid=(grid,),
            in_specs=[spec_of(spec) for _, spec in ins]
            + [pl.BlockSpec(memory_space=pl.ANY) for _ in after],
            out_specs=[spec_of(out[2]) for out in outs],
            scratch_shapes=list(scratch),
        ),
        out_shape=[
            (pltpu.VMEM if kept else pltpu.HBM)(shape, kind)
            for shape, kind, _, *kept in outs
        ],
        compiler_params=pltpu.CompilerParams(vmem_limit_bytes=room << 20),
        cost_estimate=pl.CostEstimate(flops=flops, bytes_accessed=moved, transcendentals=0),
    )(*scalars, *[placed(array) for array, _ in ins], *after)
    return [
        pltpu.with_memory_space_constraint(array, pltpu.VMEM) if out[3:] else array
        for array, out in zip(made, outs)
    ]


def rows_of(block, columns):
    return pl.BlockSpec((block, columns), lambda i: (i, 0))


def fixed(shape, place=None):
    place = (0,) * len(shape) if place is None else place
    return pl.BlockSpec(shape, lambda i: place, pipeline_mode=pl.Buffered(1))


def all_of(array):
    return (array, fixed(array.shape))


def out_all(shape, kind):
    return (shape, kind, fixed(shape))


def near(out):
    return (*out, True)


def placed(array):
    if jax.typeof(array).memory_space == pltpu.VMEM:
        return array
    return pltpu.with_memory_space_constraint(array, pltpu.HBM)


def attend(queries, hot, keys_ref, values_ref, count, causal):
    rows = queries.shape[0]
    heads = queries.shape[1] // HEAD
    lane = lax.broadcasted_iota(jnp.int32, (rows, LANES), 1)
    logs = jnp.zeros((rows, LANES), FULL)
    if causal:
        query, key = later_keys(rows, rows)
        ahead = jnp.where(key <= query, 0.0, FAR)

    def scores_of(head):
        columns = slice(head // 2 * LANES, (head // 2 + 1) * LANES)
        asked = jnp.concatenate([one_head(queries[:, columns], head % 2), hot], axis=1)
        scores = nt(asked, keys_ref[head // 2, :count, :])
        if not causal:
            return scores
        if count == rows:
            return scores + ahead
        return jnp.concatenate(
            [scores[:, : count - rows], scores[:, count - rows :] + ahead], axis=1
        )

    mixed = []
    following = scores_of(0)
    for head in range(heads):
        scores = following
        if head + 1 < heads:
            following = scores_of(head + 1)
        columns = slice(head // 2 * LANES, (head // 2 + 1) * LANES)
        top = jnp.max(scores, axis=1, keepdims=True)
        weights = jnp.exp(scores - top)
        amount = jnp.sum(weights, axis=1, keepdims=True)
        low = (weights * (1.0 / amount)).astype(LOW)
        here = nn(low, values_ref[:count, columns])
        if head % 2:
            mixed.append(jnp.where(lane < HEAD, other, here))
        other = here
        logs = jnp.where(lane == head, top + jnp.log(amount), logs)
    return jnp.concatenate(mixed, axis=1), logs.T[:heads]


def keep_keys(keys_ref, place, keys, hot):
    pairs = keys.shape[1] // LANES
    for pair in range(pairs):
        keys_ref[pair, place, :LANES] = keys[:, pair * LANES : (pair + 1) * LANES]
        keys_ref[pair, place, LANES:] = hot


def self_forward(
    tokens, hot, far, gate, w_in, w_out, bias_columns, w_query,
    projected, mixed, logs, first, first_low, cross_queries, keys, values, bias,
):
    step = pl.program_id(0)
    rows, d = tokens.shape

    @pl.when(step == 0)
    def _():
        bias[...] = bias_columns[...].astype(FULL).T[:8]

    joined_bias = jnp.concatenate([bias[0:1, :], jnp.zeros((1, d), FULL), bias[1:2, :]], axis=1)
    made = (nn(tokens[...], w_in[...]) + joined_bias).astype(LOW)
    projected[...] = made
    place = pl.ds(pl.multiple_of(step * rows, rows), rows)
    keep_keys(keys, place, made[:, d : 2 * d], far[...])
    values[place, :] = made[:, 2 * d :]
    for block in range(values.shape[0] // rows):

        @pl.when(step == block)
        def _(count=(block + 1) * rows):
            scaled = made[:, :d] * jnp.asarray(HEAD**-0.5, LOW)
            mixed[...], logs[...] = attend(scaled, hot[...], keys, values, count, True)

    branch = nt(mixed[...].astype(LOW), w_out[...]) + bias[2:3, :]
    total = tokens[...].astype(FULL) + gate[...] * branch
    first[...] = total
    first_low[...] = total.astype(LOW)
    cross_queries[...] = (nn(total.astype(LOW), w_query[...]) + bias[3:4, :]).astype(LOW)


def cross_forward(
    queries, memory, hot, far, gate, first, w_kv, w_out, bias_columns,
    memory_kv, mixed, logs, second, keys, bias,
):
    d = memory.shape[1]

    @pl.when(pl.program_id(0) == 0)
    def _():
        bias[...] = bias_columns[...].astype(FULL).T[:8]
        made = nn(memory[...], w_kv[...])
        memory_kv[:, :d] = made[:, :d].astype(LOW)
        memory_kv[:, d:] = (made[:, d:] + bias[4:5, :]).astype(LOW)
        keep_keys(keys, slice(None), memory_kv[:, :d], far[...])

    scaled = queries[...] * jnp.asarray(HEAD**-0.5, LOW)
    mixed[...], logs[...] = attend(
        scaled, hot[...], keys, memory_kv.at[:, d:], memory.shape[0], False
    )
    branch = nt(mixed[...].astype(LOW), w_out[...]) + bias[5:6, :]
    second[...] = first[...] + gate[...] * branch


def head_sums(left, right):
    d = left.shape[1]
    head = lax.broadcasted_iota(jnp.int32, (d // HEAD, d), 0)
    column = lax.broadcasted_iota(jnp.int32, (d // HEAD, d), 1)
    chosen = (column // HEAD == head).astype(LOW)
    product = left.astype(FULL) * right.astype(FULL)
    high = product.astype(LOW)
    rest = product - high.astype(FULL)
    middle = rest.astype(LOW)
    last = (rest - middle.astype(FULL)).astype(LOW)
    return nt(chosen, high) + nt(chosen, middle) + nt(chosen, last)


def gelu_both(z):
    c = 0.7978845608028654
    square = z * z
    bent = jnp.tanh(c * z * (1.0 + 0.044715 * square))
    half = 0.5 * (1.0 + bent)
    slope = half + 0.5 * z * (1.0 - bent * bent) * (c * (1.0 + 3.0 * 0.044715 * square))
    return z * half, slope


def spread(d, ff):
    each = ff // d
    row = lax.broadcasted_iota(jnp.int32, (d, ff), 0)
    entry = lax.broadcasted_iota(jnp.int32, (d, ff), 1)
    column = lax.broadcasted_iota(jnp.int32, (LANES, ff), 0)
    there = lax.broadcasted_iota(jnp.int32, (LANES, ff), 1)
    return entry // each == row, (there % each + FIRST == column).astype(LOW)


def columns_to_row(columns, ff):
    owner, place = spread(columns.shape[0], ff)
    return jnp.sum(jnp.where(owner, nn(columns, place), 0.0), axis=0, keepdims=True)


def row_to_columns(row, d):
    owner, place = spread(d, row.shape[1])
    return nt(jnp.where(owner, row, 0.0).astype(LOW), place).astype(LOW)


def rows_to_columns(*rows):
    d = rows[0].shape[1]
    stack = jnp.concatenate([*rows, jnp.zeros((LANES - len(rows), d), FULL)], axis=0)
    return stack.T.astype(LOW)


def feed_both(
    second, upstream, gate, mixed, w_in, w_out, w_cross_out, bias_columns,
    output, second_grad, mixed_grad, deltas, feed_grad, sums,
    second_low, signal_all, hidden_all, before_all, cross_all, mixed_all, bias, bias_in, bias_in_grad,
    *, inner, own,
):
    step = pl.program_id(0)
    rows, d = second.shape
    ff = w_in.shape[1]
    place = pl.ds(pl.multiple_of(step * rows, rows), rows)
    low = second[...].astype(LOW)
    second_low[place, :] = low
    mixed_all[place, :] = mixed[...].astype(LOW)
    given = upstream[...].astype(FULL)
    signal = (gate[...] * given).astype(LOW)
    signal_all[place, :] = signal

    @pl.when(step == 0)
    def _():
        bias[...] = bias_columns[...].astype(FULL).T[:8]
        bias_in[...] = columns_to_row(bias_columns[...], ff)
        bias_in_grad[...] = jnp.zeros_like(bias_in_grad)
        sums[...] = jnp.zeros_like(sums)

    made = bias[6:7, :]
    back = given
    width = 1024
    parts = [slice(start, start + width) for start in range(0, ff, width)]
    products = lambda part: (nn(low, w_in[:, part]) + bias_in[:, part], nn(signal, w_out[:, part]))
    following = products(parts[0])
    for index, part in enumerate(parts):
        before, hidden_back = following
        if index + 1 < len(parts):
            following = products(parts[index + 1])
        hidden, slope = gelu_both(before)
        hidden = hidden.astype(LOW)
        hidden_all[place, part] = hidden
        before_grad = (hidden_back * slope).astype(LOW)
        before_all[place, part] = before_grad
        bias_in_grad[:, part] += column_sum(before_grad)
        made = made + nt(hidden, w_out[:, part])
        back = back + nt(before_grad, w_in[:, part])
    output[...] = (second[...] + gate[...] * made).astype(LOW)
    second_grad[...] = back
    crossed = (gate[...] * back).astype(LOW)
    cross_all[place, :] = crossed
    mixed_back = nn(crossed, w_cross_out[...]).astype(LOW)
    mixed_grad[...] = mixed_back
    deltas[...] = head_sums(mixed_back, mixed[...])
    sums[0:1, :] += column_sum(signal)
    sums[1:2, :] += column_sum(crossed)

    @pl.when(step == pl.num_programs(0) - 1)
    def _():
        def keep(start, grad):
            end = start + grad.shape[1]
            outer = d // own // inner
            for owner in range(inner * outer if inner > 1 else 0):
                to = (owner % inner * outer + owner // inner) * own
                feed_grad[to : to + own, start:end] = grad[owner * own : (owner + 1) * own]
            if inner == 1:
                feed_grad[:, start:end] = grad

        for part in parts:
            keep(part.start, tn(second_low[...], before_all[:, part]).astype(LOW))
            keep(ff + part.start, tn(signal_all[...], hidden_all[:, part]).astype(LOW))
        keep(2 * ff, tn(cross_all[...], mixed_all[...]).astype(LOW))
        at = 2 * ff + d
        keep(at, rows_to_columns(sums[0:1, :]))
        keep(at + LANES, row_to_columns(bias_in_grad[...], d))


def column_sum(array):
    return jnp.sum(array.astype(FULL), axis=0, keepdims=True)


def attend_back(
    queries, keys, values, hot, far, mixed_grad, logs, deltas, pair,
    query_grad, key_grad, value_grad, key_sum, value_sum, reached, causal, block=256,
):
    count = keys.shape[0]
    reached[:, :LANES] = keys[...]
    reached[:, LANES:] = far[...]
    turned = keys[...].T
    if causal:
        key, query = later_keys(block, block)
        ahead = jnp.where(key <= query, 0.0, FAR)
    items = [
        (start, odd) for start in range(queries.shape[0] - block, -1, -block) for odd in range(2)
    ]

    def products(item):
        start, odd = item
        place = slice(start, start + block)
        reach = start + block if causal else count
        asked = one_head(queries[place, :], odd) * jnp.asarray(HEAD**-0.5, LOW)
        incoming = one_head(mixed_grad[place, :], odd)
        scores = nt(reached[:reach, :], jnp.concatenate([asked, hot[place, :]], axis=1))
        if causal and start:
            scores = jnp.concatenate([scores[:start], scores[start:] + ahead], axis=0)
        elif causal:
            scores = scores + ahead
        return scores, nt(values[:reach, :], incoming), asked, incoming, place, reach

    following = products(items[0])
    for index, (start, odd) in enumerate(items):
        scores, pushed, asked, incoming, place, reach = following
        if index + 1 < len(items):
            following = products(items[index + 1])
        head = pl.ds(2 * pair + odd, 1)
        chances = jnp.exp(scores - logs[head, place])
        score_grad = (chances * (pushed - deltas[head, place])).astype(LOW)
        turned_grad = nn(turned[odd * HEAD : (odd + 1) * HEAD, :reach], score_grad)
        value_part = nn(chances.astype(LOW), incoming)
        key_part = nn(score_grad, asked)
        if index == 0:
            value_sum[...] = value_part
            key_sum[...] = key_part
        else:
            value_sum[:reach, :] += value_part
            key_sum[:reach, :] += key_part
        if odd:
            both = jnp.concatenate([other, turned_grad], axis=0) * HEAD**-0.5
            query_grad[place, :] = both.T.astype(LOW)
        other = turned_grad
    key_grad[...] = key_sum[...].astype(LOW)
    value_grad[...] = value_sum[...].astype(LOW)


def cross_back(
    bits, queries, keys, values, hot, far, in_grad, logs, cross_deltas, sums,
    first, second_grad, memory, self_mixed, gate, weights, self_weights,
    *outs,
):
    (
        *owned, key_grad, value_grad, first_grad, mixed_grad, deltas,
        key_sum, value_sum, reached, signals, first_here, second_here, memory_here, mixed_here,
        w_query, w_out, grads, arrived,
    ) = outs
    pair = pl.program_id(0)
    d = memory.shape[1]
    copies = [
        pltpu.make_async_copy(source, target, arrived.at[index])
        for index, (source, target) in enumerate(
            [
                (first, first_here), (second_grad, second_here), (memory, memory_here),
                (self_mixed, mixed_here), (weights.at[:, 2 * d : 3 * d], w_query),
                (self_weights.at[:, 3 * d : 4 * d], w_out),
            ]
        )
    ]

    @pl.when(pair == 0)
    def _():
        for copy in copies:
            copy.start()

    attend_back(
        queries, keys, values, hot, far, in_grad, logs, cross_deltas, pair,
        signals.at[0, pair], signals.at[1, pair], signals.at[2, pair],
        key_sum, value_sum, reached, False,
    )
    key_grad[...] = signals[1, pair]
    value_grad[...] = signals[2, pair]

    @pl.when(pair == pl.num_programs(0) - 1)
    def _():
        for copy in copies:
            copy.wait()
        pairs = signals.shape[1]
        query_signal, key_signal, value_signal = (
            jnp.concatenate([signals[which, place] for place in range(pairs)], axis=1)
            for which in range(3)
        )
        back = second_here[...] + nt(query_signal, w_query[...])
        first_grad[...] = back
        signal = (gate[...] * back).astype(LOW)
        mixed_back = nn(signal, w_out[...]).astype(LOW)
        mixed_grad[...] = mixed_back
        deltas[...] = head_sums(mixed_back, mixed_here[...])
        grads[:, :d] = tn(memory_here[...], key_signal).astype(LOW)
        grads[:, d : 2 * d] = tn(memory_here[...], value_signal).astype(LOW)
        grads[:, 2 * d : 3 * d] = tn(first_here[...], query_signal).astype(LOW)
        grads[:, 3 * d : 4 * d] = tn(signal, mixed_here[...].astype(LOW)).astype(LOW)
        grads[:, 4 * d :] = rows_to_columns(
            column_sum(query_signal), column_sum(value_signal), sums[1:2, :], column_sum(signal)
        )
        if len(owned) == 2:
            part_by_core(bits, grads, *owned)
        else:
            owned[0][...] = grads[...]


def self_back(
    bits, queries, keys, values, hot, far, in_grad, logs, deltas, tokens, *rest, before, ending
):
    if ending:
        earlier, earlier_sums, *rest = rest
    *owned, query_grad, key_grad, value_grad, key_sum, value_sum, reached, signals, grads = rest
    step = pl.program_id(0)
    pairs = signals.shape[1]
    wide = pairs * LANES
    attend_back(
        queries, keys, values, hot, far, in_grad, logs, deltas, before + step,
        signals.at[0, step], signals.at[1, step], signals.at[2, step],
        key_sum, value_sum, reached, True,
    )
    query_grad[...] = signals[0, step]
    key_grad[...] = signals[1, step]
    value_grad[...] = signals[2, step]

    @pl.when(step == pl.num_programs(0) - 1)
    def _():
        at = 3 * wide if ending else 0
        if ending:
            grads[:, :at] = earlier[...]
        added = []
        for which in range(3):
            part = jnp.concatenate([signals[which, place] for place in range(pairs)], axis=1)
            grads[:, at + which * wide : at + (which + 1) * wide] = tn(
                tokens[...], part
            ).astype(LOW)
            if which != 1:
                added.append(column_sum(part))
        if not ending:
            owned[0][...] = grads[...]
            owned[1][0:1, :] = added[0]
            owned[1][1:2, :] = added[1]
            return
        grads[:, 2 * at :] = rows_to_columns(
            *[
                jnp.concatenate([earlier_sums[row : row + 1, :], added[row]], axis=1)
                for row in range(2)
            ]
        )
        if len(owned) == 2:
            part_by_core(bits, grads, *owned)
        else:
            owned[0][...] = grads[...]


def part_by_core(bits, grads, keep, away):
    own = keep.shape[1]
    for core in range(2):

        @pl.when(bits[0] == core)
        def _(core=core):
            for slab in range(2 * keep.shape[0]):
                there = keep if slab % 2 == core else away
                there[slab // 2] = grads[slab * own : (slab + 1) * own, :]


def memory_back(key_signal, value_signal, w_kv, memory_grad):
    d = key_signal.shape[1]
    memory_grad[...] = nt(key_signal[...], w_kv[:, :d]) + nt(value_signal[...], w_kv[:, d:])


def tokens_back(first_grad, w_in, *refs):
    *signals, tokens_grad = refs
    d = first_grad.shape[1]
    total = first_grad[...]
    wide = signals[0].shape[1]
    for index, signal in enumerate(signals):
        start = index % 3 * d + index // 3 * wide
        total = total + nt(signal[...], w_in[:, start : start + wide])
    tokens_grad[...] = total


def sum_to_owners(grads, device_count, orders):
    me = lax.axis_index(AXES)
    bits = device_count.bit_length() - 1
    running = []
    for grad in grads:
        rows, columns = grad.shape
        running.append(grad.reshape((2,) * bits + (rows // device_count, columns)))
    left = [list(range(bits)) for _ in grads]
    for step in range(bits):
        sent = []
        for part, order in enumerate(orders):
            bit = order[step]
            axis = len(left[part]) - 1 - left[part].index(bit)
            mine = (me >> bit) & 1
            away = lax.dynamic_index_in_dim(running[part], 1 - mine, axis, keepdims=False)
            pairs = [(i, i ^ (1 << bit)) for i in range(device_count)]
            sent.append((axis, mine, lax.ppermute(away.astype(LOW), AXES, pairs)))
            left[part].remove(bit)
        for part, (axis, mine, got) in enumerate(sent):
            kept = lax.dynamic_index_in_dim(running[part], mine, axis, keepdims=False)
            running[part] = kept.astype(FULL) + got.astype(FULL)
    return running


def swap(array, bit, device_count):
    return lax.ppermute(array, AXES, [(i, i ^ (1 << bit)) for i in range(device_count)])


def scatter_rows(grad, device_count):
    bits = device_count.bit_length() - 1
    high = list(range(1, bits))[::-1]
    half = grad.shape[1] // 256 * 128
    orders = ([0] + high, [0, high[1], high[0]] + high[2:])
    return jnp.concatenate(
        sum_to_owners([grad[:, :half], grad[:, half:]], device_count, orders), axis=1
    )


def swap(array, change, device_count):
    return lax.ppermute(array, AXES, [(i, i ^ change) for i in range(device_count)])


def picked(terms, first, second):
    total = None
    for term in terms:
        for place in (first, second):
            term = lax.dynamic_index_in_dim(term, place, 0, keepdims=False)
        total = term.astype(FULL) if total is None else total + term.astype(FULL)
    return total


class Halving:
    changes = ((0, 1), (1, 0), (1, 1))

    def __init__(self, me, keep, away, device_count):
        self.count = device_count
        self.x, self.y = (me >> 3) & 1, (me >> 4) & 1
        self.low, self.high = (me >> 1) & 1, (me >> 2) & 1
        shape = (2, 2, 4, *keep.shape[1:])
        self.terms = [keep.reshape(shape)]
        self.got = [swap(away.reshape(shape), 1, device_count)]

    def plane(self):
        terms = self.terms + self.got
        self.sent = [picked(terms, self.y ^ y, self.x ^ x).astype(LOW) for y, x in self.changes]
        self.got = [
            swap(array, 8 * x + 16 * y, self.count)
            for array, (y, x) in zip(self.sent, self.changes)
        ]
        self.terms = [
            lax.dynamic_index_in_dim(
                lax.dynamic_index_in_dim(term, self.y, 0, keepdims=False), self.x, 0, keepdims=False
            )
            for term in terms
        ]

    def line(self):
        terms = [term.reshape(2, 2, *term.shape[1:]) for term in self.terms + self.got]
        self.sent = [
            picked(terms, self.high ^ high, self.low ^ low).astype(LOW)
            for high, low in self.changes
        ]
        self.kept = picked(terms, self.high, self.low)

    def send_line(self, *after):
        self.sent = list(lax.optimization_barrier((*self.sent, *after))[: len(self.sent)])
        self.got = [
            swap(array, 2 * low + 4 * high, self.count)
            for array, (high, low) in zip(self.sent, self.changes)
        ]

    def wait_for(self, *arrays):
        self.got = list(lax.optimization_barrier((*self.got, *arrays))[: len(self.got)])


def total_of(keep, *got):
    total = keep[...]
    for part in got:
        total = total + part[...].astype(FULL)
    return total


def cross_last(*refs):
    *parts, kv, query, self_out, cross_bias, self_bias = refs
    total = total_of(*parts)
    d = query.shape[1]
    kv[...] = total[:, : 2 * d]
    query[...] = total[:, 2 * d : 3 * d]
    self_out[...] = total[:, 3 * d : 4 * d]
    turned = turned_bias(total[:, 4 * d :])
    cross_bias[...] = turned[0:3]
    self_bias[...] = turned[3:4]


def turned_bias(columns):
    own = columns.shape[0]
    square = jnp.concatenate([columns, jnp.zeros((LANES - own, LANES), FULL)], axis=0)
    return square.T[:8, :own]


def self_last(third, *refs):
    *parts, self_in, bias = refs
    total = total_of(*parts)
    columns = self_in.shape[1]
    half = columns // 2
    wide = half // 3
    for call_index in range(2):
        for which in range(3):
            at = call_index * half + which * wide
            to = which * 2 * wide + call_index * wide
            self_in[:, to : to + wide] = total[:, at : at + wide]
    bias[0:2, :] = turned_bias(total[:, columns:])[0:2]
    bias[2:3, :] = third[...]


def feed_last(total, feed_in, feed_out, cross_out, bias_out, bias_in):
    ff = feed_in.shape[1]
    at = 2 * ff + cross_out.shape[1]
    feed_in[...] = total[:, :ff].astype(FULL)
    feed_out[...] = total[:, ff : 2 * ff].astype(FULL)
    cross_out[...] = total[:, 2 * ff : at].astype(FULL)
    bias_out[...] = turned_bias(total[:, at : at + LANES].astype(FULL))[0:1]
    bias_in[...] = columns_to_row(total[:, at + LANES :], bias_in.shape[1])


def pack(
    self_in, self_out, cross_query, cross_kv, cross_out, feed_in, feed_out, self_bias, cross_bias,
    bias_out, bias_in, near, own_feed,
):
    d = self_out.shape[1]
    ff = feed_in.shape[1]
    own = self_in.shape[0]
    near[:, : 3 * d] = self_in[...].astype(LOW)
    near[:, 3 * d : 4 * d] = self_out[...].astype(LOW)
    rows = jnp.concatenate(
        [self_bias[...], cross_bias[...], bias_out[...], jnp.zeros((LANES - 7, own), FULL)], axis=0
    )
    wide = jnp.concatenate([rows, jnp.zeros((LANES, LANES - own), FULL)], axis=1)
    at = 4 * d + LANES
    near[:, 4 * d : at] = wide.T[:own].astype(LOW) + row_to_columns(bias_in[...], own)
    near[:, at : at + 2 * d] = cross_kv[...].astype(LOW)
    near[:, at + 2 * d : at + 3 * d] = cross_query[...].astype(LOW)
    near[:, at + 3 * d :] = cross_out[...].astype(LOW)
    own_feed[:, :ff] = feed_in[...].astype(LOW)
    own_feed[:, ff:] = feed_out[...].astype(LOW)


def marks(seq_lengths, memory_lengths, residual_gate, hot, self_far, memory_far, gate):
    slots = seq_lengths.shape[0]
    lane = lax.broadcasted_iota(jnp.int32, hot.shape, 1)

    def numbered(lengths, padding):
        position = lax.broadcasted_iota(jnp.int32, hot.shape, 0)
        end = lengths[0]
        number = jnp.where(position >= end, 1, 0)
        for slot in range(1, slots):
            end = end + lengths[slot]
            number = number + jnp.where(position >= end, 1, 0)
        present = position < end
        return jnp.where(present, number, padding), present

    ids, present = numbered(seq_lengths, slots)
    hot[...] = jnp.where(ids == lane, 1.0, 0.0).astype(LOW)
    self_far[...] = jnp.where(ids == lane, 0.0, FAR).astype(LOW)
    gate[...] = jnp.where(present[:, :1], residual_gate[0], 0.0)
    ids, _ = numbered(memory_lengths, slots + 1)
    memory_far[...] = jnp.where(ids == lane, 0.0, FAR).astype(LOW)


def gather_near(near, cut, device_count):
    me = lax.axis_index(AXES)
    others = [swap(near, 2 * change, device_count) for change in (1, 2, 3)]
    first, second, third, fourth = near, *others
    odd = jnp.where(
        (me >> 1) & 1,
        jnp.stack([second, first, fourth, third]),
        jnp.stack([first, second, third, fourth]),
    )
    line = jnp.where((me >> 2) & 1, jnp.concatenate([odd[2:], odd[:2]]), odd)
    held = [line[..., :cut], line[..., cut:]]
    known = [[1, 1], [1, 1]]
    for bits in ((3, 4), (4, 3), (0, 0)):
        got = [swap(array, 1 << bit, device_count) for array, bit in zip(held, bits)]
        for part, bit in enumerate(bits):
            mine, theirs = held[part], got[part]
            if bit == 0:
                axis = mine.ndim - 2
            else:
                axis = sum(other > bit for other in known[part])
            low = jnp.stack([mine, theirs], axis)
            high = jnp.stack([theirs, mine], axis)
            held[part] = jnp.where((me >> bit) & 1, high, low)
            known[part].append(bit)
    return [array.reshape(-1, array.shape[-1]) for array in held]


def on_device(
    tokens, memory, out_cotangent, seq_lengths, memory_lengths, residual_gate,
    self_in, self_out, self_bias, cross_query, cross_key_value, cross_out, cross_bias,
    feed_in, feed_out, feed_bias_in, feed_bias_out,
):
    device_count = lax.axis_size(AXES)
    count, d = tokens.shape
    key_count = memory.shape[0]
    ff = feed_in.shape[1]
    own = self_in.shape[0]
    pairs = d // LANES
    heads = d // HEAD
    block = 256
    steps = count // block
    halving = lax.axis_size("dp") == 4 and lax.axis_size("fsdp") == 8
    me = lax.axis_index(AXES)
    bits = (me & 1).astype(jnp.int32)[None]
    cut = 4 * d + LANES
    own_near, own_feed = call(
        pack,
        "pack",
        1,
        [
            all_of(array)
            for array in (
                self_in, self_out.T, cross_query, cross_key_value, cross_out.T, feed_in,
                feed_out.T, self_bias, cross_bias, feed_bias_out[None], feed_bias_in[None],
            )
        ],
        [out_all((own, cut + 4 * d), LOW), out_all((own, 2 * ff), LOW)],
    )
    feed_whole = lax.all_gather(own_feed, AXES, axis=0, tiled=True)
    if halving:
        self_whole, cross_whole = gather_near(own_near, cut, device_count)
    else:
        self_whole = lax.all_gather(own_near[:, :cut], AXES, axis=0, tiled=True)
        cross_whole = lax.all_gather(own_near[:, cut:], AXES, axis=0, tiled=True)
    hot, self_far, memory_far, gate = call(
        marks,
        "marks",
        1,
        [],
        [near(out_all((count, LANES), LOW)), near(out_all((count, LANES), LOW)),
         near(out_all((key_count, LANES), LOW)), near(out_all((count, 1), FULL))],
        scalars=(seq_lengths[0], memory_lengths[0], residual_gate),
    )
    w_self_in = (self_whole, fixed((d, 3 * d), (0, 0)))
    w_self_out = (self_whole, fixed((d, d), (0, 3)))
    bias_columns = (self_whole, fixed((d, LANES), (0, 4 * d // LANES)))
    w_kv = (cross_whole, fixed((d, 2 * d), (0, 0)))
    w_query = (cross_whole, fixed((d, d), (0, 2)))
    w_cross_out = (cross_whole, fixed((d, d), (0, 3)))
    w_feed_in = (feed_whole, fixed((d, ff), (0, 0)))
    w_feed_out = (feed_whole, fixed((d, ff), (0, 1)))

    each = lambda array: (array, rows_of(block, array.shape[1]))
    out_rows = lambda columns, kind: ((count, columns), kind, rows_of(block, columns))
    out_heads = ((heads, count), FULL, pl.BlockSpec((heads, block), lambda i: (0, i)))

    projected, self_mixed, self_logs, first, first_low, cross_queries = call(
        self_forward,
        "self_forward",
        steps,
        [each(tokens), each(hot), each(self_far), each(gate), w_self_in, w_self_out, bias_columns,
         w_query],
        [out_rows(3 * d, LOW), out_rows(d, FULL), near(out_heads), near(out_rows(d, FULL)),
         out_rows(d, LOW), out_rows(d, LOW)],
        [pltpu.VMEM((pairs, count, 2 * LANES), LOW), pltpu.VMEM((count, d), LOW),
         pltpu.VMEM((8, d), FULL)],
        flops=15 << 30, moved=8 << 20,
    )
    block = 512
    steps = count // block
    out_heads = ((heads, count), FULL, pl.BlockSpec((heads, block), lambda i: (0, i)))
    memory_kv, cross_mixed, cross_logs, second = call(
        cross_forward,
        "cross_forward",
        steps,
        [each(cross_queries), all_of(memory), each(hot), all_of(memory_far), each(gate),
         each(first), w_kv, w_cross_out, bias_columns],
        [out_all((key_count, 2 * d), LOW), near(out_rows(d, FULL)), near(out_heads),
         out_rows(d, FULL)],
        [pltpu.VMEM((pairs, key_count, 2 * LANES), LOW), pltpu.VMEM((8, d), FULL)],
        flops=20 << 30, moved=8 << 20,
    )
    inner = lax.axis_size("fsdp") if halving else 1
    output, second_grad, cross_mixed_grad, cross_deltas, feed_grad, feed_sums = call(
        functools.partial(feed_both, inner=inner, own=own),
        "feed_both",
        steps,
        [each(second), each(out_cotangent), each(gate), each(cross_mixed), w_feed_in, w_feed_out,
         w_cross_out, bias_columns],
        [out_rows(d, LOW), out_rows(d, FULL), out_rows(d, LOW), near(out_heads),
         out_all((d, 2 * ff + d + 2 * LANES), LOW), near(out_all((8, d), FULL))],
        [pltpu.VMEM((count, d), LOW), pltpu.VMEM((count, d), LOW), pltpu.VMEM((count, ff), LOW),
         pltpu.VMEM((count, ff), LOW), pltpu.VMEM((count, d), LOW), pltpu.VMEM((count, d), LOW),
         pltpu.VMEM((8, d), FULL), pltpu.VMEM((1, ff), FULL), pltpu.VMEM((1, ff), FULL)],
        flops=25 << 30, moved=16 << 20,
    )
    ways = ("fsdp", "dp") if halving else ("dp", "fsdp")
    feed_total = lax.psum_scatter(feed_grad, ways[0], scatter_dimension=0, tiled=True)

    def pair_columns(array, start, width=LANES):
        return (array, pl.BlockSpec((array.shape[0], width), lambda i: (0, start + i)))

    def out_pairs(rows, columns):
        return ((rows, columns), LOW, pl.BlockSpec((rows, LANES), lambda i: (0, i)))

    def owned(columns):
        if halving:
            return [out_all((device_count // 2, own, columns), LOW)] * 2
        return [out_all((d, columns), LOW)]

    def pair_room(rows, steps):
        return [
            pltpu.VMEM((rows, LANES), FULL), pltpu.VMEM((rows, LANES), FULL),
            pltpu.VMEM((rows, 2 * LANES), LOW), pltpu.VMEM((3, steps, rows, LANES), LOW),
        ]

    left_there = lambda array: (array, pl.BlockSpec(memory_space=pl.ANY))
    cross_columns = 4 * d + LANES
    *cross_owned, key_signal, value_signal, first_grad, self_mixed_grad, self_deltas = call(
        cross_back,
        "cross_back",
        pairs,
        [pair_columns(cross_queries, 0), pair_columns(memory_kv, 0),
         pair_columns(memory_kv, pairs), all_of(hot), all_of(memory_far),
         pair_columns(cross_mixed_grad, 0), all_of(cross_logs), all_of(cross_deltas),
         all_of(feed_sums), left_there(first_low), left_there(second_grad), left_there(memory),
         left_there(self_mixed), all_of(gate), left_there(cross_whole), left_there(self_whole)],
        owned(cross_columns)
        + [out_pairs(key_count, d), out_pairs(key_count, d), out_all((count, d), FULL),
           near(out_all((count, d), LOW)), near(out_all((heads, count), FULL))],
        pair_room(key_count, pairs)
        + [pltpu.VMEM((count, d), LOW), pltpu.VMEM((count, d), FULL),
           pltpu.VMEM((key_count, d), LOW), pltpu.VMEM((count, d), FULL),
           pltpu.VMEM((d, d), LOW), pltpu.VMEM((d, d), LOW),
           pltpu.VMEM((d, cross_columns), LOW), pltpu.SemaphoreType.DMA((6,))],
        flops=30 << 30, moved=24 << 20, scalars=(bits,),
    )
    if halving:
        cross_sum = Halving(me, *cross_owned, device_count)

    half = pairs // 2
    self_columns = 3 * d + LANES

    def self_part(before, ending, outs, earlier=(), after=()):
        wide = half * LANES
        columns = self_columns if ending else 3 * wide
        return call(
            functools.partial(self_back, before=before, ending=ending),
            "self_back",
            half,
            [pair_columns(projected, before), pair_columns(projected, pairs + before),
             pair_columns(projected, 2 * pairs + before), all_of(hot), all_of(self_far),
             pair_columns(self_mixed_grad, before), all_of(self_logs), all_of(self_deltas),
             all_of(tokens)]
            + [all_of(array) for array in earlier],
            outs + [out_pairs(count, wide)] * 3,
            pair_room(count, half) + [pltpu.VMEM((d, columns), LOW)],
            flops=12 << 30, moved=8 << 20, scalars=(bits,), after=after,
        )

    wide = half * LANES
    *earlier, query_one, key_one, value_one = self_part(
        0, False, [out_all((d, 3 * wide), LOW), out_all((8, wide), FULL)]
    )
    after = ()
    if halving:
        cross_sum.wait_for(query_one)
        cross_sum.plane()
        after = tuple(cross_sum.sent)
    *self_owned, query_two, key_two, value_two = self_part(
        half, True, owned(self_columns), earlier, after
    )
    after = ()
    if halving:
        cross_sum.wait_for(query_two)
        feed_total, _ = lax.optimization_barrier((feed_total, cross_sum.got[0]))
    feed_total = lax.psum_scatter(feed_total, ways[1], scatter_dimension=0, tiled=True)
    if halving:
        self_sum = Halving(me, *self_owned, device_count)
        cross_sum.line()
        self_sum.wait_for(*cross_sum.sent)
        self_sum.plane()
        cross_sum.send_line(*self_sum.sent)
        after = tuple(self_sum.sent)
    tokens_grad, = call(
        tokens_back,
        "tokens_back",
        steps,
        [each(first_grad), w_self_in]
        + [each(array) for array in (query_one, key_one, value_one, query_two, key_two, value_two)],
        [out_rows(d, FULL)],
        flops=3 << 30, moved=8 << 20, after=after,
    )
    memory_grad, = call(
        memory_back,
        "memory_back",
        steps,
        [each(key_signal), each(value_signal), w_kv],
        [((key_count, d), FULL, rows_of(block, d))],
        flops=2 << 30, moved=5 << 20, after=after,
    )
    if halving:
        self_sum.wait_for(tokens_grad, memory_grad)
        self_sum.line()
        self_sum.send_line()
        cross_sum.wait_for(*self_sum.sent)
        ends = [(cross_sum.kept, *cross_sum.got), (self_sum.kept, *self_sum.got)]
    else:
        ends = [(scatter_rows(grads[0], device_count),) for grads in (cross_owned, self_owned)]
    kv_grad, query_grad, self_out_grad, cross_bias_grad, third = call(
        cross_last, "cross_last", 1, [all_of(array) for array in ends[0]],
        [out_all((own, 2 * d), FULL), out_all((own, d), FULL), out_all((own, d), FULL),
         out_all((3, own), FULL), out_all((1, own), FULL)],
    )
    feed_in_grad, feed_out_grad, cross_out_grad, bias_out_grad, bias_in_grad = call(
        feed_last, "feed_last", 1, [all_of(feed_total)],
        [out_all((own, ff), FULL), out_all((own, ff), FULL), out_all((own, d), FULL),
         out_all((1, own), FULL), out_all((1, own * ff // d), FULL)],
    )
    if halving:
        ends[1] = lax.optimization_barrier((*ends[1], feed_in_grad))[:-1]
    self_in_grad, self_bias_grad = call(
        self_last, "self_last", 1, [all_of(array) for array in (third, *ends[1])],
        [out_all((own, 3 * d), FULL), out_all((3, own), FULL)],
    )
    return (
        output,
        tokens_grad,
        memory_grad,
        self_in_grad,
        self_out_grad.T,
        self_bias_grad,
        query_grad,
        kv_grad,
        cross_out_grad.T,
        cross_bias_grad,
        feed_in_grad,
        feed_out_grad.T,
        bias_in_grad[0],
        bias_out_grad[0],
    )


def solution(mesh):
    return jax.shard_map(
        on_device,
        mesh=mesh,
        in_specs=(
            P(("dp", "fsdp"), None),
            P(("dp", "fsdp"), None),
            P(("dp", "fsdp"), None),
            P(("dp", "fsdp"), None),
            P(("dp", "fsdp"), None),
            P(),
            P(("dp", "fsdp"), None),
            P(None, ("dp", "fsdp")),
            P(None, ("dp", "fsdp")),
            P(("dp", "fsdp"), None),
            P(("dp", "fsdp"), None),
            P(None, ("dp", "fsdp")),
            P(None, ("dp", "fsdp")),
            P(("dp", "fsdp"), None),
            P(None, ("dp", "fsdp")),
            P(("dp", "fsdp")),
            P(("dp", "fsdp")),
        ),
        out_specs=(
            P(("dp", "fsdp"), None),
            P(("dp", "fsdp"), None),
            P(("dp", "fsdp"), None),
            P(("dp", "fsdp"), None),
            P(None, ("dp", "fsdp")),
            P(None, ("dp", "fsdp")),
            P(("dp", "fsdp"), None),
            P(("dp", "fsdp"), None),
            P(None, ("dp", "fsdp")),
            P(None, ("dp", "fsdp")),
            P(("dp", "fsdp"), None),
            P(None, ("dp", "fsdp")),
            P(("dp", "fsdp")),
            P(("dp", "fsdp")),
        ),
        check_vma=False,
    )
```

```python
import functools

import jax
import jax.numpy as jnp
from jax import lax
from jax.experimental import pallas as pl
from jax.experimental.pallas import tpu as pltpu
from jax.sharding import PartitionSpec as P

HEAD = 64
LANES = 128
FAR = -1e30
FIRST = 7
AXES = ("dp", "fsdp")
LOW = jnp.bfloat16
FULL = jnp.float32


def nn(left, right):
    return lax.dot_general(left, right, (((1,), (0,)), ((), ())), preferred_element_type=FULL)


def nt(left, right):
    return lax.dot_general(left, right, (((1,), (1,)), ((), ())), preferred_element_type=FULL)


def tn(left, right):
    return lax.dot_general(left, right, (((0,), (0,)), ((), ())), preferred_element_type=FULL)


def one_head(pair, odd):
    lane = lax.broadcasted_iota(jnp.int32, pair.shape, 1)
    return jnp.where((lane >= HEAD) == bool(odd), pair, jnp.zeros_like(pair))


def later_keys(rows, keys):
    query = lax.broadcasted_iota(jnp.int32, (rows, keys), 0)
    key = lax.broadcasted_iota(jnp.int32, (rows, keys), 1)
    return query, key


def call(
    body, name, grid, ins, outs, scratch=(), flops=0, moved=0, after=(), scalars=(), room=46,
    anywhere=(),
):
    used = len(ins)

    def only_used(*refs):
        front = len(scalars)
        body(*refs[: front + used], *refs[front + used + len(after) :])

    def spec_of(spec):
        if not scalars or spec.index_map is None:
            return spec
        place = spec.index_map
        return pl.BlockSpec(
            spec.block_shape, lambda i, *_: place(i), pipeline_mode=spec.pipeline_mode
        )

    made = pl.pallas_call(
        only_used if after else body,
        name=name,
        grid_spec=pltpu.PrefetchScalarGridSpec(
            num_scalar_prefetch=len(scalars),
            grid=(grid,),
            in_specs=[spec_of(spec) for _, spec in ins]
            + [pl.BlockSpec(memory_space=pl.ANY) for _ in after],
            out_specs=[spec_of(out[2]) for out in outs],
            scratch_shapes=list(scratch),
        ),
        out_shape=[
            (pltpu.VMEM if kept else pltpu.HBM)(shape, kind)
            for shape, kind, _, *kept in outs
        ],
        compiler_params=pltpu.CompilerParams(vmem_limit_bytes=room << 20),
        cost_estimate=pl.CostEstimate(flops=flops, bytes_accessed=moved, transcendentals=0),
    )(
        *scalars,
        *[placed(array, any(array is free for free in anywhere)) for array, _ in ins],
        *after,
    )
    return [
        pltpu.with_memory_space_constraint(array, pltpu.VMEM) if out[3:] else array
        for array, out in zip(made, outs)
    ]


def rows_of(block, columns):
    return pl.BlockSpec((block, columns), lambda i: (i, 0))


def fixed(shape, place=None):
    place = (0,) * len(shape) if place is None else place
    return pl.BlockSpec(shape, lambda i: place, pipeline_mode=pl.Buffered(1))


def all_of(array):
    return (array, fixed(array.shape))


def out_all(shape, kind):
    return (shape, kind, fixed(shape))


def near(out):
    return (*out, True)


def placed(array, anywhere):
    if anywhere or jax.typeof(array).memory_space == pltpu.VMEM:
        return array
    return pltpu.with_memory_space_constraint(array, pltpu.HBM)


def attend(queries, hot, keys_ref, values_ref, count, causal):
    rows = queries.shape[0]
    heads = queries.shape[1] // HEAD
    lane = lax.broadcasted_iota(jnp.int32, (rows, LANES), 1)
    logs = jnp.zeros((rows, LANES), FULL)
    if causal:
        query, key = later_keys(rows, rows)
        ahead = jnp.where(key <= query, 0.0, FAR)

    def scores_of(head):
        columns = slice(head // 2 * LANES, (head // 2 + 1) * LANES)
        asked = jnp.concatenate([one_head(queries[:, columns], head % 2), hot], axis=1)
        scores = nt(asked, keys_ref[head // 2, :count, :])
        if not causal:
            return scores
        if count == rows:
            return scores + ahead
        return jnp.concatenate(
            [scores[:, : count - rows], scores[:, count - rows :] + ahead], axis=1
        )

    mixed = []
    following = scores_of(0)
    for head in range(heads):
        scores = following
        if head + 1 < heads:
            following = scores_of(head + 1)
        columns = slice(head // 2 * LANES, (head // 2 + 1) * LANES)
        top = jnp.max(scores, axis=1, keepdims=True)
        weights = jnp.exp(scores - top)
        amount = jnp.sum(weights, axis=1, keepdims=True)
        low = (weights * (1.0 / amount)).astype(LOW)
        here = nn(low, values_ref[:count, columns])
        if head % 2:
            mixed.append(jnp.where(lane < HEAD, other, here))
        other = here
        logs = jnp.where(lane == head, top + jnp.log(amount), logs)
    return jnp.concatenate(mixed, axis=1), logs.T[:heads]


def keep_keys(keys_ref, place, keys, hot):
    pairs = keys.shape[1] // LANES
    for pair in range(pairs):
        keys_ref[pair, place, :LANES] = keys[:, pair * LANES : (pair + 1) * LANES]
        keys_ref[pair, place, LANES:] = hot


def self_forward(
    tokens, hot, far, gate, w_in, w_out, bias_columns, w_query,
    projected, mixed, logs, first, first_low, cross_queries, keys, values, bias,
):
    step = pl.program_id(0)
    rows, d = tokens.shape

    @pl.when(step == 0)
    def _():
        bias[...] = bias_columns[...].astype(FULL).T[:8]

    joined_bias = jnp.concatenate([bias[0:1, :], jnp.zeros((1, d), FULL), bias[1:2, :]], axis=1)
    made = (nn(tokens[...], w_in[...]) + joined_bias).astype(LOW)
    projected[...] = made
    place = pl.ds(pl.multiple_of(step * rows, rows), rows)
    keep_keys(keys, place, made[:, d : 2 * d], far[...])
    values[place, :] = made[:, 2 * d :]
    part = min(rows, 256)
    for block in range(values.shape[0] // rows):

        @pl.when(step == block)
        def _(before=block * rows):
            scaled = made[:, :d] * jnp.asarray(HEAD**-0.5, LOW)
            for start in range(0, rows, part):
                here = slice(start, start + part)
                mixed[here, :], logs[:, here] = attend(
                    scaled[here, :], hot[here, :], keys, values, before + start + part, True
                )

    branch = nt(mixed[...].astype(LOW), w_out[...]) + bias[2:3, :]
    total = tokens[...].astype(FULL) + gate[...] * branch
    first[...] = total
    first_low[...] = total.astype(LOW)
    cross_queries[...] = (nn(total.astype(LOW), w_query[...]) + bias[3:4, :]).astype(LOW)


def self_forward_joining(
    bits, self_mine, self_got, cross_mine, cross_got, tokens, hot, far, gate, *refs
):
    *outs, self_whole, cross_whole, keys, values, bias, self_here, cross_here, sent = refs
    d = tokens.shape[1]
    own = self_mine.shape[-2]
    copies = [
        pltpu.make_async_copy(self_here, self_whole, sent.at[0]),
        pltpu.make_async_copy(cross_here, cross_whole, sent.at[1]),
    ]

    @pl.when(pl.program_id(0) == 0)
    def _():
        for here, *halves in (
            (self_here, self_mine, self_got), (cross_here, cross_mine, cross_got)
        ):
            for index in range(self_mine.shape[0]):
                for core, half in zip((bits[0], 1 - bits[0]), halves):
                    start = pl.multiple_of((2 * index + core) * own, own)
                    here[pl.ds(start, own), :] = half[index]
        for copy in copies:
            copy.start()

    self_forward(
        tokens, hot, far, gate, self_here.at[:, : 3 * d], self_here.at[:, 3 * d : 4 * d],
        self_here.at[:, 4 * d :], cross_here.at[:, 2 * d : 3 * d], *outs, keys, values, bias,
    )

    @pl.when(pl.program_id(0) == pl.num_programs(0) - 1)
    def _():
        for copy in copies:
            copy.wait()


def cross_forward(
    queries, memory, hot, far, gate, first, w_kv, w_out, bias_columns,
    memory_kv, mixed, logs, second, keys, bias,
):
    d = memory.shape[1]

    @pl.when(pl.program_id(0) == 0)
    def _():
        bias[...] = bias_columns[...].astype(FULL).T[:8]
        made = nn(memory[...], w_kv[...])
        memory_kv[:, :d] = made[:, :d].astype(LOW)
        memory_kv[:, d:] = (made[:, d:] + bias[4:5, :]).astype(LOW)
        keep_keys(keys, slice(None), memory_kv[:, :d], far[...])

    scaled = queries[...] * jnp.asarray(HEAD**-0.5, LOW)
    mixed[...], logs[...] = attend(
        scaled, hot[...], keys, memory_kv.at[:, d:], memory.shape[0], False
    )
    branch = nt(mixed[...].astype(LOW), w_out[...]) + bias[5:6, :]
    second[...] = first[...] + gate[...] * branch


def head_sums(left, right):
    d = left.shape[1]
    head = lax.broadcasted_iota(jnp.int32, (d // HEAD, d), 0)
    column = lax.broadcasted_iota(jnp.int32, (d // HEAD, d), 1)
    chosen = (column // HEAD == head).astype(LOW)
    product = left.astype(FULL) * right.astype(FULL)
    high = product.astype(LOW)
    rest = product - high.astype(FULL)
    middle = rest.astype(LOW)
    last = (rest - middle.astype(FULL)).astype(LOW)
    return nt(chosen, high) + nt(chosen, middle) + nt(chosen, last)


def gelu_both(z):
    c = 0.7978845608028654
    square = z * z
    bent = jnp.tanh(c * z * (1.0 + 0.044715 * square))
    half = 0.5 * (1.0 + bent)
    slope = half + 0.5 * z * (1.0 - bent * bent) * (c * (1.0 + 3.0 * 0.044715 * square))
    return z * half, slope


def spread(d, ff):
    each = ff // d
    row = lax.broadcasted_iota(jnp.int32, (d, ff), 0)
    entry = lax.broadcasted_iota(jnp.int32, (d, ff), 1)
    column = lax.broadcasted_iota(jnp.int32, (LANES, ff), 0)
    there = lax.broadcasted_iota(jnp.int32, (LANES, ff), 1)
    return entry // each == row, (there % each + FIRST == column).astype(LOW)


def columns_to_row(columns, ff):
    owner, place = spread(columns.shape[0], ff)
    return jnp.sum(jnp.where(owner, nn(columns, place), 0.0), axis=0, keepdims=True)


def row_to_columns(row, d):
    owner, place = spread(d, row.shape[1])
    return nt(jnp.where(owner, row, 0.0).astype(LOW), place).astype(LOW)


def rows_to_columns(*rows):
    d = rows[0].shape[1]
    stack = jnp.concatenate([*rows, jnp.zeros((LANES - len(rows), d), FULL)], axis=0)
    return stack.T.astype(LOW)


def feed_both(
    second, upstream, gate, mixed, w_in, w_out, w_cross_out, bias_columns,
    output, second_grad, mixed_grad, deltas, feed_grad, sums,
    second_low, signal_all, hidden_all, before_all, cross_all, mixed_all, bias, bias_in, bias_in_grad,
    *, inner, own,
):
    step = pl.program_id(0)
    rows, d = second.shape
    ff = w_in.shape[1]
    place = pl.ds(pl.multiple_of(step * rows, rows), rows)
    low = second[...].astype(LOW)
    second_low[place, :] = low
    mixed_all[place, :] = mixed[...].astype(LOW)
    given = upstream[...].astype(FULL)
    signal = (gate[...] * given).astype(LOW)
    signal_all[place, :] = signal

    @pl.when(step == 0)
    def _():
        bias[...] = bias_columns[...].astype(FULL).T[:8]
        bias_in[...] = columns_to_row(bias_columns[...], ff)
        bias_in_grad[...] = jnp.zeros_like(bias_in_grad)
        sums[...] = jnp.zeros_like(sums)

    made = bias[6:7, :]
    back = given
    width = 1024
    parts = [slice(start, start + width) for start in range(0, ff, width)]
    products = lambda part: (nn(low, w_in[:, part]) + bias_in[:, part], nn(signal, w_out[:, part]))
    following = products(parts[0])
    for index, part in enumerate(parts):
        before, hidden_back = following
        if index + 1 < len(parts):
            following = products(parts[index + 1])
        hidden, slope = gelu_both(before)
        hidden = hidden.astype(LOW)
        hidden_all[place, part] = hidden
        before_grad = (hidden_back * slope).astype(LOW)
        before_all[place, part] = before_grad
        bias_in_grad[:, part] += column_sum(before_grad)
        made = made + nt(hidden, w_out[:, part])
        back = back + nt(before_grad, w_in[:, part])
    output[...] = (second[...] + gate[...] * made).astype(LOW)
    second_grad[...] = back
    crossed = (gate[...] * back).astype(LOW)
    cross_all[place, :] = crossed
    mixed_back = nn(crossed, w_cross_out[...]).astype(LOW)
    mixed_grad[...] = mixed_back
    deltas[...] = head_sums(mixed_back, mixed[...])
    sums[0:1, :] += column_sum(signal)
    sums[1:2, :] += column_sum(crossed)

    @pl.when(step == pl.num_programs(0) - 1)
    def _():
        def keep(start, grad):
            end = start + grad.shape[1]
            outer = d // own // inner
            for owner in range(inner * outer if inner > 1 else 0):
                to = (owner % inner * outer + owner // inner) * own
                feed_grad[to : to + own, start:end] = grad[owner * own : (owner + 1) * own]
            if inner == 1:
                feed_grad[:, start:end] = grad

        for part in parts:
            keep(part.start, tn(second_low[...], before_all[:, part]).astype(LOW))
            keep(ff + part.start, tn(signal_all[...], hidden_all[:, part]).astype(LOW))
        keep(2 * ff, tn(cross_all[...], mixed_all[...]).astype(LOW))
        at = 2 * ff + d
        keep(at, rows_to_columns(sums[0:1, :]))
        keep(at + LANES, row_to_columns(bias_in_grad[...], d))


def column_sum(array):
    return jnp.sum(array.astype(FULL), axis=0, keepdims=True)


def attend_back(
    queries, keys, values, hot, far, mixed_grad, logs, deltas, pair,
    query_grad, key_grad, value_grad, key_sum, value_sum, reached, causal, block=256,
):
    count = keys.shape[0]
    reached[:, :LANES] = keys[...]
    reached[:, LANES:] = far[...]
    turned = keys[...].T
    if causal:
        key, query = later_keys(block, block)
        ahead = jnp.where(key <= query, 0.0, FAR)
    items = [
        (start, odd) for start in range(queries.shape[0] - block, -1, -block) for odd in range(2)
    ]

    def products(item):
        start, odd = item
        place = slice(start, start + block)
        reach = start + block if causal else count
        asked = one_head(queries[place, :], odd) * jnp.asarray(HEAD**-0.5, LOW)
        incoming = one_head(mixed_grad[place, :], odd)
        scores = nt(reached[:reach, :], jnp.concatenate([asked, hot[place, :]], axis=1))
        if causal and start:
            scores = jnp.concatenate([scores[:start], scores[start:] + ahead], axis=0)
        elif causal:
            scores = scores + ahead
        return scores, nt(values[:reach, :], incoming), asked, incoming, place, reach

    following = products(items[0])
    for index, (start, odd) in enumerate(items):
        scores, pushed, asked, incoming, place, reach = following
        if index + 1 < len(items):
            following = products(items[index + 1])
        head = pl.ds(2 * pair + odd, 1)
        chances = jnp.exp(scores - logs[head, place])
        score_grad = (chances * (pushed - deltas[head, place])).astype(LOW)
        turned_grad = nn(turned[odd * HEAD : (odd + 1) * HEAD, :reach], score_grad)
        value_part = nn(chances.astype(LOW), incoming)
        key_part = nn(score_grad, asked)
        if index == 0:
            value_sum[...] = value_part
            key_sum[...] = key_part
        else:
            value_sum[:reach, :] += value_part
            key_sum[:reach, :] += key_part
        if odd:
            both = jnp.concatenate([other, turned_grad], axis=0) * HEAD**-0.5
            query_grad[place, :] = both.T.astype(LOW)
        other = turned_grad
    key_grad[...] = key_sum[...].astype(LOW)
    value_grad[...] = value_sum[...].astype(LOW)


def cross_back(
    bits, queries, keys, values, hot, far, in_grad, logs, cross_deltas, sums,
    first, second_grad, memory, self_mixed, gate, weights, self_weights,
    *outs,
):
    (
        *owned, key_grad, value_grad, first_grad, mixed_grad, deltas,
        key_sum, value_sum, reached, signals, first_here, second_here, memory_here, mixed_here,
        w_query, w_out, grads, arrived,
    ) = outs
    pair = pl.program_id(0)
    d = memory.shape[1]
    copies = [
        pltpu.make_async_copy(source, target, arrived.at[index])
        for index, (source, target) in enumerate(
            [
                (first, first_here), (second_grad, second_here), (memory, memory_here),
                (self_mixed, mixed_here), (weights.at[:, 2 * d : 3 * d], w_query),
                (self_weights.at[:, 3 * d : 4 * d], w_out),
            ]
        )
    ]

    @pl.when(pair == 0)
    def _():
        for copy in copies:
            copy.start()

    attend_back(
        queries, keys, values, hot, far, in_grad, logs, cross_deltas, pair,
        signals.at[0, pair], signals.at[1, pair], signals.at[2, pair],
        key_sum, value_sum, reached, False,
    )
    key_grad[...] = signals[1, pair]
    value_grad[...] = signals[2, pair]

    @pl.when(pair == pl.num_programs(0) - 1)
    def _():
        for copy in copies:
            copy.wait()
        pairs = signals.shape[1]
        query_signal, key_signal, value_signal = (
            jnp.concatenate([signals[which, place] for place in range(pairs)], axis=1)
            for which in range(3)
        )
        back = second_here[...] + nt(query_signal, w_query[...])
        first_grad[...] = back
        signal = (gate[...] * back).astype(LOW)
        mixed_back = nn(signal, w_out[...]).astype(LOW)
        mixed_grad[...] = mixed_back
        deltas[...] = head_sums(mixed_back, mixed_here[...])
        grads[:, :d] = tn(memory_here[...], key_signal).astype(LOW)
        grads[:, d : 2 * d] = tn(memory_here[...], value_signal).astype(LOW)
        grads[:, 2 * d : 3 * d] = tn(first_here[...], query_signal).astype(LOW)
        grads[:, 3 * d : 4 * d] = tn(signal, mixed_here[...].astype(LOW)).astype(LOW)
        grads[:, 4 * d :] = rows_to_columns(
            column_sum(query_signal), column_sum(value_signal), sums[1:2, :], column_sum(signal)
        )
        if len(owned) == 2:
            part_by_core(bits, grads, *owned)
        else:
            owned[0][...] = grads[...]


def self_back(
    bits, queries, keys, values, hot, far, in_grad, logs, deltas, tokens, *rest, before, ending
):
    if ending:
        earlier, earlier_sums, *rest = rest
    *owned, query_grad, key_grad, value_grad, key_sum, value_sum, reached, signals, grads = rest
    step = pl.program_id(0)
    pairs = signals.shape[1]
    wide = pairs * LANES
    attend_back(
        queries, keys, values, hot, far, in_grad, logs, deltas, before + step,
        signals.at[0, step], signals.at[1, step], signals.at[2, step],
        key_sum, value_sum, reached, True,
    )
    query_grad[...] = signals[0, step]
    key_grad[...] = signals[1, step]
    value_grad[...] = signals[2, step]

    @pl.when(step == pl.num_programs(0) - 1)
    def _():
        at = 3 * wide if ending else 0
        if ending:
            grads[:, :at] = earlier[...]
        added = []
        for which in range(3):
            part = jnp.concatenate([signals[which, place] for place in range(pairs)], axis=1)
            grads[:, at + which * wide : at + (which + 1) * wide] = tn(
                tokens[...], part
            ).astype(LOW)
            if which != 1:
                added.append(column_sum(part))
        if not ending:
            owned[0][...] = grads[...]
            owned[1][0:1, :] = added[0]
            owned[1][1:2, :] = added[1]
            return
        grads[:, 2 * at :] = rows_to_columns(
            *[
                jnp.concatenate([earlier_sums[row : row + 1, :], added[row]], axis=1)
                for row in range(2)
            ]
        )
        if len(owned) == 2:
            part_by_core(bits, grads, *owned)
        else:
            owned[0][...] = grads[...]


def part_by_core(bits, grads, keep, away):
    own = keep.shape[1]
    for core in range(2):

        @pl.when(bits[0] == core)
        def _(core=core):
            for slab in range(2 * keep.shape[0]):
                there = keep if slab % 2 == core else away
                there[slab // 2] = grads[slab * own : (slab + 1) * own, :]


def memory_back(key_signal, value_signal, w_kv, memory_grad):
    d = key_signal.shape[1]
    memory_grad[...] = nt(key_signal[...], w_kv[:, :d]) + nt(value_signal[...], w_kv[:, d:])


def tokens_back(first_grad, w_in, *refs):
    *signals, tokens_grad = refs
    d = first_grad.shape[1]
    total = first_grad[...]
    wide = signals[0].shape[1]
    for index, signal in enumerate(signals):
        start = index % 3 * d + index // 3 * wide
        total = total + nt(signal[...], w_in[:, start : start + wide])
    tokens_grad[...] = total


def sum_to_owners(grads, device_count, orders):
    me = lax.axis_index(AXES)
    bits = device_count.bit_length() - 1
    running = []
    for grad in grads:
        rows, columns = grad.shape
        running.append(grad.reshape((2,) * bits + (rows // device_count, columns)))
    left = [list(range(bits)) for _ in grads]
    for step in range(bits):
        sent = []
        for part, order in enumerate(orders):
            bit = order[step]
            axis = len(left[part]) - 1 - left[part].index(bit)
            mine = (me >> bit) & 1
            away = lax.dynamic_index_in_dim(running[part], 1 - mine, axis, keepdims=False)
            pairs = [(i, i ^ (1 << bit)) for i in range(device_count)]
            sent.append((axis, mine, lax.ppermute(away.astype(LOW), AXES, pairs)))
            left[part].remove(bit)
        for part, (axis, mine, got) in enumerate(sent):
            kept = lax.dynamic_index_in_dim(running[part], mine, axis, keepdims=False)
            running[part] = kept.astype(FULL) + got.astype(FULL)
    return running


def swap(array, bit, device_count):
    return lax.ppermute(array, AXES, [(i, i ^ (1 << bit)) for i in range(device_count)])


def scatter_rows(grad, device_count):
    bits = device_count.bit_length() - 1
    high = list(range(1, bits))[::-1]
    half = grad.shape[1] // 256 * 128
    orders = ([0] + high, [0, high[1], high[0]] + high[2:])
    return jnp.concatenate(
        sum_to_owners([grad[:, :half], grad[:, half:]], device_count, orders), axis=1
    )


def swap(array, change, device_count):
    return lax.ppermute(array, AXES, [(i, i ^ change) for i in range(device_count)])


def picked(terms, first, second):
    total = None
    for term in terms:
        for place in (first, second):
            term = lax.dynamic_index_in_dim(term, place, 0, keepdims=False)
        total = term.astype(FULL) if total is None else total + term.astype(FULL)
    return total


class Halving:
    changes = ((0, 1), (1, 0), (1, 1))

    def __init__(self, me, keep, away, device_count):
        self.count = device_count
        self.x, self.y = (me >> 3) & 1, (me >> 4) & 1
        self.low, self.high = (me >> 1) & 1, (me >> 2) & 1
        shape = (2, 2, 4, *keep.shape[1:])
        self.terms = [keep.reshape(shape)]
        self.got = [swap(away.reshape(shape), 1, device_count)]

    def plane(self):
        terms = self.terms + self.got
        self.sent = [picked(terms, self.y ^ y, self.x ^ x).astype(LOW) for y, x in self.changes]
        self.got = [
            swap(array, 8 * x + 16 * y, self.count)
            for array, (y, x) in zip(self.sent, self.changes)
        ]
        self.terms = [
            lax.dynamic_index_in_dim(
                lax.dynamic_index_in_dim(term, self.y, 0, keepdims=False), self.x, 0, keepdims=False
            )
            for term in terms
        ]

    def line(self):
        terms = [term.reshape(2, 2, *term.shape[1:]) for term in self.terms + self.got]
        self.sent = [
            picked(terms, self.high ^ high, self.low ^ low).astype(LOW)
            for high, low in self.changes
        ]
        self.kept = picked(terms, self.high, self.low)

    def send_line(self, *after):
        self.sent = list(lax.optimization_barrier((*self.sent, *after))[: len(self.sent)])
        self.got = [
            swap(array, 2 * low + 4 * high, self.count)
            for array, (high, low) in zip(self.sent, self.changes)
        ]

    def wait_for(self, *arrays):
        self.got = list(lax.optimization_barrier((*self.got, *arrays))[: len(self.got)])


def total_of(keep, *got):
    total = keep[...]
    for part in got:
        total = total + part[...].astype(FULL)
    return total


def cross_last(*refs):
    *parts, kv, query, self_out, cross_bias, self_bias = refs
    total = total_of(*parts)
    d = query.shape[1]
    kv[...] = total[:, : 2 * d]
    query[...] = total[:, 2 * d : 3 * d]
    self_out[...] = total[:, 3 * d : 4 * d]
    turned = turned_bias(total[:, 4 * d :])
    cross_bias[...] = turned[0:3]
    self_bias[...] = turned[3:4]


def turned_bias(columns):
    own = columns.shape[0]
    square = jnp.concatenate([columns, jnp.zeros((LANES - own, LANES), FULL)], axis=0)
    return square.T[:8, :own]


def self_last(third, *refs):
    *parts, self_in, bias = refs
    total = total_of(*parts)
    columns = self_in.shape[1]
    half = columns // 2
    wide = half // 3
    for call_index in range(2):
        for which in range(3):
            at = call_index * half + which * wide
            to = which * 2 * wide + call_index * wide
            self_in[:, to : to + wide] = total[:, at : at + wide]
    bias[0:2, :] = turned_bias(total[:, columns:])[0:2]
    bias[2:3, :] = third[...]


def feed_last(total, feed_in, feed_out, cross_out, bias_out, bias_in):
    ff = feed_in.shape[1]
    at = 2 * ff + cross_out.shape[1]
    feed_in[...] = total[:, :ff].astype(FULL)
    feed_out[...] = total[:, ff : 2 * ff].astype(FULL)
    cross_out[...] = total[:, 2 * ff : at].astype(FULL)
    bias_out[...] = turned_bias(total[:, at : at + LANES].astype(FULL))[0:1]
    bias_in[...] = columns_to_row(total[:, at + LANES :], bias_in.shape[1])


def pack(
    self_in, self_out, cross_query, cross_kv, cross_out, feed_in, feed_out, self_bias, cross_bias,
    bias_out, bias_in, near, own_feed,
):
    d = self_out.shape[1]
    ff = feed_in.shape[1]
    own = self_in.shape[0]
    near[:, : 3 * d] = self_in[...].astype(LOW)
    near[:, 3 * d : 4 * d] = self_out[...].astype(LOW)
    rows = jnp.concatenate(
        [self_bias[...], cross_bias[...], bias_out[...], jnp.zeros((LANES - 7, own), FULL)], axis=0
    )
    wide = jnp.concatenate([rows, jnp.zeros((LANES, LANES - own), FULL)], axis=1)
    at = 4 * d + LANES
    near[:, 4 * d : at] = wide.T[:own].astype(LOW) + row_to_columns(bias_in[...], own)
    near[:, at : at + 2 * d] = cross_kv[...].astype(LOW)
    near[:, at + 2 * d : at + 3 * d] = cross_query[...].astype(LOW)
    near[:, at + 3 * d :] = cross_out[...].astype(LOW)
    own_feed[:, :ff] = feed_in[...].astype(LOW)
    own_feed[:, ff:] = feed_out[...].astype(LOW)


def marks(seq_lengths, memory_lengths, residual_gate, hot, self_far, memory_far, gate):
    slots = seq_lengths.shape[0]
    lane = lax.broadcasted_iota(jnp.int32, hot.shape, 1)

    def numbered(lengths, padding):
        position = lax.broadcasted_iota(jnp.int32, hot.shape, 0)
        end = lengths[0]
        number = jnp.where(position >= end, 1, 0)
        for slot in range(1, slots):
            end = end + lengths[slot]
            number = number + jnp.where(position >= end, 1, 0)
        present = position < end
        return jnp.where(present, number, padding), present

    ids, present = numbered(seq_lengths, slots)
    hot[...] = jnp.where(ids == lane, 1.0, 0.0).astype(LOW)
    self_far[...] = jnp.where(ids == lane, 0.0, FAR).astype(LOW)
    gate[...] = jnp.where(present[:, :1], residual_gate[0], 0.0)
    ids, _ = numbered(memory_lengths, slots + 1)
    memory_far[...] = jnp.where(ids == lane, 0.0, FAR).astype(LOW)


def gather_near(near, cut, device_count, after):
    me = lax.axis_index(AXES)
    others = [swap(near, 2 * change, device_count) for change in (1, 2, 3)]
    others = lax.optimization_barrier((*others, after))[:3]
    first, second, third, fourth = near, *others
    odd = jnp.where(
        (me >> 1) & 1,
        jnp.stack([second, first, fourth, third]),
        jnp.stack([first, second, third, fourth]),
    )
    line = jnp.where((me >> 2) & 1, jnp.concatenate([odd[2:], odd[:2]]), odd)
    held = [line[..., :cut], line[..., cut:]]
    known = [[1, 1], [1, 1]]
    for bits in ((3, 4), (4, 3)):
        got = [swap(array, 1 << bit, device_count) for array, bit in zip(held, bits)]
        for part, bit in enumerate(bits):
            axis = sum(other > bit for other in known[part])
            low = jnp.stack([held[part], got[part]], axis)
            high = jnp.stack([got[part], held[part]], axis)
            held[part] = jnp.where((me >> bit) & 1, high, low)
            known[part].append(bit)
    mine = [array.reshape(-1, *array.shape[-2:]) for array in held]
    return [(array, swap(array, 1, device_count)) for array in mine]


def on_device(
    tokens, memory, out_cotangent, seq_lengths, memory_lengths, residual_gate,
    self_in, self_out, self_bias, cross_query, cross_key_value, cross_out, cross_bias,
    feed_in, feed_out, feed_bias_in, feed_bias_out,
):
    device_count = lax.axis_size(AXES)
    count, d = tokens.shape
    key_count = memory.shape[0]
    ff = feed_in.shape[1]
    own = self_in.shape[0]
    pairs = d // LANES
    heads = d // HEAD
    block = 512
    steps = count // block
    halving = lax.axis_size("dp") == 4 and lax.axis_size("fsdp") == 8
    me = lax.axis_index(AXES)
    bits = (me & 1).astype(jnp.int32)[None]
    cut = 4 * d + LANES
    own_near, own_feed = call(
        pack,
        "pack",
        1,
        [
            all_of(array)
            for array in (
                self_in, self_out.T, cross_query, cross_key_value, cross_out.T, feed_in,
                feed_out.T, self_bias, cross_bias, feed_bias_out[None], feed_bias_in[None],
            )
        ],
        [out_all((own, cut + 4 * d), LOW), out_all((own, 2 * ff), LOW)],
    )
    hot, self_far, memory_far, gate = call(
        marks,
        "marks",
        1,
        [],
        [out_all((count, LANES), LOW), out_all((count, LANES), LOW),
         out_all((key_count, LANES), LOW), out_all((count, 1), FULL)],
        scalars=(seq_lengths[0], memory_lengths[0], residual_gate),
    )
    feed_whole = lax.all_gather(own_feed, AXES, axis=0, tiled=True)
    if halving:
        (self_mine, self_got), (cross_mine, cross_got) = gather_near(own_near, cut, device_count, gate)
    else:
        self_whole = lax.all_gather(own_near[:, :cut], AXES, axis=0, tiled=True)
        cross_whole = lax.all_gather(own_near[:, cut:], AXES, axis=0, tiled=True)
    each = lambda array: (array, rows_of(block, array.shape[1]))
    out_rows = lambda columns, kind: ((count, columns), kind, rows_of(block, columns))
    out_heads = ((heads, count), FULL, pl.BlockSpec((heads, block), lambda i: (0, i)))

    self_outs = [
        out_rows(3 * d, LOW), out_rows(d, FULL), out_heads, near(out_rows(d, FULL)),
        out_rows(d, LOW), out_rows(d, LOW),
    ]
    self_room = [
        pltpu.VMEM((pairs, count, 2 * LANES), LOW), pltpu.VMEM((count, d), LOW),
        pltpu.VMEM((8, d), FULL),
    ]
    if halving:
        there = pl.BlockSpec(memory_space=pl.ANY)
        halves = (self_mine, self_got, cross_mine, cross_got)
        (
            projected, self_mixed, self_logs, first, first_low, cross_queries,
            self_whole, cross_whole,
        ) = call(
            self_forward_joining,
            "self_forward",
            steps,
            [all_of(array) for array in halves]
            + [each(tokens), each(hot), each(self_far), each(gate)],
            self_outs + [((d, cut), LOW, there), ((d, 4 * d), LOW, there)],
            self_room
            + [pltpu.VMEM((d, cut), LOW), pltpu.VMEM((d, 4 * d), LOW),
               pltpu.SemaphoreType.DMA((2,))],
            flops=15 << 30, moved=8 << 20, scalars=(bits,), anywhere=halves,
        )
    w_self_in = (self_whole, fixed((d, 3 * d), (0, 0)))
    w_self_out = (self_whole, fixed((d, d), (0, 3)))
    bias_columns = (self_whole, fixed((d, LANES), (0, 4 * d // LANES)))
    w_kv = (cross_whole, fixed((d, 2 * d), (0, 0)))
    w_query = (cross_whole, fixed((d, d), (0, 2)))
    w_cross_out = (cross_whole, fixed((d, d), (0, 3)))
    w_feed_in = (feed_whole, fixed((d, ff), (0, 0)))
    w_feed_out = (feed_whole, fixed((d, ff), (0, 1)))

    if not halving:
        projected, self_mixed, self_logs, first, first_low, cross_queries = call(
            self_forward,
            "self_forward",
            steps,
            [each(tokens), each(hot), each(self_far), each(gate), w_self_in, w_self_out,
             bias_columns, w_query],
            self_outs,
            self_room,
            flops=15 << 30, moved=8 << 20,
        )
    memory_kv, cross_mixed, cross_logs, second = call(
        cross_forward,
        "cross_forward",
        steps,
        [each(cross_queries), all_of(memory), each(hot), all_of(memory_far), each(gate),
         each(first), w_kv, w_cross_out, bias_columns],
        [out_all((key_count, 2 * d), LOW), near(out_rows(d, FULL)), near(out_heads),
         out_rows(d, FULL)],
        [pltpu.VMEM((pairs, key_count, 2 * LANES), LOW), pltpu.VMEM((8, d), FULL)],
        flops=20 << 30, moved=8 << 20,
    )
    inner = lax.axis_size("fsdp") if halving else 1
    output, second_grad, cross_mixed_grad, cross_deltas, feed_grad, feed_sums = call(
        functools.partial(feed_both, inner=inner, own=own),
        "feed_both",
        steps,
        [each(second), each(out_cotangent), each(gate), each(cross_mixed), w_feed_in, w_feed_out,
         w_cross_out, bias_columns],
        [out_rows(d, LOW), out_rows(d, FULL), out_rows(d, LOW), near(out_heads),
         out_all((d, 2 * ff + d + 2 * LANES), LOW), near(out_all((8, d), FULL))],
        [pltpu.VMEM((count, d), LOW), pltpu.VMEM((count, d), LOW), pltpu.VMEM((count, ff), LOW),
         pltpu.VMEM((count, ff), LOW), pltpu.VMEM((count, d), LOW), pltpu.VMEM((count, d), LOW),
         pltpu.VMEM((8, d), FULL), pltpu.VMEM((1, ff), FULL), pltpu.VMEM((1, ff), FULL)],
        flops=25 << 30, moved=16 << 20,
    )
    ways = ("fsdp", "dp") if halving else ("dp", "fsdp")
    feed_total = lax.psum_scatter(feed_grad, ways[0], scatter_dimension=0, tiled=True)

    def pair_columns(array, start, width=LANES):
        return (array, pl.BlockSpec((array.shape[0], width), lambda i: (0, start + i)))

    def out_pairs(rows, columns):
        return ((rows, columns), LOW, pl.BlockSpec((rows, LANES), lambda i: (0, i)))

    def owned(columns):
        if halving:
            return [out_all((device_count // 2, own, columns), LOW)] * 2
        return [out_all((d, columns), LOW)]

    def pair_room(rows, steps):
        return [
            pltpu.VMEM((rows, LANES), FULL), pltpu.VMEM((rows, LANES), FULL),
            pltpu.VMEM((rows, 2 * LANES), LOW), pltpu.VMEM((3, steps, rows, LANES), LOW),
        ]

    left_there = lambda array: (array, pl.BlockSpec(memory_space=pl.ANY))
    cross_columns = 4 * d + LANES
    *cross_owned, key_signal, value_signal, first_grad, self_mixed_grad, self_deltas = call(
        cross_back,
        "cross_back",
        pairs,
        [pair_columns(cross_queries, 0), pair_columns(memory_kv, 0),
         pair_columns(memory_kv, pairs), all_of(hot), all_of(memory_far),
         pair_columns(cross_mixed_grad, 0), all_of(cross_logs), all_of(cross_deltas),
         all_of(feed_sums), left_there(first_low), left_there(second_grad), left_there(memory),
         left_there(self_mixed), all_of(gate), left_there(cross_whole), left_there(self_whole)],
        owned(cross_columns)
        + [out_pairs(key_count, d), out_pairs(key_count, d), out_all((count, d), FULL),
           near(out_all((count, d), LOW)), near(out_all((heads, count), FULL))],
        pair_room(key_count, pairs)
        + [pltpu.VMEM((count, d), LOW), pltpu.VMEM((count, d), FULL),
           pltpu.VMEM((key_count, d), LOW), pltpu.VMEM((count, d), FULL),
           pltpu.VMEM((d, d), LOW), pltpu.VMEM((d, d), LOW),
           pltpu.VMEM((d, cross_columns), LOW), pltpu.SemaphoreType.DMA((6,))],
        flops=30 << 30, moved=24 << 20, scalars=(bits,),
    )
    if halving:
        cross_sum = Halving(me, *cross_owned, device_count)

    half = pairs // 2
    self_columns = 3 * d + LANES

    def self_part(before, ending, outs, earlier=(), after=()):
        wide = half * LANES
        columns = self_columns if ending else 3 * wide
        return call(
            functools.partial(self_back, before=before, ending=ending),
            "self_back",
            half,
            [pair_columns(projected, before), pair_columns(projected, pairs + before),
             pair_columns(projected, 2 * pairs + before), all_of(hot), all_of(self_far),
             pair_columns(self_mixed_grad, before), all_of(self_logs), all_of(self_deltas),
             all_of(tokens)]
            + [all_of(array) for array in earlier],
            outs + [out_pairs(count, wide)] * 3,
            pair_room(count, half) + [pltpu.VMEM((d, columns), LOW)],
            flops=12 << 30, moved=8 << 20, scalars=(bits,), after=after,
        )

    wide = half * LANES
    *earlier, query_one, key_one, value_one = self_part(
        0, False, [out_all((d, 3 * wide), LOW), out_all((8, wide), FULL)]
    )
    after = ()
    if halving:
        cross_sum.wait_for(query_one)
        cross_sum.plane()
        after = tuple(cross_sum.sent)
    *self_owned, query_two, key_two, value_two = self_part(
        half, True, owned(self_columns), earlier, after
    )
    after = ()
    if halving:
        cross_sum.wait_for(query_two)
        feed_total, _ = lax.optimization_barrier((feed_total, cross_sum.got[0]))
    feed_total = lax.psum_scatter(feed_total, ways[1], scatter_dimension=0, tiled=True)
    if halving:
        self_sum = Halving(me, *self_owned, device_count)
        cross_sum.line()
        self_sum.wait_for(*cross_sum.sent)
        self_sum.plane()
        cross_sum.send_line(*self_sum.sent)
        after = tuple(self_sum.sent)
    tokens_grad, = call(
        tokens_back,
        "tokens_back",
        steps,
        [each(first_grad), w_self_in]
        + [each(array) for array in (query_one, key_one, value_one, query_two, key_two, value_two)],
        [out_rows(d, FULL)],
        flops=3 << 30, moved=8 << 20, after=after,
    )
    memory_grad, = call(
        memory_back,
        "memory_back",
        steps,
        [each(key_signal), each(value_signal), w_kv],
        [((key_count, d), FULL, rows_of(block, d))],
        flops=2 << 30, moved=5 << 20, after=after,
    )
    if halving:
        self_sum.wait_for(tokens_grad, memory_grad)
        self_sum.line()
        self_sum.send_line()
        cross_sum.wait_for(*self_sum.sent)
        ends = [(cross_sum.kept, *cross_sum.got), (self_sum.kept, *self_sum.got)]
    else:
        ends = [(scatter_rows(grads[0], device_count),) for grads in (cross_owned, self_owned)]
    kv_grad, query_grad, self_out_grad, cross_bias_grad, third = call(
        cross_last, "cross_last", 1, [all_of(array) for array in ends[0]],
        [out_all((own, 2 * d), FULL), out_all((own, d), FULL), out_all((own, d), FULL),
         out_all((3, own), FULL), out_all((1, own), FULL)],
    )
    feed_in_grad, feed_out_grad, cross_out_grad, bias_out_grad, bias_in_grad = call(
        feed_last, "feed_last", 1, [all_of(feed_total)],
        [out_all((own, ff), FULL), out_all((own, ff), FULL), out_all((own, d), FULL),
         out_all((1, own), FULL), out_all((1, own * ff // d), FULL)],
    )
    if halving:
        ends[1] = lax.optimization_barrier((*ends[1], feed_in_grad))[:-1]
    self_in_grad, self_bias_grad = call(
        self_last, "self_last", 1, [all_of(array) for array in (third, *ends[1])],
        [out_all((own, 3 * d), FULL), out_all((3, own), FULL)],
    )
    return (
        output,
        tokens_grad,
        memory_grad,
        self_in_grad,
        self_out_grad.T,
        self_bias_grad,
        query_grad,
        kv_grad,
        cross_out_grad.T,
        cross_bias_grad,
        feed_in_grad,
        feed_out_grad.T,
        bias_in_grad[0],
        bias_out_grad[0],
    )


def solution(mesh):
    return jax.shard_map(
        on_device,
        mesh=mesh,
        in_specs=(
            P(("dp", "fsdp"), None),
            P(("dp", "fsdp"), None),
            P(("dp", "fsdp"), None),
            P(("dp", "fsdp"), None),
            P(("dp", "fsdp"), None),
            P(),
            P(("dp", "fsdp"), None),
            P(None, ("dp", "fsdp")),
            P(None, ("dp", "fsdp")),
            P(("dp", "fsdp"), None),
            P(("dp", "fsdp"), None),
            P(None, ("dp", "fsdp")),
            P(None, ("dp", "fsdp")),
            P(("dp", "fsdp"), None),
            P(None, ("dp", "fsdp")),
            P(("dp", "fsdp")),
            P(("dp", "fsdp")),
        ),
        out_specs=(
            P(("dp", "fsdp"), None),
            P(("dp", "fsdp"), None),
            P(("dp", "fsdp"), None),
            P(("dp", "fsdp"), None),
            P(None, ("dp", "fsdp")),
            P(None, ("dp", "fsdp")),
            P(("dp", "fsdp"), None),
            P(("dp", "fsdp"), None),
            P(None, ("dp", "fsdp")),
            P(None, ("dp", "fsdp")),
            P(("dp", "fsdp"), None),
            P(None, ("dp", "fsdp")),
            P(("dp", "fsdp")),
            P(("dp", "fsdp")),
        ),
        check_vma=False,
    )
```

```python
import functools

import jax
import jax.numpy as jnp
from jax import lax
from jax.experimental import pallas as pl
from jax.experimental.pallas import tpu as pltpu
from jax.sharding import PartitionSpec as P

HEAD = 64
LANES = 128
FAR = -1e30
FIRST = 7
AXES = ("dp", "fsdp")
LOW = jnp.bfloat16
FULL = jnp.float32


def nn(left, right):
    return lax.dot_general(left, right, (((1,), (0,)), ((), ())), preferred_element_type=FULL)


def nt(left, right):
    return lax.dot_general(left, right, (((1,), (1,)), ((), ())), preferred_element_type=FULL)


def tn(left, right):
    return lax.dot_general(left, right, (((0,), (0,)), ((), ())), preferred_element_type=FULL)


def one_head(pair, odd):
    lane = lax.broadcasted_iota(jnp.int32, pair.shape, 1)
    return jnp.where((lane >= HEAD) == bool(odd), pair, jnp.zeros_like(pair))


def later_keys(rows, keys):
    query = lax.broadcasted_iota(jnp.int32, (rows, keys), 0)
    key = lax.broadcasted_iota(jnp.int32, (rows, keys), 1)
    return query, key


def call(
    body, name, grid, ins, outs, scratch=(), flops=0, moved=0, after=(), scalars=(), room=46,
    anywhere=(),
):
    used = len(ins)

    def only_used(*refs):
        front = len(scalars)
        body(*refs[: front + used], *refs[front + used + len(after) :])

    def spec_of(spec):
        if not scalars or spec.index_map is None:
            return spec
        place = spec.index_map
        return pl.BlockSpec(
            spec.block_shape, lambda i, *_: place(i), pipeline_mode=spec.pipeline_mode
        )

    made = pl.pallas_call(
        only_used if after else body,
        name=name,
        grid_spec=pltpu.PrefetchScalarGridSpec(
            num_scalar_prefetch=len(scalars),
            grid=(grid,),
            in_specs=[spec_of(spec) for _, spec in ins]
            + [pl.BlockSpec(memory_space=pl.ANY) for _ in after],
            out_specs=[spec_of(out[2]) for out in outs],
            scratch_shapes=list(scratch),
        ),
        out_shape=[
            (pltpu.VMEM if kept else pltpu.HBM)(shape, kind)
            for shape, kind, _, *kept in outs
        ],
        compiler_params=pltpu.CompilerParams(vmem_limit_bytes=room << 20),
        cost_estimate=pl.CostEstimate(flops=flops, bytes_accessed=moved, transcendentals=0),
    )(
        *scalars,
        *[placed(array, any(array is free for free in anywhere)) for array, _ in ins],
        *after,
    )
    return [
        pltpu.with_memory_space_constraint(array, pltpu.VMEM) if out[3:] else array
        for array, out in zip(made, outs)
    ]


def rows_of(block, columns):
    return pl.BlockSpec((block, columns), lambda i: (i, 0))


def fixed(shape, place=None):
    place = (0,) * len(shape) if place is None else place
    return pl.BlockSpec(shape, lambda i: place, pipeline_mode=pl.Buffered(1))


def all_of(array):
    return (array, fixed(array.shape))


def out_all(shape, kind):
    return (shape, kind, fixed(shape))


def near(out):
    return (*out, True)


def placed(array, anywhere):
    if anywhere or jax.typeof(array).memory_space == pltpu.VMEM:
        return array
    return pltpu.with_memory_space_constraint(array, pltpu.HBM)


def attend(queries, hot, keys_ref, values_ref, count, causal):
    rows = queries.shape[0]
    heads = queries.shape[1] // HEAD
    lane = lax.broadcasted_iota(jnp.int32, (rows, LANES), 1)
    logs = jnp.zeros((rows, LANES), FULL)
    if causal:
        query, key = later_keys(rows, rows)
        ahead = jnp.where(key <= query, 0.0, FAR)

    def scores_of(head):
        columns = slice(head // 2 * LANES, (head // 2 + 1) * LANES)
        asked = jnp.concatenate([one_head(queries[:, columns], head % 2), hot], axis=1)
        scores = nt(asked, keys_ref[head // 2, :count, :])
        if not causal:
            return scores
        if count == rows:
            return scores + ahead
        return jnp.concatenate(
            [scores[:, : count - rows], scores[:, count - rows :] + ahead], axis=1
        )

    mixed = []
    following = scores_of(0)
    for head in range(heads):
        scores = following
        if head + 1 < heads:
            following = scores_of(head + 1)
        columns = slice(head // 2 * LANES, (head // 2 + 1) * LANES)
        top = jnp.max(scores, axis=1, keepdims=True)
        weights = jnp.exp(scores - top)
        amount = jnp.sum(weights, axis=1, keepdims=True)
        low = (weights * (1.0 / amount)).astype(LOW)
        here = nn(low, values_ref[:count, columns])
        if head % 2:
            mixed.append(jnp.where(lane < HEAD, other, here))
        other = here
        logs = jnp.where(lane == head, top + jnp.log(amount), logs)
    return jnp.concatenate(mixed, axis=1), logs.T[:heads]


def keep_keys(keys_ref, place, keys, hot):
    pairs = keys.shape[1] // LANES
    for pair in range(pairs):
        keys_ref[pair, place, :LANES] = keys[:, pair * LANES : (pair + 1) * LANES]
        keys_ref[pair, place, LANES:] = hot


def self_forward(
    tokens, hot, far, gate, w_in, w_out, bias_columns, w_query,
    projected, mixed, logs, first, first_low, cross_queries, keys, values, bias,
    others_there=lambda: None,
):
    step = pl.program_id(0)
    rows, d = tokens.shape

    @pl.when(step == 0)
    def _():
        bias[...] = bias_columns[...].astype(FULL).T[:8]

    joined_bias = jnp.concatenate([bias[0:1, :], jnp.zeros((1, d), FULL), bias[1:2, :]], axis=1)
    made = (nn(tokens[...], w_in[...]) + joined_bias).astype(LOW)
    projected[...] = made
    place = pl.ds(pl.multiple_of(step * rows, rows), rows)
    keep_keys(keys, place, made[:, d : 2 * d], far[...])
    values[place, :] = made[:, 2 * d :]
    part = min(rows, 256)
    for block in range(values.shape[0] // rows):

        @pl.when(step == block)
        def _(before=block * rows):
            scaled = made[:, :d] * jnp.asarray(HEAD**-0.5, LOW)
            for start in range(0, rows, part):
                here = slice(start, start + part)
                mixed[here, :], logs[:, here] = attend(
                    scaled[here, :], hot[here, :], keys, values, before + start + part, True
                )

    branch = nt(mixed[...].astype(LOW), w_out[...]) + bias[2:3, :]
    total = tokens[...].astype(FULL) + gate[...] * branch
    first[...] = total
    first_low[...] = total.astype(LOW)
    others_there()
    cross_queries[...] = (nn(total.astype(LOW), w_query[...]) + bias[3:4, :]).astype(LOW)


class Columns:
    def __init__(self, ref, start, stop):
        self.ref, self.start, self.stop = ref, start, stop

    def __getitem__(self, everything):
        return self.ref[:, :, :, self.start : self.stop].reshape(-1, self.stop - self.start)


def self_forward_joining(
    bits, self_mine, self_got, cross_mine, cross_got, tokens, hot, far, gate, *refs
):
    *outs, self_whole, cross_whole, keys, values, bias, self_here, cross_here, arrived, sent = refs
    d = tokens.shape[1]
    core = bits[0]
    coming = [
        pltpu.make_async_copy(half, here.at[:, place], arrived.at[index])
        for index, (half, here, place) in enumerate(
            [
                (self_mine, self_here, core), (self_got, self_here, 1 - core),
                (cross_mine, cross_here, core), (cross_got, cross_here, 1 - core),
            ]
        )
    ]
    going = [
        pltpu.make_async_copy(self_here, self_whole, sent.at[0]),
        pltpu.make_async_copy(cross_here, cross_whole, sent.at[1]),
    ]

    @pl.when(pl.program_id(0) == 0)
    def _():
        for copy in coming:
            copy.start()
        for copy in coming[:2]:
            copy.wait()
        going[0].start()

    def others_there():
        @pl.when(pl.program_id(0) == 0)
        def _():
            for copy in coming[2:]:
                copy.wait()
            going[1].start()

    self_forward(
        tokens, hot, far, gate, Columns(self_here, 0, 3 * d), Columns(self_here, 3 * d, 4 * d),
        Columns(self_here, 4 * d, 4 * d + LANES), Columns(cross_here, 2 * d, 3 * d),
        *outs, keys, values, bias, others_there=others_there,
    )

    @pl.when(pl.program_id(0) == pl.num_programs(0) - 1)
    def _():
        for copy in going:
            copy.wait()


def cross_forward(
    queries, memory, hot, far, gate, first, w_kv, w_out, bias_columns,
    memory_kv, mixed, logs, second, keys, bias,
):
    d = memory.shape[1]

    @pl.when(pl.program_id(0) == 0)
    def _():
        bias[...] = bias_columns[...].astype(FULL).T[:8]
        made = nn(memory[...], w_kv[...])
        memory_kv[:, :d] = made[:, :d].astype(LOW)
        memory_kv[:, d:] = (made[:, d:] + bias[4:5, :]).astype(LOW)
        keep_keys(keys, slice(None), memory_kv[:, :d], far[...])

    scaled = queries[...] * jnp.asarray(HEAD**-0.5, LOW)
    mixed[...], logs[...] = attend(
        scaled, hot[...], keys, memory_kv.at[:, d:], memory.shape[0], False
    )
    branch = nt(mixed[...].astype(LOW), w_out[...]) + bias[5:6, :]
    second[...] = first[...] + gate[...] * branch


def head_sums(left, right):
    d = left.shape[1]
    head = lax.broadcasted_iota(jnp.int32, (d // HEAD, d), 0)
    column = lax.broadcasted_iota(jnp.int32, (d // HEAD, d), 1)
    chosen = (column // HEAD == head).astype(LOW)
    product = left.astype(FULL) * right.astype(FULL)
    high = product.astype(LOW)
    rest = product - high.astype(FULL)
    middle = rest.astype(LOW)
    last = (rest - middle.astype(FULL)).astype(LOW)
    return nt(chosen, high) + nt(chosen, middle) + nt(chosen, last)


def gelu_both(z):
    c = 0.7978845608028654
    square = z * z
    half = 0.5 + 0.5 * jnp.tanh(z * (c + c * 0.044715 * square))
    value = z * half
    slope = half + value * (1.0 - half) * (2.0 * c + 6.0 * c * 0.044715 * square)
    return value, slope


def spread(d, ff):
    each = ff // d
    row = lax.broadcasted_iota(jnp.int32, (d, ff), 0)
    entry = lax.broadcasted_iota(jnp.int32, (d, ff), 1)
    column = lax.broadcasted_iota(jnp.int32, (LANES, ff), 0)
    there = lax.broadcasted_iota(jnp.int32, (LANES, ff), 1)
    return entry // each == row, (there % each + FIRST == column).astype(LOW)


def columns_to_row(columns, ff):
    owner, place = spread(columns.shape[0], ff)
    return jnp.sum(jnp.where(owner, nn(columns, place), 0.0), axis=0, keepdims=True)


def row_to_columns(row, d):
    owner, place = spread(d, row.shape[1])
    return nt(jnp.where(owner, row, 0.0).astype(LOW), place).astype(LOW)


def rows_to_columns(*rows):
    d = rows[0].shape[1]
    stack = jnp.concatenate([*rows, jnp.zeros((LANES - len(rows), d), FULL)], axis=0)
    return stack.T.astype(LOW)


def feed_both(
    second_far, upstream, gate, mixed, weights, w_cross, bias_columns,
    output, second_grad, mixed_grad, deltas, feed_grad, sums,
    second, w_in, w_out, w_cross_out, low, signal, hidden_all, before_all, crossed, back_all,
    made_all, mixed_back, grads, arrived, sent,
    *, inner, own,
):
    rows, d = second.shape
    ff = w_in.shape[1]
    width = 1024
    parts = [slice(start, start + width) for start in range(0, ff, width)]
    incoming = [(second_far, second)]
    for part in parts:
        incoming.append((weights.at[:, part], w_in.at[:, part]))
        incoming.append(
            (weights.at[:, ff + part.start : ff + part.stop], w_out.at[:, part])
        )
    incoming.append((w_cross.at[:, 3 * d : 4 * d], w_cross_out))
    coming = [
        pltpu.make_async_copy(source, target, arrived.at[index])
        for index, (source, target) in enumerate(incoming)
    ]
    for copy in coming:
        copy.start()
    going = []

    def send(source, target):
        copy = pltpu.make_async_copy(source, target, sent.at[len(going)])
        copy.start()
        going.append(copy)

    bias = bias_columns[...].astype(FULL).T[:8]
    bias_in = columns_to_row(bias_columns[...], ff)
    signal[...] = (gate[...] * upstream[...].astype(FULL)).astype(LOW)
    coming[0].wait()
    low[...] = second[...].astype(LOW)
    half = rows // 2
    items = [(slice(start, start + half), index) for start in (0, half) for index in range(len(parts))]
    bias_grads = [jnp.zeros((1, width), FULL) for _ in parts]

    def products(item):
        place, index = item
        part = parts[index]
        if place.start == 0:
            coming[1 + 2 * index].wait()
            coming[2 + 2 * index].wait()
        before = nn(low[place, :], w_in[:, part]) + bias_in[:, part]
        return before, nn(signal[place, :], w_out[:, part])

    following = products(items[0])
    for at, (place, index) in enumerate(items):
        before, hidden_back = following
        if at + 1 < len(items):
            following = products(items[at + 1])
        if index == 0:
            made = bias[6:7, :]
            back = upstream[place, :].astype(FULL)
        part = parts[index]
        hidden, slope = gelu_both(before)
        hidden_all[place, part] = hidden.astype(LOW)
        before_grad = (hidden_back * slope).astype(LOW)
        before_all[place, part] = before_grad
        bias_grads[index] = bias_grads[index] + column_sum(before_grad)
        made = made + nt(hidden_all[place, part], w_out[:, part])
        back = back + nt(before_all[place, part], w_in[:, part])
        if index == len(parts) - 1:
            made_all[place, :] = (second[place, :] + gate[place, :] * made).astype(LOW)
            back_all[place, :] = back
            crossed[place, :] = (gate[place, :] * back).astype(LOW)
    send(made_all, output)
    send(back_all, second_grad)
    coming[-1].wait()
    mixed_back[...] = nn(crossed[...], w_cross_out[...]).astype(LOW)
    send(mixed_back, mixed_grad)
    deltas[...] = head_sums(mixed_back[...], mixed[...])
    sums[...] = jnp.zeros_like(sums)
    sums[0:1, :] = column_sum(signal[...])
    sums[1:2, :] = column_sum(crossed[...])

    def keep(start, grad):
        end = start + grad.shape[1]
        outer = d // own // inner
        for owner in range(inner * outer if inner > 1 else 0):
            to = (owner % inner * outer + owner // inner) * own
            grads[to : to + own, start:end] = grad[owner * own : (owner + 1) * own]
        if inner == 1:
            grads[:, start:end] = grad
        send(grads.at[:, start:end], feed_grad.at[:, start:end])

    for part in parts:
        keep(part.start, tn(low[...], before_all[:, part]).astype(LOW))
        keep(ff + part.start, tn(signal[...], hidden_all[:, part]).astype(LOW))
    at = 2 * ff
    last = [
        tn(crossed[...], mixed[...].astype(LOW)).astype(LOW),
        rows_to_columns(sums[0:1, :]),
        row_to_columns(jnp.concatenate(bias_grads, axis=1), d),
    ]
    keep(at, jnp.concatenate(last, axis=1))
    for copy in going:
        copy.wait()


def column_sum(array):
    return jnp.sum(array.astype(FULL), axis=0, keepdims=True)


def attend_back(
    queries, keys, values, hot, far, mixed_grad, logs, deltas, pair,
    query_grad, key_grad, value_grad, key_sum, value_sum, reached, causal, block=256,
):
    count = keys.shape[0]
    reached[:, :LANES] = keys[...]
    reached[:, LANES:] = far[...]
    turned = keys[...].T
    if causal:
        key, query = later_keys(block, block)
        ahead = jnp.where(key <= query, 0.0, FAR)
    items = [
        (start, odd) for start in range(queries.shape[0] - block, -1, -block) for odd in range(2)
    ]

    def products(item):
        start, odd = item
        place = slice(start, start + block)
        reach = start + block if causal else count
        asked = one_head(queries[place, :], odd) * jnp.asarray(HEAD**-0.5, LOW)
        incoming = one_head(mixed_grad[place, :], odd)
        scores = nt(reached[:reach, :], jnp.concatenate([asked, hot[place, :]], axis=1))
        if causal and start:
            scores = jnp.concatenate([scores[:start], scores[start:] + ahead], axis=0)
        elif causal:
            scores = scores + ahead
        return scores, nt(values[:reach, :], incoming), asked, incoming, place, reach

    following = products(items[0])
    for index, (start, odd) in enumerate(items):
        scores, pushed, asked, incoming, place, reach = following
        if index + 1 < len(items):
            following = products(items[index + 1])
        head = pl.ds(2 * pair + odd, 1)
        chances = jnp.exp(scores - logs[head, place])
        score_grad = (chances * (pushed - deltas[head, place])).astype(LOW)
        turned_grad = nn(turned[odd * HEAD : (odd + 1) * HEAD, :reach], score_grad)
        value_part = nn(chances.astype(LOW), incoming)
        key_part = nn(score_grad, asked)
        if index == 0:
            value_sum[...] = value_part
            key_sum[...] = key_part
        else:
            value_sum[:reach, :] += value_part
            key_sum[:reach, :] += key_part
        if odd:
            both = jnp.concatenate([other, turned_grad], axis=0) * HEAD**-0.5
            query_grad[place, :] = both.T.astype(LOW)
        other = turned_grad
    key_grad[...] = key_sum[...].astype(LOW)
    value_grad[...] = value_sum[...].astype(LOW)


def cross_back(
    bits, queries, keys, values, hot, far, in_grad, logs, cross_deltas, sums,
    first, second_grad, memory, self_mixed, gate, weights, self_weights,
    *outs,
):
    (
        *owned, key_grad, value_grad, first_grad, mixed_grad, deltas,
        key_sum, value_sum, reached, signals, first_here, second_here, memory_here, mixed_here,
        w_query, w_out, grads, back_here, signal_here, arrived, sent,
    ) = outs
    pair = pl.program_id(0)
    d = memory.shape[1]
    copies = [
        pltpu.make_async_copy(source, target, arrived.at[index])
        for index, (source, target) in enumerate(
            [
                (first, first_here), (second_grad, second_here), (memory, memory_here),
                (self_mixed, mixed_here), (weights.at[:, 2 * d : 3 * d], w_query),
                (self_weights.at[:, 3 * d : 4 * d], w_out),
            ]
        )
    ]

    @pl.when(pair == 0)
    def _():
        for copy in copies:
            copy.start()

    attend_back(
        queries, keys, values, hot, far, in_grad, logs, cross_deltas, pair,
        signals.at[0, pair], signals.at[1, pair], signals.at[2, pair],
        key_sum, value_sum, reached, False,
    )
    key_grad[...] = signals[1, pair]
    value_grad[...] = signals[2, pair]

    @pl.when(pair == pl.num_programs(0) - 1)
    def _():
        for copy in copies:
            copy.wait()
        pairs = signals.shape[1]
        query_signal, key_signal, value_signal = (
            jnp.concatenate([signals[which, place] for place in range(pairs)], axis=1)
            for which in range(3)
        )
        back = second_here[...] + nt(query_signal, w_query[...])
        back_here[...] = back
        signal = (gate[...] * back).astype(LOW)
        mixed_back = nn(signal, w_out[...]).astype(LOW)
        signal_here[...] = mixed_back
        going = [
            pltpu.make_async_copy(back_here, first_grad, sent.at[0]),
            pltpu.make_async_copy(signal_here, mixed_grad, sent.at[1]),
        ]
        for copy in going:
            copy.start()
        deltas[...] = head_sums(mixed_back, mixed_here[...])
        grads[:, :d] = tn(memory_here[...], key_signal).astype(LOW)
        grads[:, d : 2 * d] = tn(memory_here[...], value_signal).astype(LOW)
        grads[:, 2 * d : 3 * d] = tn(first_here[...], query_signal).astype(LOW)
        grads[:, 3 * d : 4 * d] = tn(signal, mixed_here[...].astype(LOW)).astype(LOW)
        grads[:, 4 * d :] = rows_to_columns(
            column_sum(query_signal), column_sum(value_signal), sums[1:2, :], column_sum(signal)
        )
        if len(owned) == 2:
            part_by_core(bits, grads, *owned)
        else:
            owned[0][...] = grads[...]
        for copy in going:
            copy.wait()


def self_back(
    bits, queries, keys, values, hot, far, in_grad, logs, deltas, tokens, *rest, before, ending
):
    if ending:
        earlier, earlier_sums, *rest = rest
    *owned, query_grad, key_grad, value_grad, key_sum, value_sum, reached, signals, grads = rest
    step = pl.program_id(0)
    pairs = signals.shape[1]
    wide = pairs * LANES
    attend_back(
        queries, keys, values, hot, far, in_grad, logs, deltas, before + step,
        signals.at[0, step], signals.at[1, step], signals.at[2, step],
        key_sum, value_sum, reached, True,
    )
    query_grad[...] = signals[0, step]
    key_grad[...] = signals[1, step]
    value_grad[...] = signals[2, step]

    @pl.when(step == pl.num_programs(0) - 1)
    def _():
        at = 3 * wide if ending else 0
        if ending:
            grads[:, :at] = earlier[...]
        added = []
        for which in range(3):
            part = jnp.concatenate([signals[which, place] for place in range(pairs)], axis=1)
            grads[:, at + which * wide : at + (which + 1) * wide] = tn(
                tokens[...], part
            ).astype(LOW)
            if which != 1:
                added.append(column_sum(part))
        if not ending:
            owned[0][...] = grads[...]
            owned[1][0:1, :] = added[0]
            owned[1][1:2, :] = added[1]
            return
        grads[:, 2 * at :] = rows_to_columns(
            *[
                jnp.concatenate([earlier_sums[row : row + 1, :], added[row]], axis=1)
                for row in range(2)
            ]
        )
        if len(owned) == 2:
            part_by_core(bits, grads, *owned)
        else:
            owned[0][...] = grads[...]


def part_by_core(bits, grads, keep, away):
    own = keep.shape[1]
    for core in range(2):

        @pl.when(bits[0] == core)
        def _(core=core):
            for slab in range(2 * keep.shape[0]):
                there = keep if slab % 2 == core else away
                there[slab // 2] = grads[slab * own : (slab + 1) * own, :]


def memory_back(key_signal, value_signal, w_kv, memory_grad):
    d = key_signal.shape[1]
    memory_grad[...] = nt(key_signal[...], w_kv[:, :d]) + nt(value_signal[...], w_kv[:, d:])


def tokens_back(first_grad, w_in, *refs):
    *signals, tokens_grad = refs
    d = first_grad.shape[1]
    total = first_grad[...]
    wide = signals[0].shape[1]
    for index, signal in enumerate(signals):
        start = index % 3 * d + index // 3 * wide
        total = total + nt(signal[...], w_in[:, start : start + wide])
    tokens_grad[...] = total


def sum_to_owners(grads, device_count, orders):
    me = lax.axis_index(AXES)
    bits = device_count.bit_length() - 1
    running = []
    for grad in grads:
        rows, columns = grad.shape
        running.append(grad.reshape((2,) * bits + (rows // device_count, columns)))
    left = [list(range(bits)) for _ in grads]
    for step in range(bits):
        sent = []
        for part, order in enumerate(orders):
            bit = order[step]
            axis = len(left[part]) - 1 - left[part].index(bit)
            mine = (me >> bit) & 1
            away = lax.dynamic_index_in_dim(running[part], 1 - mine, axis, keepdims=False)
            pairs = [(i, i ^ (1 << bit)) for i in range(device_count)]
            sent.append((axis, mine, lax.ppermute(away.astype(LOW), AXES, pairs)))
            left[part].remove(bit)
        for part, (axis, mine, got) in enumerate(sent):
            kept = lax.dynamic_index_in_dim(running[part], mine, axis, keepdims=False)
            running[part] = kept.astype(FULL) + got.astype(FULL)
    return running


def swap(array, bit, device_count):
    return lax.ppermute(array, AXES, [(i, i ^ (1 << bit)) for i in range(device_count)])


def scatter_rows(grad, device_count):
    bits = device_count.bit_length() - 1
    high = list(range(1, bits))[::-1]
    half = grad.shape[1] // 256 * 128
    orders = ([0] + high, [0, high[1], high[0]] + high[2:])
    return jnp.concatenate(
        sum_to_owners([grad[:, :half], grad[:, half:]], device_count, orders), axis=1
    )


def swap(array, change, device_count):
    return lax.ppermute(array, AXES, [(i, i ^ change) for i in range(device_count)])


def picked(terms, first, second):
    total = None
    for term in terms:
        for place in (first, second):
            term = lax.dynamic_index_in_dim(term, place, 0, keepdims=False)
        total = term.astype(FULL) if total is None else total + term.astype(FULL)
    return total


class Halving:
    changes = ((0, 1), (1, 0), (1, 1))

    def __init__(self, me, keep, away, device_count):
        self.count = device_count
        self.x, self.y = (me >> 3) & 1, (me >> 4) & 1
        self.low, self.high = (me >> 1) & 1, (me >> 2) & 1
        shape = (2, 2, 4, *keep.shape[1:])
        self.terms = [keep.reshape(shape)]
        self.got = [swap(away.reshape(shape), 1, device_count)]

    def plane(self):
        terms = self.terms + self.got
        self.sent = [picked(terms, self.y ^ y, self.x ^ x).astype(LOW) for y, x in self.changes]
        self.got = [
            swap(array, 8 * x + 16 * y, self.count)
            for array, (y, x) in zip(self.sent, self.changes)
        ]
        self.terms = [
            lax.dynamic_index_in_dim(
                lax.dynamic_index_in_dim(term, self.y, 0, keepdims=False), self.x, 0, keepdims=False
            )
            for term in terms
        ]

    def line(self):
        terms = [term.reshape(2, 2, *term.shape[1:]) for term in self.terms + self.got]
        self.sent = [
            picked(terms, self.high ^ high, self.low ^ low).astype(LOW)
            for high, low in self.changes
        ]
        self.kept = picked(terms, self.high, self.low)

    def send_line(self, *after):
        self.sent = list(lax.optimization_barrier((*self.sent, *after))[: len(self.sent)])
        self.got = [
            swap(array, 2 * low + 4 * high, self.count)
            for array, (high, low) in zip(self.sent, self.changes)
        ]

    def wait_for(self, *arrays):
        self.got = list(lax.optimization_barrier((*self.got, *arrays))[: len(self.got)])


def total_of(keep, *got):
    total = keep[...]
    for part in got:
        total = total + part[...].astype(FULL)
    return total


def cross_last(*refs):
    *parts, kv, query, self_out, cross_bias, self_bias = refs
    total = total_of(*parts)
    d = query.shape[1]
    kv[...] = total[:, : 2 * d]
    query[...] = total[:, 2 * d : 3 * d]
    self_out[...] = total[:, 3 * d : 4 * d]
    turned = turned_bias(total[:, 4 * d :])
    cross_bias[...] = turned[0:3]
    self_bias[...] = turned[3:4]


def turned_bias(columns):
    own = columns.shape[0]
    square = jnp.concatenate([columns, jnp.zeros((LANES - own, LANES), FULL)], axis=0)
    return square.T[:8, :own]


def self_last(third, *refs):
    *parts, self_in, bias = refs
    total = total_of(*parts)
    columns = self_in.shape[1]
    half = columns // 2
    wide = half // 3
    for call_index in range(2):
        for which in range(3):
            at = call_index * half + which * wide
            to = which * 2 * wide + call_index * wide
            self_in[:, to : to + wide] = total[:, at : at + wide]
    bias[0:2, :] = turned_bias(total[:, columns:])[0:2]
    bias[2:3, :] = third[...]


def feed_last(total, feed_in, feed_out, cross_out, bias_out, bias_in):
    ff = feed_in.shape[1]
    at = 2 * ff + cross_out.shape[1]
    feed_in[...] = total[:, :ff].astype(FULL)
    feed_out[...] = total[:, ff : 2 * ff].astype(FULL)
    cross_out[...] = total[:, 2 * ff : at].astype(FULL)
    bias_out[...] = turned_bias(total[:, at : at + LANES].astype(FULL))[0:1]
    bias_in[...] = columns_to_row(total[:, at + LANES :], bias_in.shape[1])


def pack(
    self_in, self_out, cross_query, cross_kv, cross_out, feed_in, feed_out, self_bias, cross_bias,
    bias_out, bias_in, near, own_feed,
):
    d = self_out.shape[1]
    ff = feed_in.shape[1]
    own = self_in.shape[0]
    near[:, : 3 * d] = self_in[...].astype(LOW)
    near[:, 3 * d : 4 * d] = self_out[...].astype(LOW)
    rows = jnp.concatenate(
        [self_bias[...], cross_bias[...], bias_out[...], jnp.zeros((LANES - 7, own), FULL)], axis=0
    )
    wide = jnp.concatenate([rows, jnp.zeros((LANES, LANES - own), FULL)], axis=1)
    at = 4 * d + LANES
    near[:, 4 * d : at] = wide.T[:own].astype(LOW) + row_to_columns(bias_in[...], own)
    near[:, at : at + 2 * d] = cross_kv[...].astype(LOW)
    near[:, at + 2 * d : at + 3 * d] = cross_query[...].astype(LOW)
    near[:, at + 3 * d :] = cross_out[...].astype(LOW)
    own_feed[:, :ff] = feed_in[...].astype(LOW)
    own_feed[:, ff:] = feed_out[...].astype(LOW)


def marks(seq_lengths, memory_lengths, residual_gate, hot, self_far, memory_far, gate):
    slots = seq_lengths.shape[0]
    lane = lax.broadcasted_iota(jnp.int32, hot.shape, 1)

    def numbered(lengths, padding):
        position = lax.broadcasted_iota(jnp.int32, hot.shape, 0)
        end = lengths[0]
        number = jnp.where(position >= end, 1, 0)
        for slot in range(1, slots):
            end = end + lengths[slot]
            number = number + jnp.where(position >= end, 1, 0)
        present = position < end
        return jnp.where(present, number, padding), present

    ids, present = numbered(seq_lengths, slots)
    hot[...] = jnp.where(ids == lane, 1.0, 0.0).astype(LOW)
    self_far[...] = jnp.where(ids == lane, 0.0, FAR).astype(LOW)
    gate[...] = jnp.where(present[:, :1], residual_gate[0], 0.0)
    ids, _ = numbered(memory_lengths, slots + 1)
    memory_far[...] = jnp.where(ids == lane, 0.0, FAR).astype(LOW)


def gather_near(near, cut, device_count, after):
    me = lax.axis_index(AXES)
    others = [swap(near, 2 * change, device_count) for change in (1, 2, 3)]
    others = lax.optimization_barrier((*others, after))[:3]
    first, second, third, fourth = near, *others
    odd = jnp.where(
        (me >> 1) & 1,
        jnp.stack([second, first, fourth, third]),
        jnp.stack([first, second, third, fourth]),
    )
    line = jnp.where((me >> 2) & 1, jnp.concatenate([odd[2:], odd[:2]]), odd)
    held = [line[..., :cut], line[..., cut:]]
    known = [[1, 1], [1, 1]]
    for bits in ((3, 4), (4, 3)):
        got = [swap(array, 1 << bit, device_count) for array, bit in zip(held, bits)]
        for part, bit in enumerate(bits):
            axis = sum(other > bit for other in known[part])
            low = jnp.stack([held[part], got[part]], axis)
            high = jnp.stack([got[part], held[part]], axis)
            held[part] = jnp.where((me >> bit) & 1, high, low)
            known[part].append(bit)
    mine = [array.reshape(-1, *array.shape[-2:]) for array in held]
    return [(array, swap(array, 1, device_count)) for array in mine]


def on_device(
    tokens, memory, out_cotangent, seq_lengths, memory_lengths, residual_gate,
    self_in, self_out, self_bias, cross_query, cross_key_value, cross_out, cross_bias,
    feed_in, feed_out, feed_bias_in, feed_bias_out,
):
    device_count = lax.axis_size(AXES)
    count, d = tokens.shape
    key_count = memory.shape[0]
    ff = feed_in.shape[1]
    own = self_in.shape[0]
    pairs = d // LANES
    heads = d // HEAD
    block = 512
    steps = count // block
    halving = lax.axis_size("dp") == 4 and lax.axis_size("fsdp") == 8
    me = lax.axis_index(AXES)
    bits = (me & 1).astype(jnp.int32)[None]
    cut = 4 * d + LANES
    own_near, own_feed = call(
        pack,
        "pack",
        1,
        [
            all_of(array)
            for array in (
                self_in, self_out.T, cross_query, cross_key_value, cross_out.T, feed_in,
                feed_out.T, self_bias, cross_bias, feed_bias_out[None], feed_bias_in[None],
            )
        ],
        [out_all((own, cut + 4 * d), LOW), out_all((own, 2 * ff), LOW)],
    )
    hot, self_far, memory_far, gate = call(
        marks,
        "marks",
        1,
        [],
        [out_all((count, LANES), LOW), out_all((count, LANES), LOW),
         out_all((key_count, LANES), LOW), out_all((count, 1), FULL)],
        scalars=(seq_lengths[0], memory_lengths[0], residual_gate),
    )
    feed_whole = lax.all_gather(own_feed, AXES, axis=0, tiled=True)
    if halving:
        (self_mine, self_got), (cross_mine, cross_got) = gather_near(own_near, cut, device_count, gate)
    else:
        self_whole = lax.all_gather(own_near[:, :cut], AXES, axis=0, tiled=True)
        cross_whole = lax.all_gather(own_near[:, cut:], AXES, axis=0, tiled=True)
    each = lambda array: (array, rows_of(block, array.shape[1]))
    out_rows = lambda columns, kind: ((count, columns), kind, rows_of(block, columns))
    out_heads = ((heads, count), FULL, pl.BlockSpec((heads, block), lambda i: (0, i)))

    self_outs = [
        out_rows(3 * d, LOW), out_rows(d, FULL), out_heads, near(out_rows(d, FULL)),
        out_rows(d, LOW), out_rows(d, LOW),
    ]
    self_room = [
        pltpu.VMEM((pairs, count, 2 * LANES), LOW), pltpu.VMEM((count, d), LOW),
        pltpu.VMEM((8, d), FULL),
    ]
    if halving:
        there = pl.BlockSpec(memory_space=pl.ANY)
        halves = (self_mine, self_got, cross_mine, cross_got)
        (
            projected, self_mixed, self_logs, first, first_low, cross_queries,
            self_whole, cross_whole,
        ) = call(
            self_forward_joining,
            "self_forward",
            steps,
            [(array, there) for array in halves]
            + [each(tokens), each(hot), each(self_far), each(gate)],
            self_outs
            + [((device_count // 2, 2, own, columns), LOW, there) for columns in (cut, 4 * d)],
            self_room
            + [pltpu.VMEM((device_count // 2, 2, own, columns), LOW) for columns in (cut, 4 * d)]
            + [pltpu.SemaphoreType.DMA((4,)), pltpu.SemaphoreType.DMA((2,))],
            flops=15 << 30, moved=8 << 20, scalars=(bits,), anywhere=halves,
        )
        self_whole, cross_whole = self_whole.reshape(d, cut), cross_whole.reshape(d, 4 * d)
    w_self_in = (self_whole, fixed((d, 3 * d), (0, 0)))
    w_self_out = (self_whole, fixed((d, d), (0, 3)))
    bias_columns = (self_whole, fixed((d, LANES), (0, 4 * d // LANES)))
    w_kv = (cross_whole, fixed((d, 2 * d), (0, 0)))
    w_query = (cross_whole, fixed((d, d), (0, 2)))
    w_cross_out = (cross_whole, fixed((d, d), (0, 3)))
    w_feed_in = (feed_whole, fixed((d, ff), (0, 0)))
    w_feed_out = (feed_whole, fixed((d, ff), (0, 1)))

    if not halving:
        projected, self_mixed, self_logs, first, first_low, cross_queries = call(
            self_forward,
            "self_forward",
            steps,
            [each(tokens), each(hot), each(self_far), each(gate), w_self_in, w_self_out,
             bias_columns, w_query],
            self_outs,
            self_room,
            flops=15 << 30, moved=8 << 20,
        )
    memory_kv, cross_mixed, cross_logs, second = call(
        cross_forward,
        "cross_forward",
        steps,
        [each(cross_queries), all_of(memory), each(hot), all_of(memory_far), each(gate),
         each(first), w_kv, w_cross_out, bias_columns],
        [out_all((key_count, 2 * d), LOW), near(out_rows(d, FULL)), near(out_heads),
         out_rows(d, FULL)],
        [pltpu.VMEM((pairs, key_count, 2 * LANES), LOW), pltpu.VMEM((8, d), FULL)],
        flops=20 << 30, moved=8 << 20,
    )
    inner = lax.axis_size("fsdp") if halving else 1
    left_there = lambda array: (array, pl.BlockSpec(memory_space=pl.ANY))
    out_there = lambda shape, kind: (shape, kind, pl.BlockSpec(memory_space=pl.ANY))
    out_wide = 2 * ff + d + 2 * LANES
    output, second_grad, cross_mixed_grad, cross_deltas, feed_grad, feed_sums = call(
        functools.partial(feed_both, inner=inner, own=own),
        "feed_both",
        1,
        [left_there(second), all_of(out_cotangent), all_of(gate), all_of(cross_mixed),
         left_there(feed_whole), left_there(cross_whole), bias_columns],
        [out_there((count, d), LOW), out_there((count, d), FULL), out_there((count, d), LOW),
         near(out_all((heads, count), FULL)), out_there((d, out_wide), LOW),
         near(out_all((8, d), FULL))],
        [pltpu.VMEM((count, d), FULL), pltpu.VMEM((d, ff), LOW), pltpu.VMEM((d, ff), LOW),
         pltpu.VMEM((d, d), LOW), pltpu.VMEM((count, d), LOW), pltpu.VMEM((count, d), LOW),
         pltpu.VMEM((count, ff), LOW), pltpu.VMEM((count, ff), LOW), pltpu.VMEM((count, d), LOW),
         pltpu.VMEM((count, d), FULL), pltpu.VMEM((count, d), LOW), pltpu.VMEM((count, d), LOW),
         pltpu.VMEM((d, out_wide), LOW), pltpu.SemaphoreType.DMA((6,)),
         pltpu.SemaphoreType.DMA((8,))],
        flops=25 << 30, moved=16 << 20,
    )
    ways = ("fsdp", "dp") if halving else ("dp", "fsdp")
    feed_total = lax.psum_scatter(feed_grad, ways[0], scatter_dimension=0, tiled=True)

    def pair_columns(array, start, width=LANES):
        return (array, pl.BlockSpec((array.shape[0], width), lambda i: (0, start + i)))

    def out_pairs(rows, columns):
        return ((rows, columns), LOW, pl.BlockSpec((rows, LANES), lambda i: (0, i)))

    def owned(columns):
        if halving:
            return [out_all((device_count // 2, own, columns), LOW)] * 2
        return [out_all((d, columns), LOW)]

    def pair_room(rows, steps):
        return [
            pltpu.VMEM((rows, LANES), FULL), pltpu.VMEM((rows, LANES), FULL),
            pltpu.VMEM((rows, 2 * LANES), LOW), pltpu.VMEM((3, steps, rows, LANES), LOW),
        ]

    cross_columns = 4 * d + LANES
    *cross_owned, key_signal, value_signal, first_grad, self_mixed_grad, self_deltas = call(
        cross_back,
        "cross_back",
        pairs,
        [pair_columns(cross_queries, 0), pair_columns(memory_kv, 0),
         pair_columns(memory_kv, pairs), all_of(hot), all_of(memory_far),
         pair_columns(cross_mixed_grad, 0), all_of(cross_logs), all_of(cross_deltas),
         all_of(feed_sums), left_there(first_low), left_there(second_grad), left_there(memory),
         left_there(self_mixed), all_of(gate), left_there(cross_whole), left_there(self_whole)],
        owned(cross_columns)
        + [out_pairs(key_count, d), out_pairs(key_count, d), out_there((count, d), FULL),
           out_there((count, d), LOW), near(out_all((heads, count), FULL))],
        pair_room(key_count, pairs)
        + [pltpu.VMEM((count, d), LOW), pltpu.VMEM((count, d), FULL),
           pltpu.VMEM((key_count, d), LOW), pltpu.VMEM((count, d), FULL),
           pltpu.VMEM((d, d), LOW), pltpu.VMEM((d, d), LOW),
           pltpu.VMEM((d, cross_columns), LOW), pltpu.VMEM((count, d), FULL),
           pltpu.VMEM((count, d), LOW), pltpu.SemaphoreType.DMA((6,)),
           pltpu.SemaphoreType.DMA((2,))],
        flops=30 << 30, moved=24 << 20, scalars=(bits,),
    )
    if halving:
        cross_sum = Halving(me, *cross_owned, device_count)

    half = pairs // 2
    self_columns = 3 * d + LANES

    def self_part(before, ending, outs, earlier=(), after=()):
        wide = half * LANES
        columns = self_columns if ending else 3 * wide
        return call(
            functools.partial(self_back, before=before, ending=ending),
            "self_back",
            half,
            [pair_columns(projected, before), pair_columns(projected, pairs + before),
             pair_columns(projected, 2 * pairs + before), all_of(hot), all_of(self_far),
             pair_columns(self_mixed_grad, before), all_of(self_logs), all_of(self_deltas),
             all_of(tokens)]
            + [all_of(array) for array in earlier],
            outs + [out_pairs(count, wide)] * 3,
            pair_room(count, half) + [pltpu.VMEM((d, columns), LOW)],
            flops=12 << 30, moved=8 << 20, scalars=(bits,), after=after,
        )

    wide = half * LANES
    *earlier, query_one, key_one, value_one = self_part(
        0, False, [out_all((d, 3 * wide), LOW), out_all((8, wide), FULL)]
    )
    after = ()
    if halving:
        cross_sum.wait_for(query_one)
        cross_sum.plane()
        after = tuple(cross_sum.sent)
    *self_owned, query_two, key_two, value_two = self_part(
        half, True, owned(self_columns), earlier, after
    )
    after = ()
    if halving:
        cross_sum.wait_for(query_two)
        feed_total, _ = lax.optimization_barrier((feed_total, cross_sum.got[0]))
    feed_total = lax.psum_scatter(feed_total, ways[1], scatter_dimension=0, tiled=True)
    if halving:
        self_sum = Halving(me, *self_owned, device_count)
        cross_sum.line()
        self_sum.wait_for(*cross_sum.sent)
        self_sum.plane()
        cross_sum.send_line(*self_sum.sent)
        after = tuple(self_sum.sent)
    tokens_grad, = call(
        tokens_back,
        "tokens_back",
        steps,
        [each(first_grad), w_self_in]
        + [each(array) for array in (query_one, key_one, value_one, query_two, key_two, value_two)],
        [out_rows(d, FULL)],
        flops=3 << 30, moved=8 << 20, after=after,
    )
    memory_grad, = call(
        memory_back,
        "memory_back",
        steps,
        [each(key_signal), each(value_signal), w_kv],
        [((key_count, d), FULL, rows_of(block, d))],
        flops=2 << 30, moved=5 << 20, after=after,
    )
    if halving:
        self_sum.wait_for(tokens_grad, memory_grad)
        self_sum.line()
        self_sum.send_line()
        cross_sum.wait_for(*self_sum.sent)
        ends = [(cross_sum.kept, *cross_sum.got), (self_sum.kept, *self_sum.got)]
    else:
        ends = [(scatter_rows(grads[0], device_count),) for grads in (cross_owned, self_owned)]
    kv_grad, query_grad, self_out_grad, cross_bias_grad, third = call(
        cross_last, "cross_last", 1, [all_of(array) for array in ends[0]],
        [out_all((own, 2 * d), FULL), out_all((own, d), FULL), out_all((own, d), FULL),
         out_all((3, own), FULL), out_all((1, own), FULL)],
    )
    feed_in_grad, feed_out_grad, cross_out_grad, bias_out_grad, bias_in_grad = call(
        feed_last, "feed_last", 1, [all_of(feed_total)],
        [out_all((own, ff), FULL), out_all((own, ff), FULL), out_all((own, d), FULL),
         out_all((1, own), FULL), out_all((1, own * ff // d), FULL)],
    )
    if halving:
        ends[1] = lax.optimization_barrier((*ends[1], feed_in_grad))[:-1]
    self_in_grad, self_bias_grad = call(
        self_last, "self_last", 1, [all_of(array) for array in (third, *ends[1])],
        [out_all((own, 3 * d), FULL), out_all((3, own), FULL)],
    )
    return (
        output,
        tokens_grad,
        memory_grad,
        self_in_grad,
        self_out_grad.T,
        self_bias_grad,
        query_grad,
        kv_grad,
        cross_out_grad.T,
        cross_bias_grad,
        feed_in_grad,
        feed_out_grad.T,
        bias_in_grad[0],
        bias_out_grad[0],
    )


def solution(mesh):
    return jax.shard_map(
        on_device,
        mesh=mesh,
        in_specs=(
            P(("dp", "fsdp"), None),
            P(("dp", "fsdp"), None),
            P(("dp", "fsdp"), None),
            P(("dp", "fsdp"), None),
            P(("dp", "fsdp"), None),
            P(),
            P(("dp", "fsdp"), None),
            P(None, ("dp", "fsdp")),
            P(None, ("dp", "fsdp")),
            P(("dp", "fsdp"), None),
            P(("dp", "fsdp"), None),
            P(None, ("dp", "fsdp")),
            P(None, ("dp", "fsdp")),
            P(("dp", "fsdp"), None),
            P(None, ("dp", "fsdp")),
            P(("dp", "fsdp")),
            P(("dp", "fsdp")),
        ),
        out_specs=(
            P(("dp", "fsdp"), None),
            P(("dp", "fsdp"), None),
            P(("dp", "fsdp"), None),
            P(("dp", "fsdp"), None),
            P(None, ("dp", "fsdp")),
            P(None, ("dp", "fsdp")),
            P(("dp", "fsdp"), None),
            P(("dp", "fsdp"), None),
            P(None, ("dp", "fsdp")),
            P(None, ("dp", "fsdp")),
            P(("dp", "fsdp"), None),
            P(None, ("dp", "fsdp")),
            P(("dp", "fsdp")),
            P(("dp", "fsdp")),
        ),
        check_vma=False,
    )
```

```python
import functools

import jax
import jax.numpy as jnp
from jax import lax
from jax.experimental import pallas as pl
from jax.experimental.pallas import tpu as pltpu
from jax.sharding import PartitionSpec as P

HEAD = 64
LANES = 128
FAR = -1e30
FIRST = 7
AXES = ("dp", "fsdp")
LOW = jnp.bfloat16
FULL = jnp.float32


def nn(left, right):
    return lax.dot_general(left, right, (((1,), (0,)), ((), ())), preferred_element_type=FULL)


def nt(left, right):
    return lax.dot_general(left, right, (((1,), (1,)), ((), ())), preferred_element_type=FULL)


def tn(left, right):
    return lax.dot_general(left, right, (((0,), (0,)), ((), ())), preferred_element_type=FULL)


def one_head(pair, odd):
    lane = lax.broadcasted_iota(jnp.int32, pair.shape, 1)
    return jnp.where((lane >= HEAD) == bool(odd), pair, jnp.zeros_like(pair))


def later_keys(rows, keys):
    query = lax.broadcasted_iota(jnp.int32, (rows, keys), 0)
    key = lax.broadcasted_iota(jnp.int32, (rows, keys), 1)
    return query, key


def call(
    body, name, grid, ins, outs, scratch=(), flops=0, moved=0, after=(), scalars=(), room=46,
    anywhere=(),
):
    used = len(ins)

    def only_used(*refs):
        front = len(scalars)
        body(*refs[: front + used], *refs[front + used + len(after) :])

    def spec_of(spec):
        if not scalars or spec.index_map is None:
            return spec
        place = spec.index_map
        return pl.BlockSpec(
            spec.block_shape, lambda i, *_: place(i), pipeline_mode=spec.pipeline_mode
        )

    made = pl.pallas_call(
        only_used if after else body,
        name=name,
        grid_spec=pltpu.PrefetchScalarGridSpec(
            num_scalar_prefetch=len(scalars),
            grid=(grid,),
            in_specs=[spec_of(spec) for _, spec in ins]
            + [pl.BlockSpec(memory_space=pl.ANY) for _ in after],
            out_specs=[spec_of(out[2]) for out in outs],
            scratch_shapes=list(scratch),
        ),
        out_shape=[
            (pltpu.VMEM if kept else pltpu.HBM)(shape, kind)
            for shape, kind, _, *kept in outs
        ],
        compiler_params=pltpu.CompilerParams(vmem_limit_bytes=room << 20),
        cost_estimate=pl.CostEstimate(flops=flops, bytes_accessed=moved, transcendentals=0),
    )(
        *scalars,
        *[placed(array, any(array is free for free in anywhere)) for array, _ in ins],
        *after,
    )
    return [
        pltpu.with_memory_space_constraint(array, pltpu.VMEM) if out[3:] else array
        for array, out in zip(made, outs)
    ]


def rows_of(block, columns):
    return pl.BlockSpec((block, columns), lambda i: (i, 0))


def fixed(shape, place=None):
    place = (0,) * len(shape) if place is None else place
    return pl.BlockSpec(shape, lambda i: place, pipeline_mode=pl.Buffered(1))


def all_of(array):
    return (array, fixed(array.shape))


def out_all(shape, kind):
    return (shape, kind, fixed(shape))


def near(out):
    return (*out, True)


def placed(array, anywhere):
    if anywhere or jax.typeof(array).memory_space == pltpu.VMEM:
        return array
    return pltpu.with_memory_space_constraint(array, pltpu.HBM)


def attend(queries, hot, keys_ref, values_ref, count, causal):
    rows = queries.shape[0]
    heads = queries.shape[1] // HEAD
    lane = lax.broadcasted_iota(jnp.int32, (rows, LANES), 1)
    logs = jnp.zeros((rows, LANES), FULL)
    if causal:
        query, key = later_keys(rows, rows)
        ahead = jnp.where(key <= query, 0.0, FAR)

    def scores_of(head):
        columns = slice(head // 2 * LANES, (head // 2 + 1) * LANES)
        asked = jnp.concatenate([one_head(queries[:, columns], head % 2), hot], axis=1)
        scores = nt(asked, keys_ref[head // 2, :count, :])
        if not causal:
            return scores
        if count == rows:
            return scores + ahead
        return jnp.concatenate(
            [scores[:, : count - rows], scores[:, count - rows :] + ahead], axis=1
        )

    mixed = []
    following = scores_of(0)
    for head in range(heads):
        scores = following
        if head + 1 < heads:
            following = scores_of(head + 1)
        columns = slice(head // 2 * LANES, (head // 2 + 1) * LANES)
        top = jnp.max(scores, axis=1, keepdims=True)
        weights = jnp.exp(scores - top)
        amount = jnp.sum(weights, axis=1, keepdims=True)
        low = (weights * (1.0 / amount)).astype(LOW)
        here = nn(low, values_ref[:count, columns])
        if head % 2:
            mixed.append(jnp.where(lane < HEAD, other, here))
        other = here
        logs = jnp.where(lane == head, top + jnp.log(amount), logs)
    return jnp.concatenate(mixed, axis=1), logs.T[:heads]


def keep_keys(keys_ref, place, keys, hot):
    pairs = keys.shape[1] // LANES
    for pair in range(pairs):
        keys_ref[pair, place, :LANES] = keys[:, pair * LANES : (pair + 1) * LANES]
        keys_ref[pair, place, LANES:] = hot


def self_forward(
    tokens, hot, far, gate, w_in, w_out, bias_columns, w_query,
    projected, mixed, logs, first, first_low, cross_queries, keys, values, bias,
    others_there=lambda: None,
):
    step = pl.program_id(0)
    rows, d = tokens.shape

    @pl.when(step == 0)
    def _():
        bias[...] = bias_columns[...].astype(FULL).T[:8]

    joined_bias = jnp.concatenate([bias[0:1, :], jnp.zeros((1, d), FULL), bias[1:2, :]], axis=1)
    made = (nn(tokens[...], w_in[...]) + joined_bias).astype(LOW)
    projected[...] = made
    place = pl.ds(pl.multiple_of(step * rows, rows), rows)
    keep_keys(keys, place, made[:, d : 2 * d], far[...])
    values[place, :] = made[:, 2 * d :]
    part = min(rows, 256)
    for block in range(values.shape[0] // rows):

        @pl.when(step == block)
        def _(before=block * rows):
            scaled = made[:, :d] * jnp.asarray(HEAD**-0.5, LOW)
            for start in range(0, rows, part):
                here = slice(start, start + part)
                mixed[here, :], logs[:, here] = attend(
                    scaled[here, :], hot[here, :], keys, values, before + start + part, True
                )

    branch = nt(mixed[...].astype(LOW), w_out[...]) + bias[2:3, :]
    total = tokens[...].astype(FULL) + gate[...] * branch
    first[...] = total
    first_low[...] = total.astype(LOW)
    others_there()
    cross_queries[...] = (nn(total.astype(LOW), w_query[...]) + bias[3:4, :]).astype(LOW)


class Columns:
    def __init__(self, ref, start, stop):
        self.ref, self.start, self.stop = ref, start, stop

    def __getitem__(self, everything):
        return self.ref[:, :, :, self.start : self.stop].reshape(-1, self.stop - self.start)


def self_forward_joining(
    bits, self_mine, self_got, cross_mine, cross_got, tokens, hot, far, gate, *refs
):
    *outs, self_whole, cross_whole, keys, values, bias, self_here, cross_here, arrived, sent = refs
    d = tokens.shape[1]
    core = bits[0]
    coming = [
        pltpu.make_async_copy(half, here.at[:, place], arrived.at[index])
        for index, (half, here, place) in enumerate(
            [
                (self_mine, self_here, core), (self_got, self_here, 1 - core),
                (cross_mine, cross_here, core), (cross_got, cross_here, 1 - core),
            ]
        )
    ]
    going = [
        pltpu.make_async_copy(self_here, self_whole, sent.at[0]),
        pltpu.make_async_copy(cross_here, cross_whole, sent.at[1]),
    ]

    @pl.when(pl.program_id(0) == 0)
    def _():
        for copy in coming:
            copy.start()
        for copy in coming[:2]:
            copy.wait()
        going[0].start()

    def others_there():
        @pl.when(pl.program_id(0) == 0)
        def _():
            for copy in coming[2:]:
                copy.wait()
            going[1].start()

    self_forward(
        tokens, hot, far, gate, Columns(self_here, 0, 3 * d), Columns(self_here, 3 * d, 4 * d),
        Columns(self_here, 4 * d, 4 * d + LANES), Columns(cross_here, 2 * d, 3 * d),
        *outs, keys, values, bias, others_there=others_there,
    )

    @pl.when(pl.program_id(0) == pl.num_programs(0) - 1)
    def _():
        for copy in going:
            copy.wait()


def cross_forward(
    queries, memory, hot, far, gate, first, w_kv, w_out, bias_columns,
    memory_kv, mixed, logs, second, keys, bias,
):
    d = memory.shape[1]

    @pl.when(pl.program_id(0) == 0)
    def _():
        bias[...] = bias_columns[...].astype(FULL).T[:8]
        made = nn(memory[...], w_kv[...])
        memory_kv[:, :d] = made[:, :d].astype(LOW)
        memory_kv[:, d:] = (made[:, d:] + bias[4:5, :]).astype(LOW)
        keep_keys(keys, slice(None), memory_kv[:, :d], far[...])

    scaled = queries[...] * jnp.asarray(HEAD**-0.5, LOW)
    mixed[...], logs[...] = attend(
        scaled, hot[...], keys, memory_kv.at[:, d:], memory.shape[0], False
    )
    branch = nt(mixed[...].astype(LOW), w_out[...]) + bias[5:6, :]
    second[...] = first[...] + gate[...] * branch


def head_sums(left, right):
    d = left.shape[1]
    head = lax.broadcasted_iota(jnp.int32, (d // HEAD, d), 0)
    column = lax.broadcasted_iota(jnp.int32, (d // HEAD, d), 1)
    chosen = (column // HEAD == head).astype(LOW)
    product = left.astype(FULL) * right.astype(FULL)
    high = product.astype(LOW)
    rest = product - high.astype(FULL)
    middle = rest.astype(LOW)
    last = (rest - middle.astype(FULL)).astype(LOW)
    return nt(chosen, high) + nt(chosen, middle) + nt(chosen, last)


def gelu_both(z):
    c = 0.7978845608028654
    square = z * z
    half = 0.5 + 0.5 * jnp.tanh(z * (c + c * 0.044715 * square))
    value = z * half
    slope = half + value * (1.0 - half) * (2.0 * c + 6.0 * c * 0.044715 * square)
    return value, slope


def spread(d, ff):
    each = ff // d
    row = lax.broadcasted_iota(jnp.int32, (d, ff), 0)
    entry = lax.broadcasted_iota(jnp.int32, (d, ff), 1)
    column = lax.broadcasted_iota(jnp.int32, (LANES, ff), 0)
    there = lax.broadcasted_iota(jnp.int32, (LANES, ff), 1)
    return entry // each == row, (there % each + FIRST == column).astype(LOW)


def columns_to_row(columns, ff):
    owner, place = spread(columns.shape[0], ff)
    return jnp.sum(jnp.where(owner, nn(columns, place), 0.0), axis=0, keepdims=True)


def row_to_columns(row, d):
    owner, place = spread(d, row.shape[1])
    return nt(jnp.where(owner, row, 0.0).astype(LOW), place).astype(LOW)


def rows_to_columns(*rows):
    d = rows[0].shape[1]
    stack = jnp.concatenate([*rows, jnp.zeros((LANES - len(rows), d), FULL)], axis=0)
    return stack.T.astype(LOW)


def feed_both(
    second_far, upstream, gate, mixed, weights, w_cross, bias_columns,
    output, second_grad, mixed_grad, deltas, feed_grad, sums,
    second, w_in, w_out, w_cross_out, low, signal, hidden_all, before_all, crossed, back_all,
    made_all, mixed_back, grads, arrived, sent,
    *, inner, own,
):
    rows, d = second.shape
    ff = w_in.shape[1]
    width = 1024
    parts = [slice(start, start + width) for start in range(0, ff, width)]
    incoming = [(second_far, second)]
    for part in parts:
        incoming.append((weights.at[:, part], w_in.at[:, part]))
        incoming.append(
            (weights.at[:, ff + part.start : ff + part.stop], w_out.at[:, part])
        )
    incoming.append((w_cross.at[:, 3 * d : 4 * d], w_cross_out))
    coming = [
        pltpu.make_async_copy(source, target, arrived.at[index])
        for index, (source, target) in enumerate(incoming)
    ]
    for copy in coming:
        copy.start()
    going = []

    def send(source, target):
        copy = pltpu.make_async_copy(source, target, sent.at[len(going)])
        copy.start()
        going.append(copy)

    bias = bias_columns[...].astype(FULL).T[:8]
    bias_in = columns_to_row(bias_columns[...], ff)
    signal[...] = (gate[...] * upstream[...].astype(FULL)).astype(LOW)
    coming[0].wait()
    low[...] = second[...].astype(LOW)
    half = rows // 2
    items = [(slice(start, start + half), index) for start in (0, half) for index in range(len(parts))]
    bias_grads = [jnp.zeros((1, width), FULL) for _ in parts]

    def products(item):
        place, index = item
        part = parts[index]
        if place.start == 0:
            coming[1 + 2 * index].wait()
            coming[2 + 2 * index].wait()
        before = nn(low[place, :], w_in[:, part]) + bias_in[:, part]
        return before, nn(signal[place, :], w_out[:, part])

    following = products(items[0])
    for at, (place, index) in enumerate(items):
        before, hidden_back = following
        if at + 1 < len(items):
            following = products(items[at + 1])
        if index == 0:
            made = bias[6:7, :]
            back = upstream[place, :].astype(FULL)
        part = parts[index]
        hidden, slope = gelu_both(before)
        hidden_all[place, part] = hidden.astype(LOW)
        before_grad = (hidden_back * slope).astype(LOW)
        before_all[place, part] = before_grad
        bias_grads[index] = bias_grads[index] + column_sum(before_grad)
        made = made + nt(hidden_all[place, part], w_out[:, part])
        back = back + nt(before_all[place, part], w_in[:, part])
        if index == len(parts) - 1:
            made_all[place, :] = (second[place, :] + gate[place, :] * made).astype(LOW)
            back_all[place, :] = back
            crossed[place, :] = (gate[place, :] * back).astype(LOW)
    send(made_all, output)
    send(back_all, second_grad)
    coming[-1].wait()
    mixed_back[...] = nn(crossed[...], w_cross_out[...]).astype(LOW)
    send(mixed_back, mixed_grad)
    deltas[...] = head_sums(mixed_back[...], mixed[...])
    sums[...] = jnp.zeros_like(sums)
    sums[0:1, :] = column_sum(signal[...])
    sums[1:2, :] = column_sum(crossed[...])

    def keep(start, grad):
        end = start + grad.shape[1]
        outer = d // own // inner
        for owner in range(inner * outer if inner > 1 else 0):
            to = (owner % inner * outer + owner // inner) * own
            grads[to : to + own, start:end] = grad[owner * own : (owner + 1) * own]
        if inner == 1:
            grads[:, start:end] = grad
        send(grads.at[:, start:end], feed_grad.at[:, start:end])

    for part in parts:
        keep(part.start, tn(low[...], before_all[:, part]).astype(LOW))
        keep(ff + part.start, tn(signal[...], hidden_all[:, part]).astype(LOW))
    at = 2 * ff
    last = [
        tn(crossed[...], mixed[...].astype(LOW)).astype(LOW),
        rows_to_columns(sums[0:1, :]),
        row_to_columns(jnp.concatenate(bias_grads, axis=1), d),
    ]
    keep(at, jnp.concatenate(last, axis=1))
    for copy in going:
        copy.wait()


def column_sum(array):
    return jnp.sum(array.astype(FULL), axis=0, keepdims=True)


def attend_back(
    queries, keys, values, hot, far, mixed_grad, logs, deltas, pair,
    query_grad, key_grad, value_grad, key_sum, value_sum, reached, causal, block=256,
):
    count = keys.shape[0]
    reached[:, :LANES] = keys[...]
    reached[:, LANES:] = far[...]
    turned = keys[...].T
    if causal:
        key, query = later_keys(block, block)
        ahead = jnp.where(key <= query, 0.0, FAR)
    items = [
        (start, odd) for start in range(queries.shape[0] - block, -1, -block) for odd in range(2)
    ]

    def products(item):
        start, odd = item
        place = slice(start, start + block)
        reach = start + block if causal else count
        asked = one_head(queries[place, :], odd) * jnp.asarray(HEAD**-0.5, LOW)
        incoming = one_head(mixed_grad[place, :], odd)
        scores = nt(reached[:reach, :], jnp.concatenate([asked, hot[place, :]], axis=1))
        if causal and start:
            scores = jnp.concatenate([scores[:start], scores[start:] + ahead], axis=0)
        elif causal:
            scores = scores + ahead
        return scores, nt(values[:reach, :], incoming), asked, incoming, place, reach

    following = products(items[0])
    for index, (start, odd) in enumerate(items):
        scores, pushed, asked, incoming, place, reach = following
        if index + 1 < len(items):
            following = products(items[index + 1])
        head = pl.ds(2 * pair + odd, 1)
        chances = jnp.exp(scores - logs[head, place])
        score_grad = (chances * (pushed - deltas[head, place])).astype(LOW)
        turned_grad = nn(turned[odd * HEAD : (odd + 1) * HEAD, :reach], score_grad)
        value_part = nn(chances.astype(LOW), incoming)
        key_part = nn(score_grad, asked)
        if index == 0:
            value_sum[...] = value_part
            key_sum[...] = key_part
        else:
            value_sum[:reach, :] += value_part
            key_sum[:reach, :] += key_part
        if odd:
            both = jnp.concatenate([other, turned_grad], axis=0) * HEAD**-0.5
            query_grad[place, :] = both.T.astype(LOW)
        other = turned_grad
    key_grad[...] = key_sum[...].astype(LOW)
    value_grad[...] = value_sum[...].astype(LOW)


def cross_back(
    bits, queries, keys, values, hot, far, in_grad, logs, cross_deltas, sums,
    first, second_grad, memory, self_mixed, gate, weights, self_weights,
    *outs,
):
    (
        *owned, key_grad, value_grad, first_grad, mixed_grad, deltas,
        key_sum, value_sum, reached, signals, first_here, second_here, memory_here, mixed_here,
        w_query, w_out, grads, back_here, signal_here, arrived, sent,
    ) = outs
    pair = pl.program_id(0)
    d = memory.shape[1]
    copies = [
        pltpu.make_async_copy(source, target, arrived.at[index])
        for index, (source, target) in enumerate(
            [
                (first, first_here), (second_grad, second_here), (memory, memory_here),
                (self_mixed, mixed_here), (weights.at[:, 2 * d : 3 * d], w_query),
                (self_weights.at[:, 3 * d : 4 * d], w_out),
            ]
        )
    ]

    @pl.when(pair == 0)
    def _():
        for copy in copies:
            copy.start()

    attend_back(
        queries, keys, values, hot, far, in_grad, logs, cross_deltas, pair,
        signals.at[0, pair], signals.at[1, pair], signals.at[2, pair],
        key_sum, value_sum, reached, False,
    )
    key_grad[...] = signals[1, pair]
    value_grad[...] = signals[2, pair]

    @pl.when(pair == pl.num_programs(0) - 1)
    def _():
        for copy in copies:
            copy.wait()
        pairs = signals.shape[1]
        query_signal, key_signal, value_signal = (
            jnp.concatenate([signals[which, place] for place in range(pairs)], axis=1)
            for which in range(3)
        )
        back = second_here[...] + nt(query_signal, w_query[...])
        back_here[...] = back
        signal = (gate[...] * back).astype(LOW)
        mixed_back = nn(signal, w_out[...]).astype(LOW)
        signal_here[...] = mixed_back
        going = [
            pltpu.make_async_copy(back_here, first_grad, sent.at[0]),
            pltpu.make_async_copy(signal_here, mixed_grad, sent.at[1]),
        ]
        for copy in going:
            copy.start()
        deltas[...] = head_sums(mixed_back, mixed_here[...])
        grads[:, :d] = tn(memory_here[...], key_signal).astype(LOW)
        grads[:, d : 2 * d] = tn(memory_here[...], value_signal).astype(LOW)
        grads[:, 2 * d : 3 * d] = tn(first_here[...], query_signal).astype(LOW)
        grads[:, 3 * d : 4 * d] = tn(signal, mixed_here[...].astype(LOW)).astype(LOW)
        grads[:, 4 * d :] = rows_to_columns(
            column_sum(query_signal), column_sum(value_signal), sums[1:2, :], column_sum(signal)
        )
        if len(owned) == 2:
            part_by_core(bits, grads, *owned)
        else:
            owned[0][...] = grads[...]
        for copy in going:
            copy.wait()


def self_back(
    bits, queries, keys, values, hot, far, in_grad, logs, deltas, tokens, *rest, before, ending
):
    if ending:
        earlier, earlier_sums, *rest = rest
    *owned, query_grad, key_grad, value_grad, key_sum, value_sum, reached, signals, grads = rest
    step = pl.program_id(0)
    pairs = signals.shape[1]
    wide = pairs * LANES
    attend_back(
        queries, keys, values, hot, far, in_grad, logs, deltas, before + step,
        signals.at[0, step], signals.at[1, step], signals.at[2, step],
        key_sum, value_sum, reached, True,
    )
    query_grad[...] = signals[0, step]
    key_grad[...] = signals[1, step]
    value_grad[...] = signals[2, step]

    @pl.when(step == pl.num_programs(0) - 1)
    def _():
        at = 3 * wide if ending else 0
        if ending:
            grads[:, :at] = earlier[...]
        added = []
        for which in range(3):
            part = jnp.concatenate([signals[which, place] for place in range(pairs)], axis=1)
            grads[:, at + which * wide : at + (which + 1) * wide] = tn(
                tokens[...], part
            ).astype(LOW)
            if which != 1:
                added.append(column_sum(part))
        if not ending:
            owned[0][...] = grads[...]
            owned[1][0:1, :] = added[0]
            owned[1][1:2, :] = added[1]
            return
        grads[:, 2 * at :] = rows_to_columns(
            *[
                jnp.concatenate([earlier_sums[row : row + 1, :], added[row]], axis=1)
                for row in range(2)
            ]
        )
        if len(owned) == 2:
            part_by_core(bits, grads, *owned)
        else:
            owned[0][...] = grads[...]


def part_by_core(bits, grads, keep, away):
    own = keep.shape[1]
    for core in range(2):

        @pl.when(bits[0] == core)
        def _(core=core):
            for slab in range(2 * keep.shape[0]):
                there = keep if slab % 2 == core else away
                there[slab // 2] = grads[slab * own : (slab + 1) * own, :]


def inputs_back(first_grad, w_in, key_signal, value_signal, w_kv, *refs):
    *signals, tokens_grad, memory_grad = refs
    d = first_grad.shape[1]
    total = first_grad[...]
    wide = signals[0].shape[1]
    for index, signal in enumerate(signals):
        start = index % 3 * d + index // 3 * wide
        total = total + nt(signal[...], w_in[:, start : start + wide])
    tokens_grad[...] = total
    memory_grad[...] = nt(key_signal[...], w_kv[:, :d]) + nt(value_signal[...], w_kv[:, d:])


def sum_to_owners(grads, device_count, orders):
    me = lax.axis_index(AXES)
    bits = device_count.bit_length() - 1
    running = []
    for grad in grads:
        rows, columns = grad.shape
        running.append(grad.reshape((2,) * bits + (rows // device_count, columns)))
    left = [list(range(bits)) for _ in grads]
    for step in range(bits):
        sent = []
        for part, order in enumerate(orders):
            bit = order[step]
            axis = len(left[part]) - 1 - left[part].index(bit)
            mine = (me >> bit) & 1
            away = lax.dynamic_index_in_dim(running[part], 1 - mine, axis, keepdims=False)
            pairs = [(i, i ^ (1 << bit)) for i in range(device_count)]
            sent.append((axis, mine, lax.ppermute(away.astype(LOW), AXES, pairs)))
            left[part].remove(bit)
        for part, (axis, mine, got) in enumerate(sent):
            kept = lax.dynamic_index_in_dim(running[part], mine, axis, keepdims=False)
            running[part] = kept.astype(FULL) + got.astype(FULL)
    return running


def swap(array, bit, device_count):
    return lax.ppermute(array, AXES, [(i, i ^ (1 << bit)) for i in range(device_count)])


def scatter_rows(grad, device_count):
    bits = device_count.bit_length() - 1
    high = list(range(1, bits))[::-1]
    half = grad.shape[1] // 256 * 128
    orders = ([0] + high, [0, high[1], high[0]] + high[2:])
    return jnp.concatenate(
        sum_to_owners([grad[:, :half], grad[:, half:]], device_count, orders), axis=1
    )


def swap(array, change, device_count):
    return lax.ppermute(array, AXES, [(i, i ^ change) for i in range(device_count)])


def picked(terms, first, second):
    total = None
    for term in terms:
        for place in (first, second):
            term = lax.dynamic_index_in_dim(term, place, 0, keepdims=False)
        total = term.astype(FULL) if total is None else total + term.astype(FULL)
    return total


class Halving:
    changes = ((0, 1), (1, 0), (1, 1))

    def __init__(self, me, keep, away, device_count):
        self.count = device_count
        self.x, self.y = (me >> 3) & 1, (me >> 4) & 1
        self.low, self.high = (me >> 1) & 1, (me >> 2) & 1
        shape = (2, 2, 4, *keep.shape[1:])
        self.terms = [keep.reshape(shape)]
        self.got = [swap(away.reshape(shape), 1, device_count)]

    def plane(self):
        terms = self.terms + self.got
        self.sent = [picked(terms, self.y ^ y, self.x ^ x).astype(LOW) for y, x in self.changes]
        self.got = [
            swap(array, 8 * x + 16 * y, self.count)
            for array, (y, x) in zip(self.sent, self.changes)
        ]
        self.terms = [
            lax.dynamic_index_in_dim(
                lax.dynamic_index_in_dim(term, self.y, 0, keepdims=False), self.x, 0, keepdims=False
            )
            for term in terms
        ]

    def line(self):
        terms = [term.reshape(2, 2, *term.shape[1:]) for term in self.terms + self.got]
        self.sent = [
            picked(terms, self.high ^ high, self.low ^ low).astype(LOW)
            for high, low in self.changes
        ]
        self.kept = picked(terms, self.high, self.low)

    def send_line(self, *after):
        self.sent = list(lax.optimization_barrier((*self.sent, *after))[: len(self.sent)])
        self.got = [
            swap(array, 2 * low + 4 * high, self.count)
            for array, (high, low) in zip(self.sent, self.changes)
        ]

    def wait_for(self, *arrays):
        self.got = list(lax.optimization_barrier((*self.got, *arrays))[: len(self.got)])


def total_of(keep, *got):
    total = keep[...]
    for part in got:
        total = total + part[...].astype(FULL)
    return total


def cross_last(*refs):
    *parts, kv, query, self_out, cross_bias, self_bias = refs
    total = total_of(*parts)
    d = query.shape[1]
    kv[...] = total[:, : 2 * d]
    query[...] = total[:, 2 * d : 3 * d]
    self_out[...] = total[:, 3 * d : 4 * d]
    turned = turned_bias(total[:, 4 * d :])
    cross_bias[...] = turned[0:3]
    self_bias[...] = turned[3:4]


def turned_bias(columns):
    own = columns.shape[0]
    square = jnp.concatenate([columns, jnp.zeros((LANES - own, LANES), FULL)], axis=0)
    return square.T[:8, :own]


def self_last(third, *refs):
    *parts, self_in, bias = refs
    total = total_of(*parts)
    columns = self_in.shape[1]
    half = columns // 2
    wide = half // 3
    for call_index in range(2):
        for which in range(3):
            at = call_index * half + which * wide
            to = which * 2 * wide + call_index * wide
            self_in[:, to : to + wide] = total[:, at : at + wide]
    bias[0:2, :] = turned_bias(total[:, columns:])[0:2]
    bias[2:3, :] = third[...]


def feed_last(total, feed_in, feed_out, cross_out, bias_out, bias_in):
    ff = feed_in.shape[1]
    at = 2 * ff + cross_out.shape[1]
    feed_in[...] = total[:, :ff].astype(FULL)
    feed_out[...] = total[:, ff : 2 * ff].astype(FULL)
    cross_out[...] = total[:, 2 * ff : at].astype(FULL)
    bias_out[...] = turned_bias(total[:, at : at + LANES].astype(FULL))[0:1]
    bias_in[...] = columns_to_row(total[:, at + LANES :], bias_in.shape[1])


def pack(
    self_in, self_out, cross_query, cross_kv, cross_out, feed_in, feed_out, self_bias, cross_bias,
    bias_out, bias_in, near, own_feed,
):
    d = self_out.shape[1]
    ff = feed_in.shape[1]
    own = self_in.shape[0]
    near[:, : 3 * d] = self_in[...].astype(LOW)
    near[:, 3 * d : 4 * d] = self_out[...].astype(LOW)
    rows = jnp.concatenate(
        [self_bias[...], cross_bias[...], bias_out[...], jnp.zeros((LANES - 7, own), FULL)], axis=0
    )
    wide = jnp.concatenate([rows, jnp.zeros((LANES, LANES - own), FULL)], axis=1)
    at = 4 * d + LANES
    near[:, 4 * d : at] = wide.T[:own].astype(LOW) + row_to_columns(bias_in[...], own)
    near[:, at : at + 2 * d] = cross_kv[...].astype(LOW)
    near[:, at + 2 * d : at + 3 * d] = cross_query[...].astype(LOW)
    near[:, at + 3 * d :] = cross_out[...].astype(LOW)
    own_feed[:, :ff] = feed_in[...].astype(LOW)
    own_feed[:, ff:] = feed_out[...].astype(LOW)


def marks(seq_lengths, memory_lengths, residual_gate, hot, self_far, memory_far, gate):
    slots = seq_lengths.shape[0]
    lane = lax.broadcasted_iota(jnp.int32, hot.shape, 1)

    def numbered(lengths, padding):
        position = lax.broadcasted_iota(jnp.int32, hot.shape, 0)
        end = lengths[0]
        number = jnp.where(position >= end, 1, 0)
        for slot in range(1, slots):
            end = end + lengths[slot]
            number = number + jnp.where(position >= end, 1, 0)
        present = position < end
        return jnp.where(present, number, padding), present

    ids, present = numbered(seq_lengths, slots)
    hot[...] = jnp.where(ids == lane, 1.0, 0.0).astype(LOW)
    self_far[...] = jnp.where(ids == lane, 0.0, FAR).astype(LOW)
    gate[...] = jnp.where(present[:, :1], residual_gate[0], 0.0)
    ids, _ = numbered(memory_lengths, slots + 1)
    memory_far[...] = jnp.where(ids == lane, 0.0, FAR).astype(LOW)


def gather_near(near, cut, device_count, after):
    me = lax.axis_index(AXES)
    others = [swap(near, 2 * change, device_count) for change in (1, 2, 3)]
    others = lax.optimization_barrier((*others, after))[:3]
    first, second, third, fourth = near, *others
    odd = jnp.where(
        (me >> 1) & 1,
        jnp.stack([second, first, fourth, third]),
        jnp.stack([first, second, third, fourth]),
    )
    line = jnp.where((me >> 2) & 1, jnp.concatenate([odd[2:], odd[:2]]), odd)
    held = [line[..., :cut], line[..., cut:]]
    known = [[1, 1], [1, 1]]
    for bits in ((3, 4), (4, 3)):
        got = [swap(array, 1 << bit, device_count) for array, bit in zip(held, bits)]
        for part, bit in enumerate(bits):
            axis = sum(other > bit for other in known[part])
            low = jnp.stack([held[part], got[part]], axis)
            high = jnp.stack([got[part], held[part]], axis)
            held[part] = jnp.where((me >> bit) & 1, high, low)
            known[part].append(bit)
    mine = [array.reshape(-1, *array.shape[-2:]) for array in held]
    return [(array, swap(array, 1, device_count)) for array in mine]


def on_device(
    tokens, memory, out_cotangent, seq_lengths, memory_lengths, residual_gate,
    self_in, self_out, self_bias, cross_query, cross_key_value, cross_out, cross_bias,
    feed_in, feed_out, feed_bias_in, feed_bias_out,
):
    device_count = lax.axis_size(AXES)
    count, d = tokens.shape
    key_count = memory.shape[0]
    ff = feed_in.shape[1]
    own = self_in.shape[0]
    pairs = d // LANES
    heads = d // HEAD
    block = 512
    steps = count // block
    halving = lax.axis_size("dp") == 4 and lax.axis_size("fsdp") == 8
    me = lax.axis_index(AXES)
    bits = (me & 1).astype(jnp.int32)[None]
    cut = 4 * d + LANES
    own_near, own_feed = call(
        pack,
        "pack",
        1,
        [
            all_of(array)
            for array in (
                self_in, self_out.T, cross_query, cross_key_value, cross_out.T, feed_in,
                feed_out.T, self_bias, cross_bias, feed_bias_out[None], feed_bias_in[None],
            )
        ],
        [out_all((own, cut + 4 * d), LOW), out_all((own, 2 * ff), LOW)],
    )
    hot, self_far, memory_far, gate = call(
        marks,
        "marks",
        1,
        [],
        [out_all((count, LANES), LOW), out_all((count, LANES), LOW),
         out_all((key_count, LANES), LOW), out_all((count, 1), FULL)],
        scalars=(seq_lengths[0], memory_lengths[0], residual_gate),
    )
    feed_whole = lax.all_gather(own_feed, AXES, axis=0, tiled=True)
    if halving:
        (self_mine, self_got), (cross_mine, cross_got) = gather_near(own_near, cut, device_count, gate)
    else:
        self_whole = lax.all_gather(own_near[:, :cut], AXES, axis=0, tiled=True)
        cross_whole = lax.all_gather(own_near[:, cut:], AXES, axis=0, tiled=True)
    each = lambda array: (array, rows_of(block, array.shape[1]))
    out_rows = lambda columns, kind: ((count, columns), kind, rows_of(block, columns))
    out_heads = ((heads, count), FULL, pl.BlockSpec((heads, block), lambda i: (0, i)))

    self_outs = [
        out_rows(3 * d, LOW), out_rows(d, FULL), out_heads, near(out_rows(d, FULL)),
        out_rows(d, LOW), out_rows(d, LOW),
    ]
    self_room = [
        pltpu.VMEM((pairs, count, 2 * LANES), LOW), pltpu.VMEM((count, d), LOW),
        pltpu.VMEM((8, d), FULL),
    ]
    if halving:
        there = pl.BlockSpec(memory_space=pl.ANY)
        halves = (self_mine, self_got, cross_mine, cross_got)
        (
            projected, self_mixed, self_logs, first, first_low, cross_queries,
            self_whole, cross_whole,
        ) = call(
            self_forward_joining,
            "self_forward",
            steps,
            [(array, there) for array in halves]
            + [each(tokens), each(hot), each(self_far), each(gate)],
            self_outs
            + [((device_count // 2, 2, own, columns), LOW, there) for columns in (cut, 4 * d)],
            self_room
            + [pltpu.VMEM((device_count // 2, 2, own, columns), LOW) for columns in (cut, 4 * d)]
            + [pltpu.SemaphoreType.DMA((4,)), pltpu.SemaphoreType.DMA((2,))],
            flops=15 << 30, moved=8 << 20, scalars=(bits,), anywhere=halves,
        )
        self_whole, cross_whole = self_whole.reshape(d, cut), cross_whole.reshape(d, 4 * d)
    w_self_in = (self_whole, fixed((d, 3 * d), (0, 0)))
    w_self_out = (self_whole, fixed((d, d), (0, 3)))
    bias_columns = (self_whole, fixed((d, LANES), (0, 4 * d // LANES)))
    w_kv = (cross_whole, fixed((d, 2 * d), (0, 0)))
    w_query = (cross_whole, fixed((d, d), (0, 2)))
    w_cross_out = (cross_whole, fixed((d, d), (0, 3)))
    w_feed_in = (feed_whole, fixed((d, ff), (0, 0)))
    w_feed_out = (feed_whole, fixed((d, ff), (0, 1)))

    if not halving:
        projected, self_mixed, self_logs, first, first_low, cross_queries = call(
            self_forward,
            "self_forward",
            steps,
            [each(tokens), each(hot), each(self_far), each(gate), w_self_in, w_self_out,
             bias_columns, w_query],
            self_outs,
            self_room,
            flops=15 << 30, moved=8 << 20,
        )
    memory_kv, cross_mixed, cross_logs, second = call(
        cross_forward,
        "cross_forward",
        steps,
        [each(cross_queries), all_of(memory), each(hot), all_of(memory_far), each(gate),
         each(first), w_kv, w_cross_out, bias_columns],
        [out_all((key_count, 2 * d), LOW), near(out_rows(d, FULL)), near(out_heads),
         out_rows(d, FULL)],
        [pltpu.VMEM((pairs, key_count, 2 * LANES), LOW), pltpu.VMEM((8, d), FULL)],
        flops=20 << 30, moved=8 << 20,
    )
    inner = lax.axis_size("fsdp") if halving else 1
    left_there = lambda array: (array, pl.BlockSpec(memory_space=pl.ANY))
    out_there = lambda shape, kind: (shape, kind, pl.BlockSpec(memory_space=pl.ANY))
    out_wide = 2 * ff + d + 2 * LANES
    output, second_grad, cross_mixed_grad, cross_deltas, feed_grad, feed_sums = call(
        functools.partial(feed_both, inner=inner, own=own),
        "feed_both",
        1,
        [left_there(second), all_of(out_cotangent), all_of(gate), all_of(cross_mixed),
         left_there(feed_whole), left_there(cross_whole), bias_columns],
        [out_there((count, d), LOW), out_there((count, d), FULL), out_there((count, d), LOW),
         near(out_all((heads, count), FULL)), out_there((d, out_wide), LOW),
         near(out_all((8, d), FULL))],
        [pltpu.VMEM((count, d), FULL), pltpu.VMEM((d, ff), LOW), pltpu.VMEM((d, ff), LOW),
         pltpu.VMEM((d, d), LOW), pltpu.VMEM((count, d), LOW), pltpu.VMEM((count, d), LOW),
         pltpu.VMEM((count, ff), LOW), pltpu.VMEM((count, ff), LOW), pltpu.VMEM((count, d), LOW),
         pltpu.VMEM((count, d), FULL), pltpu.VMEM((count, d), LOW), pltpu.VMEM((count, d), LOW),
         pltpu.VMEM((d, out_wide), LOW), pltpu.SemaphoreType.DMA((6,)),
         pltpu.SemaphoreType.DMA((8,))],
        flops=25 << 30, moved=16 << 20,
    )
    ways = ("fsdp", "dp") if halving else ("dp", "fsdp")
    feed_total = lax.psum_scatter(feed_grad, ways[0], scatter_dimension=0, tiled=True)

    def pair_columns(array, start, width=LANES):
        return (array, pl.BlockSpec((array.shape[0], width), lambda i: (0, start + i)))

    def out_pairs(rows, columns):
        return ((rows, columns), LOW, pl.BlockSpec((rows, LANES), lambda i: (0, i)))

    def owned(columns):
        if halving:
            return [out_all((device_count // 2, own, columns), LOW)] * 2
        return [out_all((d, columns), LOW)]

    def pair_room(rows, steps):
        return [
            pltpu.VMEM((rows, LANES), FULL), pltpu.VMEM((rows, LANES), FULL),
            pltpu.VMEM((rows, 2 * LANES), LOW), pltpu.VMEM((3, steps, rows, LANES), LOW),
        ]

    cross_columns = 4 * d + LANES
    *cross_owned, key_signal, value_signal, first_grad, self_mixed_grad, self_deltas = call(
        cross_back,
        "cross_back",
        pairs,
        [pair_columns(cross_queries, 0), pair_columns(memory_kv, 0),
         pair_columns(memory_kv, pairs), all_of(hot), all_of(memory_far),
         pair_columns(cross_mixed_grad, 0), all_of(cross_logs), all_of(cross_deltas),
         all_of(feed_sums), left_there(first_low), left_there(second_grad), left_there(memory),
         left_there(self_mixed), all_of(gate), left_there(cross_whole), left_there(self_whole)],
        owned(cross_columns)
        + [out_pairs(key_count, d), out_pairs(key_count, d), out_there((count, d), FULL),
           out_there((count, d), LOW), near(out_all((heads, count), FULL))],
        pair_room(key_count, pairs)
        + [pltpu.VMEM((count, d), LOW), pltpu.VMEM((count, d), FULL),
           pltpu.VMEM((key_count, d), LOW), pltpu.VMEM((count, d), FULL),
           pltpu.VMEM((d, d), LOW), pltpu.VMEM((d, d), LOW),
           pltpu.VMEM((d, cross_columns), LOW), pltpu.VMEM((count, d), FULL),
           pltpu.VMEM((count, d), LOW), pltpu.SemaphoreType.DMA((6,)),
           pltpu.SemaphoreType.DMA((2,))],
        flops=30 << 30, moved=24 << 20, scalars=(bits,),
    )
    if halving:
        cross_sum = Halving(me, *cross_owned, device_count)

    half = pairs // 2
    self_columns = 3 * d + LANES

    def self_part(before, ending, outs, earlier=(), after=()):
        wide = half * LANES
        columns = self_columns if ending else 3 * wide
        return call(
            functools.partial(self_back, before=before, ending=ending),
            "self_back",
            half,
            [pair_columns(projected, before), pair_columns(projected, pairs + before),
             pair_columns(projected, 2 * pairs + before), all_of(hot), all_of(self_far),
             pair_columns(self_mixed_grad, before), all_of(self_logs), all_of(self_deltas),
             all_of(tokens)]
            + [all_of(array) for array in earlier],
            outs + [out_pairs(count, wide)] * 3,
            pair_room(count, half) + [pltpu.VMEM((d, columns), LOW)],
            flops=12 << 30, moved=8 << 20, scalars=(bits,), after=after,
        )

    wide = half * LANES
    *earlier, query_one, key_one, value_one = self_part(
        0, False, [out_all((d, 3 * wide), LOW), out_all((8, wide), FULL)]
    )
    after = ()
    if halving:
        cross_sum.wait_for(query_one)
        cross_sum.plane()
        after = tuple(cross_sum.sent)
    *self_owned, query_two, key_two, value_two = self_part(
        half, True, owned(self_columns), earlier, after
    )
    after = ()
    if halving:
        cross_sum.wait_for(query_two)
        feed_total, _ = lax.optimization_barrier((feed_total, cross_sum.got[0]))
    feed_part = feed_total
    feed_total = lax.psum_scatter(feed_total, ways[1], scatter_dimension=0, tiled=True)
    if halving:
        self_sum = Halving(me, *self_owned, device_count)
        cross_sum.line()
        self_sum.wait_for(*cross_sum.sent, feed_part)
        self_sum.plane()
        cross_sum.send_line(*self_sum.sent)
        after = tuple(self_sum.sent)
    tokens_grad, memory_grad = call(
        inputs_back,
        "inputs_back",
        steps,
        [each(first_grad), w_self_in, each(key_signal), each(value_signal), w_kv]
        + [each(array) for array in (query_one, key_one, value_one, query_two, key_two, value_two)],
        [out_rows(d, FULL), ((key_count, d), FULL, rows_of(block, d))],
        flops=5 << 30, moved=13 << 20, after=after,
    )
    if halving:
        self_sum.wait_for(tokens_grad, memory_grad)
        self_sum.line()
        self_sum.send_line()
        cross_sum.wait_for(*self_sum.sent)
        ends = [(cross_sum.kept, *cross_sum.got), (self_sum.kept, *self_sum.got)]
    else:
        ends = [(scatter_rows(grads[0], device_count),) for grads in (cross_owned, self_owned)]
    kv_grad, query_grad, self_out_grad, cross_bias_grad, third = call(
        cross_last, "cross_last", 1, [all_of(array) for array in ends[0]],
        [out_all((own, 2 * d), FULL), out_all((own, d), FULL), out_all((own, d), FULL),
         out_all((3, own), FULL), out_all((1, own), FULL)],
    )
    feed_in_grad, feed_out_grad, cross_out_grad, bias_out_grad, bias_in_grad = call(
        feed_last, "feed_last", 1, [all_of(feed_total)],
        [out_all((own, ff), FULL), out_all((own, ff), FULL), out_all((own, d), FULL),
         out_all((1, own), FULL), out_all((1, own * ff // d), FULL)],
    )
    if halving:
        ends[1] = lax.optimization_barrier((*ends[1], feed_in_grad))[:-1]
    self_in_grad, self_bias_grad = call(
        self_last, "self_last", 1, [all_of(array) for array in (third, *ends[1])],
        [out_all((own, 3 * d), FULL), out_all((3, own), FULL)],
    )
    return (
        output,
        tokens_grad,
        memory_grad,
        self_in_grad,
        self_out_grad.T,
        self_bias_grad,
        query_grad,
        kv_grad,
        cross_out_grad.T,
        cross_bias_grad,
        feed_in_grad,
        feed_out_grad.T,
        bias_in_grad[0],
        bias_out_grad[0],
    )


def solution(mesh):
    return jax.shard_map(
        on_device,
        mesh=mesh,
        in_specs=(
            P(("dp", "fsdp"), None),
            P(("dp", "fsdp"), None),
            P(("dp", "fsdp"), None),
            P(("dp", "fsdp"), None),
            P(("dp", "fsdp"), None),
            P(),
            P(("dp", "fsdp"), None),
            P(None, ("dp", "fsdp")),
            P(None, ("dp", "fsdp")),
            P(("dp", "fsdp"), None),
            P(("dp", "fsdp"), None),
            P(None, ("dp", "fsdp")),
            P(None, ("dp", "fsdp")),
            P(("dp", "fsdp"), None),
            P(None, ("dp", "fsdp")),
            P(("dp", "fsdp")),
            P(("dp", "fsdp")),
        ),
        out_specs=(
            P(("dp", "fsdp"), None),
            P(("dp", "fsdp"), None),
            P(("dp", "fsdp"), None),
            P(("dp", "fsdp"), None),
            P(None, ("dp", "fsdp")),
            P(None, ("dp", "fsdp")),
            P(("dp", "fsdp"), None),
            P(("dp", "fsdp"), None),
            P(None, ("dp", "fsdp")),
            P(None, ("dp", "fsdp")),
            P(("dp", "fsdp"), None),
            P(None, ("dp", "fsdp")),
            P(("dp", "fsdp")),
            P(("dp", "fsdp")),
        ),
        check_vma=False,
    )
```
